32 devices in a mesh: ctx: 8 (over y, x, core), wsh: 4 (over z).
Axes of the slice: x: 2, y: 2, z: 4, core: 2. Of those that a mesh axis runs over, the one named last changes fastest.
Arguments:
- tokens: bfloat16 [1024, 4, 768], P('ctx'), may hold values from -6 to 6
- gain_one: float32 [768], replicated, may hold values from 0.5 to 1.5
- qkv_weight: bfloat16 [768, 3, 768], P(None, None, 'wsh'), may hold values from -0.21875 to 0.21875
- out_weight: bfloat16 [768, 768], P('wsh'), may hold values from -5 to 5
- rel_weight: float32 [32, 12], P(None, 'wsh'), may hold values from -6 to 6
- gain_two: float32 [768], replicated, may hold values from 0.5 to 1.5
- router_weight: float32 [768, 4], replicated, may hold values from -0.15625 to 0.15625
- expert_in: bfloat16 [8, 768, 1536], P('ctx', None, 'wsh'), may hold values from -0.21875 to 0.21875
- expert_out: bfloat16 [8, 1536, 768], P('ctx', 'wsh'), may hold values from -0.4375 to 0.4375
- routes: int32 [1024, 4, 1], P('ctx'), may hold values from 0 to 3; in each aligned block of 512 rows (0 to 511, 512 to 1023, ..., all dimensions but the last counted through in order) at most 256 rows name the same one
- bucket_table: int32 [128], replicated, may hold values from 0 to 31, as said below
- grad_out: bfloat16 [1024, 4, 768], P('ctx'), may hold values from -6 to 6
Outputs:
- out: bfloat16 [1024, 4, 768], P('ctx')
- grad_tokens: float32 [1024, 4, 768], P('ctx')
- grad_gain_one: float32 [768], replicated
- grad_qkv: float32 [768, 3, 768], P(None, None, 'wsh')
- grad_out_weight: float32 [768, 768], P('wsh')
- grad_rel: float32 [32, 12], P(None, 'wsh')
- grad_gain_two: float32 [768], replicated
- grad_router: float32 [768, 4], replicated
- grad_expert_in: float32 [8, 768, 1536], P('ctx', None, 'wsh')
- grad_expert_out: float32 [8, 1536, 768], P('ctx', 'wsh')
The draws below stay inside these ranges and needn't reach their ends.
Inputs may be any that keep to these rules, and one draw needn't show every extreme that they name: `routes`: among the 512 tokens of one device (aligned blocks of rows), at most 256 name the same expert, and in every draw some device and expert reach 256. `bucket_table`: never falls; entry d is d for d < 16; the last entry is 31.
All inputs are finite; a program needn't handle non-finite values.
Results may differ from the reference program's by a relative error of at most 0.03.
Values may be sent and summed in bfloat16 or wider, within the bound.
No kernel may reach another device: no remote copies, remote signals or barrier semaphores. Data moves between devices by JAX's collectives and lax.ppermute only.
A program may use at most 192 MiB of HBM per device.

```python
import math
from functools import partial
import jax
import jax.numpy as jnp
import numpy as np
from jax import lax

D = 768
HEADS = 12
HD = 64
FF = 3072
BUCKETS = 32
MAXD = 128
EXACT = 16
BLK = 64
SEQS = 4
TOK_DEV = 512
SEQ_LEN = 1024
EXPERTS = 4
CAP = 256
N_CTX = 8


def draw_bucket_table(key, part):
    key = jax.random.fold_in(key, 11)
    spread_count = MAXD - EXACT
    cuts = jax.random.permutation(key, spread_count - 1)[:BUCKETS - EXACT - 1].astype(jnp.int32) + 1
    far_steps = jnp.arange(spread_count, dtype=jnp.int32)
    climbed = jnp.sum((cuts[None, :] <= far_steps[:, None]).astype(jnp.int32), axis=1)
    return jnp.concatenate([jnp.arange(EXACT, dtype=jnp.int32), EXACT + climbed]).astype(jnp.int32)


def block_levels(own_key, shape, shards, low, top_value):
    gain, own = 1.0, jax.random.fold_in(own_key, 6)
    for axis_at, blocks in shards:
        draws = jnp.exp(jax.random.uniform(jax.random.fold_in(own, axis_at), (blocks,), jnp.float32, low / len(shards), top_value / len(shards)))
        gain = gain * jnp.repeat(draws, shape[axis_at] // blocks).reshape([-1 if axis == axis_at else 1 for axis in range(len(shape))])
    return gain


def shared_out(rng, own, number, rows, amount, top, reach, skew):
    order = jax.random.permutation(rng, amount)
    packed, ordinary = portions_of(amount, rows * top, reach, skew, True), portions_of(amount, rows * top, reach, skew, False)
    places = jnp.arange(amount)

    def named(lengths, offset_by):
        used = int((lengths > 0).sum())
        fixed = max(1, used // 4)
        moved = fixed + (places - fixed + offset_by * (used - fixed)) % max(1, amount - fixed)
        return jnp.zeros((amount,), jnp.int32).at[order[jnp.where(places < fixed, places, moved)]].set(jnp.asarray(lengths, jnp.int32))

    lengths = jnp.where(number % 4 == 0, named(packed, number // 4), named(ordinary, number - number // 4 - 1))
    mixed = jax.random.permutation(jax.random.fold_in(own, 3), amount)
    source_of, receiver = mixed[0:amount // 2 * 2:2], mixed[1:amount // 2 * 2:2]
    margin = jnp.minimum(lengths[source_of] - 1, reach - lengths[receiver]) // 2
    margin = jnp.where((source_of == order[0]) | (receiver == order[0]) | (lengths[receiver] == 0), 0, jnp.maximum(margin, 0))
    moved = jax.random.randint(jax.random.fold_in(own, 4), (amount // 2,), 0, 1 << 20) % (margin + 1)
    lengths = lengths.at[source_of].add(-moved).at[receiver].add(moved)
    members = jnp.searchsorted(jnp.cumsum(lengths), jnp.arange(rows * top), side="right").astype(jnp.int32)
    table = members.reshape(top, rows).T
    table = table[jax.random.permutation(jax.random.fold_in(own, 1), rows)]
    offset_by = jax.random.randint(jax.random.fold_in(own, 2), (rows, 1), 0, top)
    return jnp.take_along_axis(table, (jnp.arange(top)[None, :] + offset_by) % top, axis=1)


def portions_of(count, total, limit, skew, full):
    loads = [(1 << 20) // math.isqrt(standing ** skew) + 1 for standing in range(1, count + 1)]
    largest = limit if full else min(limit, max(-(-total // count), total * loads[0] // sum(loads)))
    least = 1 if total - largest >= count - 1 else 0
    given, rest = [largest] + [least] * (count - 1), total - largest - least * (count - 1)
    while rest > 0:
        free = [i for i in range(1, count) if given[i] < largest] or [i for i in range(1, count) if given[i] < limit]
        pool, remaining = sum([loads[i] for i in free]), rest
        for i in free:
            extra = min(limit - given[i], max(1, remaining * loads[i] // pool), rest)
            given[i] = given[i] + extra
            rest = rest - extra
    return np.array(given)


def normal_values(stream_key, extent, deviation, limit, split=(), kind=jnp.bfloat16):
    gain = block_levels(stream_key, extent, split, -0.22, 0.18) if split else 1.0
    entries = jax.random.normal(stream_key, extent, jnp.float32) * deviation * gain
    return jnp.minimum(jnp.maximum(entries, -limit), limit).astype(kind)


def setup_inputs(seed: int = 0) -> dict:
    streams_of = jax.random.split(jax.random.key(seed), 13)
    tokens = normal_values(streams_of[0], (SEQ_LEN, SEQS, D), 1.0, 6.0, ((0, 8),))
    gain_one = jnp.clip(1.0 + 0.1 * jax.random.normal(streams_of[1], (D,), jnp.float32), 0.5, 1.5)
    qkv_weight = normal_values(streams_of[2], (D, 3, D), D ** -0.5, 0.21875, ((2, 4),))
    out_weight = normal_values(streams_of[3], (D, D), ((SEQ_LEN // 2) ** 0.5 * D ** -0.5), 5.0, ((0, 4),))
    rel_weight = normal_values(streams_of[4], (BUCKETS, HEADS), 1.0, 6.0, ((1, 4),), jnp.float32)
    gain_two = jnp.clip(1.0 + 0.1 * jax.random.normal(streams_of[5], (D,), jnp.float32), 0.5, 1.5)
    router_weight = normal_values(streams_of[6], (D, EXPERTS), (0.7 * D ** -0.5), 0.15625, (), jnp.float32)
    expert_in = normal_values(streams_of[7], (2 * EXPERTS, D, FF // 2), D ** -0.5, 0.21875, ((0, 8), (2, 4)))
    expert_out = normal_values(streams_of[8], (2 * EXPERTS, FF // 2, D), (max(1, FF // (EXPERTS * EXPERTS))) ** -0.5, 0.4375, ((0, 8), (1, 4)))
    routes_keys = jax.random.split(jax.random.fold_in(streams_of[9], 1), SEQ_LEN * SEQS // TOK_DEV)
    routes_turns = jax.random.permutation(jax.random.fold_in(streams_of[9], 3), SEQ_LEN * SEQS // TOK_DEV)
    routes = jax.vmap(lambda own, number: shared_out(jax.random.fold_in(streams_of[9], 2), own, number, TOK_DEV, EXPERTS, 1, CAP, 2))(routes_keys, routes_turns).reshape((SEQ_LEN, SEQS, 1))
    bucket_table = draw_bucket_table(jax.random.fold_in(streams_of[12], 71), 0)
    grad_out = normal_values(streams_of[11], (SEQ_LEN, SEQS, D), 1.0, 6.0, ((0, 8),))
    return dict(tokens=tokens, gain_one=gain_one, qkv_weight=qkv_weight, out_weight=out_weight, rel_weight=rel_weight, gain_two=gain_two, router_weight=router_weight, expert_in=expert_in, expert_out=expert_out, routes=routes, bucket_table=bucket_table, grad_out=grad_out)


EPSILON = 1e-06
MASKED = -1e+30
PRECISE = lax.Precision.HIGHEST

@jax.custom_vjp
def low(v):
    return lax.optimization_barrier(v.astype(jnp.bfloat16)).astype(jnp.float32)

@jax.custom_vjp
def low_back(v):
    return v

def low_keep(v):
    return (low(v), None)

def low_pass(kept, grad):
    return (grad,)

def back_keep(v):
    return (v, None)

def back_low(kept, grad):
    return (low(grad),)
low.defvjp(low_keep, low_pass)
low_back.defvjp(back_keep, back_low)

def dealt_positions():
    rows_all = jnp.arange(SEQ_LEN, dtype=jnp.int32)
    owner_dev = rows_all // (2 * BLK)
    within = rows_all % (2 * BLK)
    early_pos = owner_dev * BLK + within
    late_pos = (2 * N_CTX - 1 - owner_dev) * BLK + within - BLK
    return jnp.where(within < BLK, early_pos, late_pos)

def norm_apply(values, gain_vec):
    return values * lax.rsqrt(lax.optimization_barrier(jnp.mean(values * values, axis=-1, keepdims=True)) + EPSILON) * gain_vec

def attention(query, key_all, value_all, head_table, position):
    rows_block = min(512, SEQ_LEN)
    blocks = SEQ_LEN // rows_block
    query_seq = jnp.transpose(query, (1, 0, 2, 3)).reshape(SEQS * blocks, rows_block, HEADS, HD)
    key_seq = jnp.transpose(key_all, (1, 0, 2, 3))
    value_seq = jnp.transpose(value_all, (1, 0, 2, 3))
    pos_blocks = jnp.tile(position.reshape(blocks, rows_block), (SEQS, 1))
    seq_ids = jnp.repeat(jnp.arange(SEQS, dtype=jnp.int32), blocks)

    def one_block(entry):
        query_rows, pos_rows, seq_id = entry
        key_rows = key_seq[seq_id]
        value_rows = value_seq[seq_id]
        raw_score = jnp.einsum('qhd,khd->hqk', query_rows, key_rows, precision=PRECISE) * HD ** (-0.5)
        distance = pos_rows[:, None] - position[None, :]
        bucket_index = jnp.clip(distance, 0, MAXD - 1)
        score = low_back(raw_score + head_table[:, bucket_index])
        score = jnp.where((distance >= 0)[None], score, MASKED)
        shifted = jnp.exp(score - lax.optimization_barrier(jnp.max(score, axis=-1, keepdims=True)))
        weights = shifted / lax.optimization_barrier(jnp.sum(shifted, axis=-1, keepdims=True))
        return jnp.einsum('hqk,khd->qhd', low(weights), value_rows, precision=PRECISE)
    result = lax.map(jax.checkpoint(one_block), (query_seq, pos_blocks, seq_ids))
    result = jnp.transpose(result.reshape(SEQS, SEQ_LEN, HEADS, HD), (1, 0, 2, 3))
    return result.reshape(SEQ_LEN, SEQS, D)

def forward(tokens, gain_one, qkv_weight, out_weight, rel_weight, gain_two, router_weight, expert_in, expert_out, routes, bucket_table):
    position = dealt_positions()
    normed_one = low(norm_apply(tokens, gain_one))
    projected = low_back(low(jnp.einsum('lsd,dce->lsce', normed_one, qkv_weight, precision=PRECISE)))
    head_shape = (SEQ_LEN, SEQS, HEADS, HD)
    query = projected[:, :, 0].reshape(head_shape)
    key_all = projected[:, :, 1].reshape(head_shape)
    value_all = projected[:, :, 2].reshape(head_shape)
    bucket_pick = (bucket_table[:, None] == jnp.arange(BUCKETS, dtype=jnp.int32)[None, :]).astype(jnp.float32)
    head_table = jnp.dot(bucket_pick, rel_weight, precision=PRECISE).T
    attended = low_back(low(attention(query, key_all, value_all, head_table, position)))
    branch = low_back(jnp.einsum('lsd,de->lse', attended, out_weight, precision=PRECISE))
    resid = tokens + branch
    normed_two = norm_apply(resid, gain_two)
    logits = jnp.einsum('lsd,de->lse', normed_two, router_weight, precision=PRECISE)
    shifted = jnp.exp(logits - lax.optimization_barrier(jnp.max(logits, axis=-1, keepdims=True)))
    gate_probs = shifted / lax.optimization_barrier(jnp.sum(shifted, axis=-1, keepdims=True))
    expert_ids = routes[..., 0]
    choose = (expert_ids[..., None] == jnp.arange(EXPERTS, dtype=jnp.int32)).astype(jnp.float32)
    gate_value = lax.optimization_barrier(jnp.sum(gate_probs * choose, axis=-1))
    per_device = expert_ids.reshape(N_CTX, TOK_DEV)
    chosen = (per_device[..., None] == jnp.arange(EXPERTS, dtype=jnp.int32)).astype(jnp.int32)
    filled = jnp.cumsum(chosen, axis=1)
    slot_index = lax.optimization_barrier(jnp.sum((filled - 1) * chosen, axis=2))
    device_ids = jnp.arange(N_CTX, dtype=jnp.int32)[:, None]
    target = (per_device * (N_CTX * CAP) + device_ids * CAP + slot_index).reshape(-1).astype(jnp.int32)
    sent = low_back(low(normed_two)).reshape(-1, D)
    buffer = jnp.zeros((EXPERTS * N_CTX * CAP, D), jnp.float32).at[target].set(sent)
    weight_in_all = jnp.transpose(expert_in.reshape(EXPERTS, 2, D, FF // 2), (0, 2, 1, 3)).reshape(EXPERTS, D, FF)
    weight_out_all = expert_out.reshape(EXPERTS, FF, D)

    def run_expert(entry):
        rows_in, weight_first, weight_second = entry
        pre_act = low_back(jnp.dot(rows_in, weight_first, precision=PRECISE))
        hidden = low(jax.nn.gelu(pre_act, approximate=False))
        return jnp.dot(hidden, weight_second, precision=PRECISE)
    outputs = lax.map(jax.checkpoint(run_expert), (buffer.reshape(EXPERTS, N_CTX * CAP, D), weight_in_all, weight_out_all))
    expert_rows = low_back(outputs.reshape(-1, D)[target].reshape(SEQ_LEN, SEQS, D))
    return resid + gate_value[..., None] * expert_rows

def reference(tokens, gain_one, qkv_weight, out_weight, rel_weight, gain_two, router_weight, expert_in, expert_out, routes, bucket_table, grad_out):
    layer = partial(forward, routes=routes, bucket_table=bucket_table)
    primals = (tokens.astype(jnp.float32), gain_one, qkv_weight.astype(jnp.float32), out_weight.astype(jnp.float32), rel_weight, gain_two, router_weight, expert_in.astype(jnp.float32), expert_out.astype(jnp.float32))
    result, pullback = jax.vjp(layer, *primals)
    grads = pullback(grad_out.astype(jnp.float32))
    return (result.astype(jnp.bfloat16), grads[0], grads[1], grads[2], grads[3], grads[4], grads[5], grads[6], grads[7], grads[8])
```

```python
import jax
import jax.numpy as jnp
from jax import lax
from jax.experimental import pallas as pl
from jax.experimental.pallas import tpu as pltpu
from jax.sharding import PartitionSpec as P

HD = 64
MAXD = 128
BLK = 64


EPSILON = 1e-06
MASKED = -1e30
PRECISE = lax.Precision.HIGHEST


def norm_forward(values, gain_vec):
    inverse = lax.rsqrt(jnp.mean(values * values, axis=-1, keepdims=True) + EPSILON)
    return (values * inverse * gain_vec, inverse)


def norm_backward(values, inverse, gain_vec, gradient):
    weighted = gradient * gain_vec
    inner_mean = jnp.mean(weighted * values, axis=-1, keepdims=True)
    grad_values = inverse * weighted - values * inverse**3 * inner_mean
    grad_gain = jnp.sum(gradient * values * inverse, axis=0)
    return (grad_values, grad_gain)


def exact_gelu(values):
    return jax.nn.gelu(values, approximate=False)


def dealt_positions(first_row, row_total, devices):
    row_ids = first_row + lax.iota(jnp.int32, row_total)
    owner_dev = row_ids // (2 * BLK)
    within = row_ids % (2 * BLK)
    early_pos = owner_dev * BLK + within
    late_pos = (2 * devices - 1 - owner_dev) * BLK + within - BLK
    return jnp.where(within < BLK, early_pos, late_pos)


def block_size():
    return 512


def split_heads(packed, head_count):
    return packed.reshape(
        packed.shape[0], packed.shape[1], head_count, packed.shape[2] // head_count
    )


def run_bias(pos_query, pos_keys, head_table):
    span = 2 * BLK - 1
    starts_query = pos_query[::BLK]
    starts_keys = pos_keys[::BLK]
    query_runs = starts_query.shape[0]
    key_runs = starts_keys.shape[0]
    head_count = head_table.shape[0]
    offsets = lax.iota(jnp.int32, span) - (BLK - 1)
    distance = starts_query[:, None, None] - starts_keys[None, :, None] + offsets[None, None, :]
    clipped = jnp.clip(distance, 0, MAXD - 1)
    onehot = (clipped.reshape(-1)[:, None] == lax.iota(jnp.int32, MAXD)[None, :]).astype(
        jnp.float32
    )
    diag_values = jnp.dot(onehot, head_table.T, precision=PRECISE)
    diag_values = jnp.transpose(
        diag_values.reshape(query_runs, key_runs, span, head_count), (3, 0, 1, 2)
    )
    tiled = jnp.tile(diag_values, (1, 1, 1, BLK + 1))[..., : BLK * (span + 1)]
    tiled = tiled.reshape(head_count, query_runs, key_runs, BLK, span + 1)[..., :BLK][..., ::-1]
    bias = jnp.transpose(tiled, (1, 3, 0, 2, 4)).reshape(
        query_runs * BLK, head_count, key_runs * BLK
    )
    return (bias[:, None], onehot)


def score_block(query, key_heads, pos_query, pos_keys, head_table):
    raw_score = jnp.einsum(
        "qshd,kshd->qshk", query, key_heads, preferred_element_type=jnp.float32
    ) * HD ** (-0.5)
    distance = pos_query[:, None] - pos_keys[None, :]
    score_bias, onehot = run_bias(pos_query, pos_keys, head_table)
    score = jnp.where((distance >= 0)[:, None, None, :], raw_score + score_bias, MASKED)
    return (score, onehot)


def bias_grad(grad_score, onehot):
    span = 2 * BLK - 1
    summed = jnp.sum(grad_score.astype(jnp.float32), axis=1)
    query_rows, head_count, key_rows = summed.shape
    query_runs = query_rows // BLK
    key_runs = key_rows // BLK
    tiles = jnp.transpose(
        summed.reshape(query_runs, BLK, head_count, key_runs, BLK), (2, 0, 3, 1, 4)
    )[..., ::-1]
    widened = jnp.pad(tiles, ((0, 0), (0, 0), (0, 0), (0, 0), (0, span + 1 - BLK)))
    flat = widened.reshape(head_count, query_runs, key_runs, BLK * (span + 1))
    flat = jnp.pad(flat, ((0, 0), (0, 0), (0, 0), (0, (BLK + 1) * span - BLK * (span + 1))))
    diag_sums = jnp.sum(flat.reshape(head_count, query_runs, key_runs, BLK + 1, span), axis=3)
    diag_rows = jnp.transpose(diag_sums, (1, 2, 3, 0)).reshape(-1, head_count)
    return jnp.dot(onehot.T, diag_rows, precision=PRECISE)


def over_blocks(step_fn, carried, piece):
    piece_rows = piece[0].shape[0]
    step_rows = block_size()
    block_count = piece_rows // step_rows
    blocks = tuple(
        (member.reshape((block_count, step_rows) + member.shape[1:]) for member in piece)
    )
    firsts = step_rows * lax.iota(jnp.int32, block_count)

    def advance(carry_state, scan_item):
        return (step_fn(carry_state, scan_item[0], scan_item[1]), None)

    carried, _ = lax.scan(advance, carried, (blocks, firsts))
    return carried


def local(
    tokens,
    gain_one,
    qkv_weight,
    out_weight,
    rel_weight,
    gain_two,
    router_weight,
    expert_in,
    expert_out,
    routes,
    bucket_table,
    grad_out,
):
    ctx_count = lax.axis_size("ctx")
    row_count, seq_count, model_width = tokens.shape
    token_count = row_count * seq_count
    head_count = qkv_weight.shape[2] // HD
    head_width = head_count * HD
    score_scale = HD ** (-0.5)
    pos_query = dealt_positions(lax.axis_index("ctx") * row_count, row_count, ctx_count)
    token_rows = tokens.astype(jnp.float32).reshape(token_count, model_width)
    normed_one, inverse_one = norm_forward(token_rows, gain_one)
    normed_low = normed_one.astype(jnp.bfloat16)
    projected = jnp.einsum(
        "nd,dce->nce", normed_low, qkv_weight, preferred_element_type=jnp.float32
    ).astype(jnp.bfloat16)
    query_flat = projected[:, 0].reshape(row_count, seq_count, head_width)
    query = split_heads(query_flat, head_count)
    keyval = projected[:, 1:].reshape(row_count, seq_count, 2 * head_width)
    own_keys = split_heads(keyval[..., :head_width], head_count)
    own_values = split_heads(keyval[..., head_width:], head_count)
    bucket_pick = (
        bucket_table[:, None] == lax.iota(jnp.int32, rel_weight.shape[0])[None, :]
    ).astype(jnp.float32)
    head_table = jnp.dot(bucket_pick, rel_weight, precision=PRECISE).T

    def attend(carry_state, key_block, first_row):
        key_heads = split_heads(key_block[0][..., :head_width], head_count)
        value_heads = split_heads(key_block[0][..., head_width:], head_count)
        pos_keys = dealt_positions(first_row, key_heads.shape[0], ctx_count)
        score, _ = score_block(query, key_heads, pos_query, pos_keys, head_table)
        row_max, denominator, weighted = carry_state
        new_max = jnp.maximum(row_max, jnp.max(score, axis=-1))
        rescale = jnp.exp(row_max - new_max)
        weights = jnp.exp(score - new_max[..., None])
        denominator = rescale * denominator + jnp.sum(weights, axis=-1)
        weighted = rescale[..., None] * weighted + jnp.einsum(
            "qshk,kshd->qshd",
            weights.astype(jnp.bfloat16),
            value_heads,
            preferred_element_type=jnp.float32,
        )
        return (new_max, denominator, weighted)

    stat_shape = (row_count, seq_count, head_count)
    zero_heads = jnp.zeros((row_count, seq_count, head_count, HD), jnp.float32)
    initial = (
        jnp.full(stat_shape, MASKED, jnp.float32),
        jnp.zeros(stat_shape, jnp.float32),
        zero_heads,
    )
    row_max, denominator, weighted = over_blocks(
        attend, initial, (lax.all_gather(keyval, "ctx", axis=0, tiled=True),)
    )
    attended = weighted / denominator[..., None]
    log_total = row_max + jnp.log(denominator)
    attended_low = attended.reshape(token_count, head_width).astype(jnp.bfloat16)
    branch = lax.psum(
        jnp.dot(attended_low, out_weight, preferred_element_type=jnp.float32).astype(jnp.bfloat16),
        "wsh",
    ).astype(jnp.float32)
    resid = token_rows + branch
    normed_two, inverse_two = norm_forward(resid, gain_two)
    logits = jnp.dot(normed_two, router_weight, precision=PRECISE)
    shifted = jnp.exp(logits - jnp.max(logits, axis=-1, keepdims=True))
    gate_probs = shifted / jnp.sum(shifted, axis=-1, keepdims=True)
    expert_count = router_weight.shape[1]
    expert_ids = routes.reshape(token_count)
    choose = expert_ids[:, None] == lax.iota(jnp.int32, expert_count)[None, :]
    gate_value = jnp.sum(jnp.where(choose, gate_probs, 0.0), axis=1)
    lower_ones = (
        lax.iota(jnp.int32, token_count)[:, None] >= lax.iota(jnp.int32, token_count)[None, :]
    ).astype(jnp.bfloat16)
    filled = jnp.dot(
        lower_ones, choose.astype(jnp.bfloat16), preferred_element_type=jnp.float32
    ).astype(jnp.int32)
    slot_index = jnp.sum(jnp.where(choose, filled - 1, 0), axis=1)
    capacity = max(2, 2 * token_count // expert_count)
    target = expert_ids * capacity + slot_index
    slot_pick = target[:, None] == lax.iota(jnp.int32, expert_count * capacity)[None, :]
    slot_low = slot_pick.astype(jnp.bfloat16)
    slot_full = slot_pick.astype(jnp.float32)
    weight_in = expert_in[0]
    weight_out = expert_out[0]

    def spread(values):
        buffer = jnp.einsum(
            "nm,nd->md", slot_low, values, preferred_element_type=jnp.float32
        ).astype(jnp.bfloat16)
        doubled = jnp.broadcast_to(
            buffer.reshape(expert_count, 1, capacity, model_width),
            (expert_count, 2, capacity, model_width),
        )
        return doubled.reshape(2 * expert_count, capacity, model_width)

    def collect(returned):
        row_width = returned.shape[-1]
        paired = jnp.sum(returned.reshape(expert_count, 2, capacity, row_width), axis=1)
        return jnp.dot(
            slot_full, paired.reshape(expert_count * capacity, row_width), precision=PRECISE
        )

    arrived_rows = lax.all_to_all(
        spread(normed_two.astype(jnp.bfloat16)), "ctx", split_axis=0, concat_axis=0, tiled=True
    )
    flat_rows = arrived_rows.reshape(-1, model_width)
    pre_act = jnp.dot(flat_rows, weight_in, preferred_element_type=jnp.float32)
    hidden = exact_gelu(pre_act).astype(jnp.bfloat16)
    returned = lax.all_to_all(
        jnp.dot(hidden, weight_out, preferred_element_type=jnp.float32)
        .reshape(arrived_rows.shape)
        .astype(jnp.bfloat16),
        "ctx",
        split_axis=0,
        concat_axis=0,
        tiled=True,
    ).astype(jnp.float32)
    expert_rows = lax.psum(collect(returned).astype(jnp.bfloat16), "wsh").astype(jnp.float32)
    result = resid + gate_value[:, None] * expert_rows
    out = result.astype(jnp.bfloat16).reshape(row_count, seq_count, model_width)
    grad_rows_f = grad_out.astype(jnp.float32).reshape(token_count, model_width)
    grad_gate = jnp.sum(grad_rows_f * expert_rows, axis=1)
    grad_expert_rows = (gate_value[:, None] * grad_rows_f).astype(jnp.bfloat16)
    arrived_grad = lax.all_to_all(
        spread(grad_expert_rows), "ctx", split_axis=0, concat_axis=0, tiled=True
    )
    flat_rows = arrived_rows.reshape(-1, model_width)
    flat_grad = arrived_grad.reshape(-1, model_width)
    pre_act = jnp.dot(flat_rows, weight_in, preferred_element_type=jnp.float32)
    hidden, gelu_pull = jax.vjp(exact_gelu, pre_act)
    hidden_low = hidden.astype(jnp.bfloat16)
    grad_weight_out = jnp.einsum(
        "rf,rd->fd", hidden_low, flat_grad, preferred_element_type=jnp.float32
    )
    grad_hidden = jnp.einsum("rd,fd->rf", flat_grad, weight_out, preferred_element_type=jnp.float32)
    grad_pre = gelu_pull(grad_hidden)[0].astype(jnp.bfloat16)
    grad_weight_in = jnp.einsum(
        "rd,rf->df", flat_rows, grad_pre, preferred_element_type=jnp.float32
    )
    partial_back = jnp.einsum(
        "rf,df->rd", grad_pre, weight_in, preferred_element_type=jnp.float32
    ).reshape(arrived_rows.shape)
    returned_grad = lax.all_to_all(
        partial_back.astype(jnp.bfloat16), "ctx", split_axis=0, concat_axis=0, tiled=True
    ).astype(partial_back.dtype)
    grad_sent = lax.psum(collect(returned_grad).astype(jnp.bfloat16), "wsh").astype(jnp.float32)
    grad_sent = lax.optimization_barrier(grad_sent.astype(jnp.bfloat16)).astype(jnp.float32)
    grad_logits = gate_probs * (
        jnp.where(choose, grad_gate[:, None], 0.0) - (gate_value * grad_gate)[:, None]
    )
    grad_router = jnp.dot(normed_two.T, grad_logits, precision=PRECISE)
    grad_normed_two = grad_sent + jnp.dot(grad_logits, router_weight.T, precision=PRECISE)
    grad_resid, grad_gain_two = norm_backward(resid, inverse_two, gain_two, grad_normed_two)
    grad_resid = grad_resid + grad_rows_f
    grad_branch = grad_resid.astype(jnp.bfloat16)
    grad_out_rows = jnp.einsum(
        "nw,nd->wd", attended_low, grad_branch, preferred_element_type=jnp.float32
    )
    grad_att = jnp.einsum(
        "nd,wd->nw", grad_branch, out_weight, preferred_element_type=jnp.float32
    ).astype(jnp.bfloat16)
    grad_att_flat = grad_att.reshape(row_count, seq_count, head_width)
    grad_att_heads = split_heads(grad_att_flat, head_count)
    row_inner = jnp.sum(grad_att_heads.astype(jnp.float32) * attended, axis=-1)

    def query_grads(carry_state, key_block, first_row):
        key_heads = split_heads(key_block[0][..., :head_width], head_count)
        value_heads = split_heads(key_block[0][..., head_width:], head_count)
        pos_keys = dealt_positions(first_row, key_heads.shape[0], ctx_count)
        score, onehot = score_block(query, key_heads, pos_query, pos_keys, head_table)
        weights = jnp.exp(score - log_total[..., None])
        grad_weights = jnp.einsum(
            "qshd,kshd->qshk", grad_att_heads, value_heads, preferred_element_type=jnp.float32
        )
        grad_score = (weights * (grad_weights - row_inner[..., None])).astype(jnp.bfloat16)
        grad_query = (
            carry_state[0]
            + jnp.einsum(
                "qshk,kshd->qshd", grad_score, key_heads, preferred_element_type=jnp.float32
            )
            * score_scale
        )
        return (grad_query, carry_state[1] + bias_grad(grad_score, onehot))

    def key_grads(carry_state, query_block, first_row):
        query_heads = split_heads(query_block[0][..., :head_width], head_count)
        grad_heads = split_heads(query_block[0][..., head_width:], head_count)
        pos_rows = dealt_positions(first_row, query_heads.shape[0], ctx_count)
        score, _ = score_block(query_heads, own_keys, pos_rows, pos_query, head_table)
        weights = jnp.exp(score - query_block[1][..., None])
        grad_value = carry_state[1] + jnp.einsum(
            "qshk,qshd->kshd",
            weights.astype(jnp.bfloat16),
            grad_heads,
            preferred_element_type=jnp.float32,
        )
        grad_weights = jnp.einsum(
            "qshd,kshd->qshk", grad_heads, own_values, preferred_element_type=jnp.float32
        )
        grad_score = (weights * (grad_weights - query_block[2][..., None])).astype(jnp.bfloat16)
        grad_key = (
            carry_state[0]
            + jnp.einsum(
                "qshk,qshd->kshd", grad_score, query_heads, preferred_element_type=jnp.float32
            )
            * score_scale
        )
        return (grad_key, grad_value)

    packed = jnp.concatenate([query_flat, grad_att_flat], axis=-1)
    zero_table = jnp.zeros((MAXD, head_count), jnp.float32)
    grad_query, grad_table = over_blocks(
        query_grads, (zero_heads, zero_table), (lax.all_gather(keyval, "ctx", axis=0, tiled=True),)
    )
    grad_key, grad_value = over_blocks(
        key_grads,
        (zero_heads, zero_heads),
        (
            lax.all_gather(packed, "ctx", axis=0, tiled=True),
            lax.all_gather(log_total.astype(jnp.bfloat16), "ctx", axis=0, tiled=True).astype(
                jnp.float32
            ),
            lax.all_gather(row_inner.astype(jnp.bfloat16), "ctx", axis=0, tiled=True).astype(
                jnp.float32
            ),
        ),
    )
    grad_projected = jnp.stack(
        [member.reshape(token_count, head_width) for member in (grad_query, grad_key, grad_value)],
        axis=1,
    ).astype(jnp.bfloat16)
    grad_normed_one = lax.psum(
        jnp.einsum(
            "nce,dce->nd", grad_projected, qkv_weight, preferred_element_type=jnp.float32
        ).astype(jnp.bfloat16),
        "wsh",
    ).astype(jnp.float32)
    grad_qkv = jnp.einsum(
        "nd,nce->dce", normed_low, grad_projected, preferred_element_type=jnp.float32
    )
    grad_tokens, grad_gain_one = norm_backward(token_rows, inverse_one, gain_one, grad_normed_one)
    grad_tokens = grad_tokens + grad_resid
    grad_rel = jnp.dot(bucket_pick.T, grad_table, precision=PRECISE)
    summed_grads = lax.psum(
        (grad_qkv, grad_out_rows, grad_rel, grad_gain_one, grad_gain_two, grad_router), "ctx"
    )
    return (
        out,
        grad_tokens.reshape(row_count, seq_count, model_width),
        summed_grads[3],
        summed_grads[0],
        summed_grads[1],
        summed_grads[2],
        summed_grads[4],
        summed_grads[5],
        grad_weight_in[None],
        grad_weight_out[None],
    )


NT = (((1,), (1,)), ((), ()))
TN = (((0,), (0,)), ((), ()))
SEQ_CHIPS = 4


def strip(step, side):
    width = 128 * (step + 1) if side == 0 else 128 * (8 - step)
    first = 0 if side == 0 else 128 * (step + 1)
    return (width, first)


def attend_kernel(ids_ref, own_ref, other_ref, bias_ref, att_ref, prob_ref, keyval_ref):
    chip = ids_ref[0]
    core = ids_ref[1]

    def gather_keys(parity):
        for place in range(16):
            owner = place if place < 8 else 15 - place
            half = 0 if place < 8 else BLK
            source = own_ref if owner % 2 == parity else other_ref
            keyval_ref[place * BLK : (place + 1) * BLK, :] = source[
                chip ^ (owner // 2), half : half + BLK, :384
            ]

    @pl.when(core == 0)
    def _():
        gather_keys(0)

    @pl.when(core == 1)
    def _():
        gather_keys(1)

    for head in range(3):
        for step in range(4):
            for side in range(2):
                width, first = strip(step, side)
                rows = slice(side * BLK, (side + 1) * BLK)
                query = own_ref[chip ^ step, rows, 384 + HD * head : 384 + HD * (head + 1)]
                query = query * jnp.bfloat16(HD ** (-0.5))
                keys = keyval_ref[:width, HD * head : HD * (head + 1)]
                values = keyval_ref[:width, 192 + HD * head : 192 + HD * (head + 1)]
                score = lax.dot_general(query, keys, NT, preferred_element_type=jnp.float32)
                near = min(width, 256)
                close = score[:, width - near :] + bias_ref[head, side, :, 256 - near :]
                if width > near:
                    score = jnp.concatenate([score[:, : width - near], close], axis=1)
                else:
                    score = close
                top = jnp.max(score, axis=-1, keepdims=True)
                weights = jnp.exp(score - top)
                total = jnp.sum(weights, axis=-1, keepdims=True)
                prob = (weights * (1.0 / total)).astype(jnp.bfloat16)
                prob_ref[head, step, :, first : first + width] = prob
                mixed = jnp.dot(prob, values, preferred_element_type=jnp.float32)
                att_ref[chip ^ step, rows, HD * head : HD * (head + 1)] = mixed.astype(jnp.bfloat16)


def attend_back_kernel(
    ids_ref, own_ref, prob_ref, keyval_ref, grad_ref, dq_ref, mine_ref, theirs_ref, near_ref, total_ref
):
    chip = ids_ref[0]
    core = ids_ref[1]
    total_ref[...] = jnp.zeros_like(total_ref)
    near_ref[...] = jnp.zeros_like(near_ref)
    for head in range(3):
        key_cols = slice(HD * head, HD * (head + 1))
        value_cols = slice(192 + HD * head, 192 + HD * (head + 1))
        for step in range(4):
            for side in range(2):
                width, first = strip(step, side)
                rows = slice(side * BLK, (side + 1) * BLK)
                query = own_ref[chip ^ step, rows, 384 + HD * head : 384 + HD * (head + 1)]
                query = query * jnp.bfloat16(HD ** (-0.5))
                grad = grad_ref[chip ^ step, rows, key_cols]
                keys = keyval_ref[:width, key_cols]
                values = keyval_ref[:width, value_cols]
                prob = prob_ref[head, step, :, first : first + width]
                wide = prob.astype(jnp.float32)
                grad_prob = lax.dot_general(grad, values, NT, preferred_element_type=jnp.float32)
                product = wide * grad_prob
                inner = jnp.sum(product, axis=-1, keepdims=True)
                low = (product - wide * inner).astype(jnp.bfloat16)
                dq = jnp.dot(low, keys, preferred_element_type=jnp.float32) * HD ** (-0.5)
                dq_ref[chip ^ step, rows, key_cols] = dq.astype(jnp.bfloat16)
                total_ref[:width, key_cols] += lax.dot_general(
                    low, query, TN, preferred_element_type=jnp.float32
                )
                total_ref[:width, value_cols] += lax.dot_general(
                    prob, grad, TN, preferred_element_type=jnp.float32
                )
                score = low.astype(jnp.float32)
                near_ref[head, 2 * side] += score[:, width - 128 :]
                if width >= 256:
                    near_ref[head, 2 * side + 1] += score[:, width - 256 : width - 128]
                if width > 256:
                    far = score[:, :128]
                    for chunk in range(1, (width - 256) // 128):
                        far = far + score[:, 128 * chunk : 128 * (chunk + 1)]
                    near_ref[head, 4] += far

    def scatter_keys(parity):
        for place in range(16):
            owner = place if place < 8 else 15 - place
            half = 0 if place < 8 else BLK
            target = mine_ref if owner % 2 == parity else theirs_ref
            target[chip ^ (owner // 2), half : half + BLK, :] = total_ref[
                place * BLK : (place + 1) * BLK, :
            ].astype(jnp.bfloat16)

    @pl.when(core == 0)
    def _():
        scatter_keys(0)

    @pl.when(core == 1)
    def _():
        scatter_keys(1)


def in_vmem(count):
    return [pl.BlockSpec(memory_space=pltpu.VMEM)] * count


def attend_call(ids, own, other, bias):
    return pl.pallas_call(
        attend_kernel,
        out_shape=(
            jax.ShapeDtypeStruct((4, 128, 192), jnp.bfloat16),
            jax.ShapeDtypeStruct((3, 4, BLK, 1152), jnp.bfloat16),
            jax.ShapeDtypeStruct((1024, 384), jnp.bfloat16),
        ),
        in_specs=[pl.BlockSpec(memory_space=pltpu.SMEM)] + in_vmem(3),
        out_specs=tuple(in_vmem(3)),
        compiler_params=pltpu.CompilerParams(vmem_limit_bytes=32 * 1024 * 1024),
        cost_estimate=pl.CostEstimate(
            flops=3 * 4 * 64 * 1152 * 256, bytes_accessed=4_000_000, transcendentals=900_000
        ),
        name="attend",
    )(ids, own, other, bias)


def attend_back_call(ids, own, prob, keyval, grad):
    return pl.pallas_call(
        attend_back_kernel,
        out_shape=(
            jax.ShapeDtypeStruct((4, 128, 192), jnp.bfloat16),
            jax.ShapeDtypeStruct((4, 128, 384), jnp.bfloat16),
            jax.ShapeDtypeStruct((4, 128, 384), jnp.bfloat16),
            jax.ShapeDtypeStruct((3, 5, BLK, 128), jnp.float32),
        ),
        in_specs=[pl.BlockSpec(memory_space=pltpu.SMEM)] + in_vmem(4),
        out_specs=tuple(in_vmem(4)),
        scratch_shapes=[pltpu.VMEM((1024, 384), jnp.float32)],
        compiler_params=pltpu.CompilerParams(vmem_limit_bytes=32 * 1024 * 1024),
        cost_estimate=pl.CostEstimate(
            flops=3 * 4 * 64 * 1152 * 640, bytes_accessed=5_000_000, transcendentals=0
        ),
        name="attend_back",
    )(ids, own, prob, keyval, grad)


def to_core(values):
    return lax.ppermute(values, "ctx", [(at, at ^ 1) for at in range(8)])


def to_chip(values, away):
    return lax.ppermute(values, "ctx", [(at, at ^ (2 * away)) for at in range(8)])


def to_plane(values, away):
    return lax.ppermute(values, "wsh", [(at, at ^ away) for at in range(4)])


def chip_swap(blocks):
    return jnp.stack([blocks[0]] + [to_chip(blocks[away], away) for away in range(1, 4)])


def pick(blocks, at):
    return lax.dynamic_index_in_dim(blocks, at, 0, keepdims=False)


def near_distance(core):
    parity = jnp.stack([core, 1 - core])
    lag = lax.iota(jnp.int32, 319) - 63
    return BLK * parity[:, None] + 128 - lag[None, :]


def bias_tiles(head_table, core):
    distance = near_distance(core)
    clipped = jnp.clip(distance, 0, MAXD - 1)
    onehot = (clipped[..., None] == lax.iota(jnp.int32, MAXD)).astype(jnp.float32)
    shifted = head_table - head_table[:, MAXD - 1 :]
    lagged = jnp.einsum("pzd,hd->hpz", onehot, shifted, precision=PRECISE)
    lagged = jnp.where((distance >= 0)[None], lagged, MASKED)
    rolled = jnp.concatenate([lagged[..., 63:], lagged[..., :63]], axis=-1)
    tiled = jnp.tile(rolled, (1, 1, BLK))[..., : BLK * 318]
    return tiled.reshape(3, 2, BLK, 318)[..., :256]


def table_grad(near, core):
    wide = jnp.pad(near[:, :4], ((0, 0), (0, 0), (0, 0), (0, 127)))
    flat = jnp.pad(wide.reshape(3, 4, BLK * 255), ((0, 0), (0, 0), (0, BLK)))
    lags = jnp.sum(flat.reshape(3, 4, BLK, 256), axis=2)
    offsets = lax.iota(jnp.int32, 256)
    offsets = jnp.where(offsets < 128, offsets, offsets - 256)
    base = BLK * jnp.stack([core, core + 2, 1 - core, 3 - core])
    clipped = jnp.clip(base[:, None] - offsets[None, :], 0, MAXD - 1)
    onehot = (clipped[..., None] == lax.iota(jnp.int32, MAXD)).astype(jnp.float32)
    table = jnp.einsum("hkz,kzd->dh", lags, onehot, precision=PRECISE)
    return table.at[MAXD - 1].add(jnp.sum(near[:, 4], axis=(1, 2)))


def gelu_parts(values):
    cdf = 0.5 * (1.0 + lax.erf(values * (0.5**0.5)))
    density = jnp.exp(-0.5 * values * values) * ((0.5 / jnp.pi) ** 0.5)
    return (values * cdf, cdf + values * density)


def local_planned(
    tokens,
    gain_one,
    qkv_weight,
    out_weight,
    rel_weight,
    gain_two,
    router_weight,
    expert_in,
    expert_out,
    routes,
    bucket_table,
    grad_out,
):
    row_count, seq_count, width = tokens.shape
    token_count = row_count * seq_count
    expert_count = router_weight.shape[1]
    capacity = 2 * token_count // expert_count
    ctx_at = lax.axis_index("ctx")
    plane = lax.axis_index("wsh")
    chip = ctx_at // 2
    core = ctx_at % 2
    ids = jnp.stack([chip, core]).astype(jnp.int32)

    def by_chip(values):
        turned = jnp.swapaxes(values, 0, 1)
        return jnp.stack([pick(turned, chip ^ away) for away in range(4)])

    token_blocks = by_chip(tokens)
    token_rows = token_blocks.reshape(token_count, width).astype(jnp.float32)
    normed_one, inverse_one = norm_forward(token_rows, gain_one)
    normed_low = normed_one.astype(jnp.bfloat16)
    weight_qkv = jnp.concatenate([qkv_weight[:, 1], qkv_weight[:, 2], qkv_weight[:, 0]], axis=1)
    projected = jnp.dot(normed_low, weight_qkv, preferred_element_type=jnp.float32)
    projected = projected.astype(jnp.bfloat16).reshape(4, 128, 576)
    own = chip_swap(projected)
    other = to_core(own[..., :384])

    bucket_pick = (
        bucket_table[:, None] == lax.iota(jnp.int32, rel_weight.shape[0])[None, :]
    ).astype(jnp.float32)
    head_table = jnp.dot(bucket_pick, rel_weight, precision=PRECISE).T
    bias = bias_tiles(head_table, core)
    out_weights = [out_weight] + [to_plane(out_weight, away) for away in range(1, 4)]

    def gather_weights(weight):
        near = jnp.stack([weight] + [to_chip(weight, away) for away in range(1, 4)])
        return (near, to_core(near))

    weights_in = gather_weights(expert_in[0])
    weights_out = gather_weights(expert_out[0])

    grad_blocks = by_chip(grad_out)
    grad_low = grad_blocks.reshape(token_count, width)
    route_rel = by_chip(routes).reshape(token_count) ^ chip
    choose = route_rel[:, None] == lax.iota(jnp.int32, expert_count)[None, :]
    lower_ones = (
        lax.iota(jnp.int32, token_count)[:, None] >= lax.iota(jnp.int32, token_count)[None, :]
    ).astype(jnp.bfloat16)
    filled = jnp.dot(
        lower_ones, choose.astype(jnp.bfloat16), preferred_element_type=jnp.float32
    ).astype(jnp.int32)
    slot_index = jnp.sum(jnp.where(choose, filled - 1, 0), axis=1)
    target = route_rel * capacity + slot_index
    slot_pick = target[:, None] == lax.iota(jnp.int32, expert_count * capacity)[None, :]
    slot_low = slot_pick.astype(jnp.bfloat16)

    def spread(values):
        placed = jnp.einsum("nm,nd->md", slot_low, values, preferred_element_type=jnp.float32)
        return placed.astype(jnp.bfloat16).reshape(expert_count, capacity, width)

    grad_slots = spread(grad_low)
    grad_hidden = [
        jnp.einsum("mnd,mfd->mnf", grad_slots, part, preferred_element_type=jnp.float32)
        for part in weights_out
    ]

    mixed, prob, keyval = attend_call(ids, own, other, bias)
    attended = chip_swap(mixed)
    att_rows = attended.reshape(token_count, 192)
    branch = jnp.dot(att_rows, out_weight, preferred_element_type=jnp.float32)
    for away in range(1, 4):
        branch = branch + jnp.dot(
            to_plane(att_rows, away), out_weights[away], preferred_element_type=jnp.float32
        )
    resid = token_rows + branch
    normed_two, inverse_two = norm_forward(resid, gain_two)
    logits = jnp.dot(normed_two, router_weight, precision=PRECISE)
    shifted = jnp.exp(logits - jnp.max(logits, axis=-1, keepdims=True))
    gate_probs = shifted / jnp.sum(shifted, axis=-1, keepdims=True)
    local_choose = by_chip(routes).reshape(token_count)[:, None] == lax.iota(
        jnp.int32, expert_count
    )
    gate_value = jnp.sum(jnp.where(local_choose, gate_probs, 0.0), axis=1)

    sent_slots = spread(normed_two.astype(jnp.bfloat16))
    back = 0.0
    inner = 0.0
    hidden_parts = []
    grad_pre_parts = []
    for part in range(2):
        pre_act = jnp.einsum(
            "mnd,mdf->mnf", sent_slots, weights_in[part], preferred_element_type=jnp.float32
        )
        hidden, slope = gelu_parts(pre_act)
        hidden_low = hidden.astype(jnp.bfloat16)
        inner = inner + jnp.sum(hidden_low.astype(jnp.float32) * grad_hidden[part], axis=-1)
        grad_pre = (grad_hidden[part] * slope).astype(jnp.bfloat16)
        back = back + jnp.einsum(
            "mnf,mdf->mnd", grad_pre, weights_in[part], preferred_element_type=jnp.float32
        )
        hidden_parts.append(hidden_low)
        grad_pre_parts.append(grad_pre)
    slots = expert_count * capacity
    inner = inner.reshape(slots, 1)
    inner_high = inner.astype(jnp.bfloat16)
    inner_low = (inner - inner_high.astype(jnp.float32)).astype(jnp.bfloat16)
    lane = lax.iota(jnp.int32, 128)[None, :]
    extra = jnp.where(lane == 0, inner_high, jnp.where(lane == 1, inner_low, jnp.bfloat16(0)))
    payload = jnp.concatenate([back.astype(jnp.bfloat16).reshape(slots, width), extra], axis=1)
    slot_blocks = slot_low.reshape(4, 128, slots)

    def collect_sum(values):
        total = 0.0
        for away in range(4):
            part = jnp.dot(
                pick(slot_blocks, plane ^ away), values, preferred_element_type=jnp.float32
            ).astype(jnp.bfloat16)
            if away:
                part = to_plane(part, away)
            total = total + part.astype(jnp.float32)
        return total

    def mine(values):
        return pick(values.reshape((4, 128) + values.shape[1:]), plane)

    collected = collect_sum(payload)
    my_gate = mine(gate_value)[:, None]
    grad_gate = collected[:, width : width + 1] + collected[:, width + 1 : width + 2]
    grad_sent = (collected[:, :width] * my_gate).astype(jnp.bfloat16).astype(jnp.float32)
    my_probs = mine(gate_probs)
    my_choose = mine(local_choose)
    my_resid = mine(resid)
    my_normed = mine(normed_two)
    my_grad = mine(grad_low).astype(jnp.float32)
    grad_logits = my_probs * (jnp.where(my_choose, grad_gate, 0.0) - my_gate * grad_gate)
    grad_router = jnp.dot(my_normed.T, grad_logits, precision=PRECISE)
    grad_normed_two = grad_sent + jnp.dot(grad_logits, router_weight.T, precision=PRECISE)
    grad_resid, grad_gain_two = norm_backward(
        my_resid, mine(inverse_two), gain_two, grad_normed_two
    )
    grad_resid = grad_resid + my_grad
    grad_branch = grad_resid.astype(jnp.bfloat16)
    grad_att = []
    for away in range(4):
        part = lax.dot_general(
            grad_branch, out_weights[away], NT, preferred_element_type=jnp.float32
        ).astype(jnp.bfloat16)
        grad_att.append(to_plane(part, away) if away else part)
    grad_att = jnp.stack(grad_att)
    grad_mixed = jnp.stack(
        [pick(grad_att, plane)]
        + [to_chip(pick(grad_att, plane ^ away), away) for away in range(1, 4)]
    )

    dq, mine_kv, theirs_kv, near = attend_back_call(ids, own, prob, keyval, grad_mixed)
    dkv = mine_kv.astype(jnp.float32) + to_core(theirs_kv).astype(jnp.float32)
    grad_projected = chip_swap(jnp.concatenate([dkv.astype(jnp.bfloat16), dq], axis=-1))

    grad_normed_one = 0.0
    for away in range(4):
        part = lax.dot_general(
            pick(grad_projected, plane ^ away), weight_qkv, NT, preferred_element_type=jnp.float32
        ).astype(jnp.bfloat16)
        if away:
            part = to_plane(part, away)
        grad_normed_one = grad_normed_one + part.astype(jnp.float32)
    my_tokens = mine(token_rows)
    my_grad_tokens, grad_gain_one = norm_backward(
        my_tokens, mine(inverse_one), gain_one, grad_normed_one
    )

    def spread_planes(block):
        gathered = jnp.stack([block] + [to_plane(block, away) for away in range(1, 4)])
        by_seq = jnp.stack([pick(gathered, at ^ chip ^ plane) for at in range(4)])
        return jnp.swapaxes(by_seq, 0, 1)

    grad_tokens = spread_planes((my_grad_tokens + grad_resid).astype(jnp.bfloat16)).astype(
        jnp.float32
    )

    expert_part = 0.0
    for part in range(2):
        expert_part = expert_part + jnp.einsum(
            "mnf,mfd->mnd", hidden_parts[part], weights_out[part], preferred_element_type=jnp.float32
        )
    expert_rows = collect_sum(expert_part.astype(jnp.bfloat16).reshape(slots, width))
    out = spread_planes((my_resid + my_gate * expert_rows).astype(jnp.bfloat16))

    gate_slots = jnp.sum(jnp.where(slot_pick, gate_value[:, None], 0.0), axis=0)
    gate_slots = gate_slots.reshape(expert_count, capacity, 1)
    grad_row_slots = (grad_slots.astype(jnp.float32) * gate_slots).astype(jnp.bfloat16)

    def reduce_weight(parts):
        near = parts[0] + to_core(parts[1].astype(jnp.bfloat16)).astype(jnp.float32)
        total = near[0]
        for away in range(1, 4):
            total = total + to_chip(near[away].astype(jnp.bfloat16), away).astype(jnp.float32)
        return total[None]

    grad_weight_out = reduce_weight(
        [
            jnp.einsum("mnf,mnd->mfd", part, grad_row_slots, preferred_element_type=jnp.float32)
            for part in hidden_parts
        ]
    )
    grad_weight_in = reduce_weight(
        [
            jnp.einsum(
                "mnd,mnf->mdf",
                sent_slots,
                (part.astype(jnp.float32) * gate_slots).astype(jnp.bfloat16),
                preferred_element_type=jnp.float32,
            )
            for part in grad_pre_parts
        ]
    )

    grad_out_rows = 0.0
    for away in range(4):
        rows = to_plane(grad_branch, away) if away else grad_branch
        grad_out_rows = grad_out_rows + lax.dot_general(
            pick(attended, plane ^ away), rows, TN, preferred_element_type=jnp.float32
        )
    grad_qkv = lax.dot_general(
        normed_low,
        grad_projected.reshape(token_count, 576),
        TN,
        preferred_element_type=jnp.float32,
    )
    grad_qkv, grad_out_rows = lax.psum(
        (grad_qkv.astype(jnp.bfloat16), grad_out_rows.astype(jnp.bfloat16)), "ctx"
    )
    grad_qkv = grad_qkv.astype(jnp.float32)
    grad_qkv = jnp.stack([grad_qkv[:, 384:], grad_qkv[:, :192], grad_qkv[:, 192:384]], axis=1)

    grad_rel = jnp.dot(bucket_pick.T, table_grad(near, core), precision=PRECISE)
    slots_rel = jnp.where(
        (lax.iota(jnp.int32, 4) == plane)[None, :, None], grad_rel[:, None, :], 0.0
    ).reshape(-1)
    small = jnp.concatenate(
        [
            grad_gain_one,
            grad_gain_two,
            grad_router.reshape(-1),
            slots_rel,
            jnp.zeros((width - slots_rel.shape[0],), jnp.float32),
        ]
    ).reshape(-1, width)
    small = small + to_core(small)
    small = small + to_chip(small, 1)
    small = small + to_chip(small, 2)
    small = small + to_plane(small, 1)
    small = small + to_plane(small, 2)
    grad_rel = pick(
        jnp.swapaxes(small[6].reshape(-1)[: slots_rel.shape[0]].reshape(-1, 4, 3), 0, 1), plane
    )
    return (
        out,
        grad_tokens,
        small[0],
        grad_qkv,
        grad_out_rows.astype(jnp.float32),
        grad_rel,
        small[1],
        small[2:6].reshape(width, expert_count),
        grad_weight_in,
        grad_weight_out,
    )


def solution(mesh):
    placed = (
        P("ctx", None, None),
        P(),
        P(None, None, "wsh"),
        P("wsh", None),
        P(None, "wsh"),
        P(),
        P(),
        P("ctx", None, "wsh"),
        P("ctx", "wsh", None),
        P("ctx", None, None),
        P(),
        P("ctx", None, None),
    )
    planned = mesh.shape['ctx'] == 8 and mesh.shape['wsh'] == 4
    return jax.shard_map(
        local_planned if planned else local,
        mesh=mesh,
        in_specs=placed,
        out_specs=(
            P("ctx", None, None),
            P("ctx", None, None),
            P(),
            P(None, None, "wsh"),
            P("wsh", None),
            P(None, "wsh"),
            P(),
            P(),
            P("ctx", None, "wsh"),
            P("ctx", "wsh", None),
        ),
        check_vma=False,
    )
```

```python
import functools

import jax
import jax.numpy as jnp
from jax import lax
from jax.experimental import pallas as pl
from jax.experimental.pallas import tpu as pltpu
from jax.sharding import PartitionSpec as P

HD = 64
MAXD = 128
BLK = 64


EPSILON = 1e-06
MASKED = -1e30
PRECISE = lax.Precision.HIGHEST


def norm_forward(values, gain_vec):
    inverse = lax.rsqrt(jnp.mean(values * values, axis=-1, keepdims=True) + EPSILON)
    return (values * inverse * gain_vec, inverse)


def norm_backward(values, inverse, gain_vec, gradient):
    weighted = gradient * gain_vec
    inner_mean = jnp.mean(weighted * values, axis=-1, keepdims=True)
    grad_values = inverse * weighted - values * inverse**3 * inner_mean
    grad_gain = jnp.sum(gradient * values * inverse, axis=0)
    return (grad_values, grad_gain)


def exact_gelu(values):
    return jax.nn.gelu(values, approximate=False)


def dealt_positions(first_row, row_total, devices):
    row_ids = first_row + lax.iota(jnp.int32, row_total)
    owner_dev = row_ids // (2 * BLK)
    within = row_ids % (2 * BLK)
    early_pos = owner_dev * BLK + within
    late_pos = (2 * devices - 1 - owner_dev) * BLK + within - BLK
    return jnp.where(within < BLK, early_pos, late_pos)


def block_size():
    return 512


def split_heads(packed, head_count):
    return packed.reshape(
        packed.shape[0], packed.shape[1], head_count, packed.shape[2] // head_count
    )


def run_bias(pos_query, pos_keys, head_table):
    span = 2 * BLK - 1
    starts_query = pos_query[::BLK]
    starts_keys = pos_keys[::BLK]
    query_runs = starts_query.shape[0]
    key_runs = starts_keys.shape[0]
    head_count = head_table.shape[0]
    offsets = lax.iota(jnp.int32, span) - (BLK - 1)
    distance = starts_query[:, None, None] - starts_keys[None, :, None] + offsets[None, None, :]
    clipped = jnp.clip(distance, 0, MAXD - 1)
    onehot = (clipped.reshape(-1)[:, None] == lax.iota(jnp.int32, MAXD)[None, :]).astype(
        jnp.float32
    )
    diag_values = jnp.dot(onehot, head_table.T, precision=PRECISE)
    diag_values = jnp.transpose(
        diag_values.reshape(query_runs, key_runs, span, head_count), (3, 0, 1, 2)
    )
    tiled = jnp.tile(diag_values, (1, 1, 1, BLK + 1))[..., : BLK * (span + 1)]
    tiled = tiled.reshape(head_count, query_runs, key_runs, BLK, span + 1)[..., :BLK][..., ::-1]
    bias = jnp.transpose(tiled, (1, 3, 0, 2, 4)).reshape(
        query_runs * BLK, head_count, key_runs * BLK
    )
    return (bias[:, None], onehot)


def score_block(query, key_heads, pos_query, pos_keys, head_table):
    raw_score = jnp.einsum(
        "qshd,kshd->qshk", query, key_heads, preferred_element_type=jnp.float32
    ) * HD ** (-0.5)
    distance = pos_query[:, None] - pos_keys[None, :]
    score_bias, onehot = run_bias(pos_query, pos_keys, head_table)
    score = jnp.where((distance >= 0)[:, None, None, :], raw_score + score_bias, MASKED)
    return (score, onehot)


def bias_grad(grad_score, onehot):
    span = 2 * BLK - 1
    summed = jnp.sum(grad_score.astype(jnp.float32), axis=1)
    query_rows, head_count, key_rows = summed.shape
    query_runs = query_rows // BLK
    key_runs = key_rows // BLK
    tiles = jnp.transpose(
        summed.reshape(query_runs, BLK, head_count, key_runs, BLK), (2, 0, 3, 1, 4)
    )[..., ::-1]
    widened = jnp.pad(tiles, ((0, 0), (0, 0), (0, 0), (0, 0), (0, span + 1 - BLK)))
    flat = widened.reshape(head_count, query_runs, key_runs, BLK * (span + 1))
    flat = jnp.pad(flat, ((0, 0), (0, 0), (0, 0), (0, (BLK + 1) * span - BLK * (span + 1))))
    diag_sums = jnp.sum(flat.reshape(head_count, query_runs, key_runs, BLK + 1, span), axis=3)
    diag_rows = jnp.transpose(diag_sums, (1, 2, 3, 0)).reshape(-1, head_count)
    return jnp.dot(onehot.T, diag_rows, precision=PRECISE)


def over_blocks(step_fn, carried, piece):
    piece_rows = piece[0].shape[0]
    step_rows = block_size()
    block_count = piece_rows // step_rows
    blocks = tuple(
        (member.reshape((block_count, step_rows) + member.shape[1:]) for member in piece)
    )
    firsts = step_rows * lax.iota(jnp.int32, block_count)

    def advance(carry_state, scan_item):
        return (step_fn(carry_state, scan_item[0], scan_item[1]), None)

    carried, _ = lax.scan(advance, carried, (blocks, firsts))
    return carried


def local(
    tokens,
    gain_one,
    qkv_weight,
    out_weight,
    rel_weight,
    gain_two,
    router_weight,
    expert_in,
    expert_out,
    routes,
    bucket_table,
    grad_out,
):
    ctx_count = lax.axis_size("ctx")
    row_count, seq_count, model_width = tokens.shape
    token_count = row_count * seq_count
    head_count = qkv_weight.shape[2] // HD
    head_width = head_count * HD
    score_scale = HD ** (-0.5)
    pos_query = dealt_positions(lax.axis_index("ctx") * row_count, row_count, ctx_count)
    token_rows = tokens.astype(jnp.float32).reshape(token_count, model_width)
    normed_one, inverse_one = norm_forward(token_rows, gain_one)
    normed_low = normed_one.astype(jnp.bfloat16)
    projected = jnp.einsum(
        "nd,dce->nce", normed_low, qkv_weight, preferred_element_type=jnp.float32
    ).astype(jnp.bfloat16)
    query_flat = projected[:, 0].reshape(row_count, seq_count, head_width)
    query = split_heads(query_flat, head_count)
    keyval = projected[:, 1:].reshape(row_count, seq_count, 2 * head_width)
    own_keys = split_heads(keyval[..., :head_width], head_count)
    own_values = split_heads(keyval[..., head_width:], head_count)
    bucket_pick = (
        bucket_table[:, None] == lax.iota(jnp.int32, rel_weight.shape[0])[None, :]
    ).astype(jnp.float32)
    head_table = jnp.dot(bucket_pick, rel_weight, precision=PRECISE).T

    def attend(carry_state, key_block, first_row):
        key_heads = split_heads(key_block[0][..., :head_width], head_count)
        value_heads = split_heads(key_block[0][..., head_width:], head_count)
        pos_keys = dealt_positions(first_row, key_heads.shape[0], ctx_count)
        score, _ = score_block(query, key_heads, pos_query, pos_keys, head_table)
        row_max, denominator, weighted = carry_state
        new_max = jnp.maximum(row_max, jnp.max(score, axis=-1))
        rescale = jnp.exp(row_max - new_max)
        weights = jnp.exp(score - new_max[..., None])
        denominator = rescale * denominator + jnp.sum(weights, axis=-1)
        weighted = rescale[..., None] * weighted + jnp.einsum(
            "qshk,kshd->qshd",
            weights.astype(jnp.bfloat16),
            value_heads,
            preferred_element_type=jnp.float32,
        )
        return (new_max, denominator, weighted)

    stat_shape = (row_count, seq_count, head_count)
    zero_heads = jnp.zeros((row_count, seq_count, head_count, HD), jnp.float32)
    initial = (
        jnp.full(stat_shape, MASKED, jnp.float32),
        jnp.zeros(stat_shape, jnp.float32),
        zero_heads,
    )
    row_max, denominator, weighted = over_blocks(
        attend, initial, (lax.all_gather(keyval, "ctx", axis=0, tiled=True),)
    )
    attended = weighted / denominator[..., None]
    log_total = row_max + jnp.log(denominator)
    attended_low = attended.reshape(token_count, head_width).astype(jnp.bfloat16)
    branch = lax.psum(
        jnp.dot(attended_low, out_weight, preferred_element_type=jnp.float32).astype(jnp.bfloat16),
        "wsh",
    ).astype(jnp.float32)
    resid = token_rows + branch
    normed_two, inverse_two = norm_forward(resid, gain_two)
    logits = jnp.dot(normed_two, router_weight, precision=PRECISE)
    shifted = jnp.exp(logits - jnp.max(logits, axis=-1, keepdims=True))
    gate_probs = shifted / jnp.sum(shifted, axis=-1, keepdims=True)
    expert_count = router_weight.shape[1]
    expert_ids = routes.reshape(token_count)
    choose = expert_ids[:, None] == lax.iota(jnp.int32, expert_count)[None, :]
    gate_value = jnp.sum(jnp.where(choose, gate_probs, 0.0), axis=1)
    lower_ones = (
        lax.iota(jnp.int32, token_count)[:, None] >= lax.iota(jnp.int32, token_count)[None, :]
    ).astype(jnp.bfloat16)
    filled = jnp.dot(
        lower_ones, choose.astype(jnp.bfloat16), preferred_element_type=jnp.float32
    ).astype(jnp.int32)
    slot_index = jnp.sum(jnp.where(choose, filled - 1, 0), axis=1)
    capacity = max(2, 2 * token_count // expert_count)
    target = expert_ids * capacity + slot_index
    slot_pick = target[:, None] == lax.iota(jnp.int32, expert_count * capacity)[None, :]
    slot_low = slot_pick.astype(jnp.bfloat16)
    slot_full = slot_pick.astype(jnp.float32)
    weight_in = expert_in[0]
    weight_out = expert_out[0]

    def spread(values):
        buffer = jnp.einsum(
            "nm,nd->md", slot_low, values, preferred_element_type=jnp.float32
        ).astype(jnp.bfloat16)
        doubled = jnp.broadcast_to(
            buffer.reshape(expert_count, 1, capacity, model_width),
            (expert_count, 2, capacity, model_width),
        )
        return doubled.reshape(2 * expert_count, capacity, model_width)

    def collect(returned):
        row_width = returned.shape[-1]
        paired = jnp.sum(returned.reshape(expert_count, 2, capacity, row_width), axis=1)
        return jnp.dot(
            slot_full, paired.reshape(expert_count * capacity, row_width), precision=PRECISE
        )

    arrived_rows = lax.all_to_all(
        spread(normed_two.astype(jnp.bfloat16)), "ctx", split_axis=0, concat_axis=0, tiled=True
    )
    flat_rows = arrived_rows.reshape(-1, model_width)
    pre_act = jnp.dot(flat_rows, weight_in, preferred_element_type=jnp.float32)
    hidden = exact_gelu(pre_act).astype(jnp.bfloat16)
    returned = lax.all_to_all(
        jnp.dot(hidden, weight_out, preferred_element_type=jnp.float32)
        .reshape(arrived_rows.shape)
        .astype(jnp.bfloat16),
        "ctx",
        split_axis=0,
        concat_axis=0,
        tiled=True,
    ).astype(jnp.float32)
    expert_rows = lax.psum(collect(returned).astype(jnp.bfloat16), "wsh").astype(jnp.float32)
    result = resid + gate_value[:, None] * expert_rows
    out = result.astype(jnp.bfloat16).reshape(row_count, seq_count, model_width)
    grad_rows_f = grad_out.astype(jnp.float32).reshape(token_count, model_width)
    grad_gate = jnp.sum(grad_rows_f * expert_rows, axis=1)
    grad_expert_rows = (gate_value[:, None] * grad_rows_f).astype(jnp.bfloat16)
    arrived_grad = lax.all_to_all(
        spread(grad_expert_rows), "ctx", split_axis=0, concat_axis=0, tiled=True
    )
    flat_rows = arrived_rows.reshape(-1, model_width)
    flat_grad = arrived_grad.reshape(-1, model_width)
    pre_act = jnp.dot(flat_rows, weight_in, preferred_element_type=jnp.float32)
    hidden, gelu_pull = jax.vjp(exact_gelu, pre_act)
    hidden_low = hidden.astype(jnp.bfloat16)
    grad_weight_out = jnp.einsum(
        "rf,rd->fd", hidden_low, flat_grad, preferred_element_type=jnp.float32
    )
    grad_hidden = jnp.einsum("rd,fd->rf", flat_grad, weight_out, preferred_element_type=jnp.float32)
    grad_pre = gelu_pull(grad_hidden)[0].astype(jnp.bfloat16)
    grad_weight_in = jnp.einsum(
        "rd,rf->df", flat_rows, grad_pre, preferred_element_type=jnp.float32
    )
    partial_back = jnp.einsum(
        "rf,df->rd", grad_pre, weight_in, preferred_element_type=jnp.float32
    ).reshape(arrived_rows.shape)
    returned_grad = lax.all_to_all(
        partial_back.astype(jnp.bfloat16), "ctx", split_axis=0, concat_axis=0, tiled=True
    ).astype(partial_back.dtype)
    grad_sent = lax.psum(collect(returned_grad).astype(jnp.bfloat16), "wsh").astype(jnp.float32)
    grad_sent = lax.optimization_barrier(grad_sent.astype(jnp.bfloat16)).astype(jnp.float32)
    grad_logits = gate_probs * (
        jnp.where(choose, grad_gate[:, None], 0.0) - (gate_value * grad_gate)[:, None]
    )
    grad_router = jnp.dot(normed_two.T, grad_logits, precision=PRECISE)
    grad_normed_two = grad_sent + jnp.dot(grad_logits, router_weight.T, precision=PRECISE)
    grad_resid, grad_gain_two = norm_backward(resid, inverse_two, gain_two, grad_normed_two)
    grad_resid = grad_resid + grad_rows_f
    grad_branch = grad_resid.astype(jnp.bfloat16)
    grad_out_rows = jnp.einsum(
        "nw,nd->wd", attended_low, grad_branch, preferred_element_type=jnp.float32
    )
    grad_att = jnp.einsum(
        "nd,wd->nw", grad_branch, out_weight, preferred_element_type=jnp.float32
    ).astype(jnp.bfloat16)
    grad_att_flat = grad_att.reshape(row_count, seq_count, head_width)
    grad_att_heads = split_heads(grad_att_flat, head_count)
    row_inner = jnp.sum(grad_att_heads.astype(jnp.float32) * attended, axis=-1)

    def query_grads(carry_state, key_block, first_row):
        key_heads = split_heads(key_block[0][..., :head_width], head_count)
        value_heads = split_heads(key_block[0][..., head_width:], head_count)
        pos_keys = dealt_positions(first_row, key_heads.shape[0], ctx_count)
        score, onehot = score_block(query, key_heads, pos_query, pos_keys, head_table)
        weights = jnp.exp(score - log_total[..., None])
        grad_weights = jnp.einsum(
            "qshd,kshd->qshk", grad_att_heads, value_heads, preferred_element_type=jnp.float32
        )
        grad_score = (weights * (grad_weights - row_inner[..., None])).astype(jnp.bfloat16)
        grad_query = (
            carry_state[0]
            + jnp.einsum(
                "qshk,kshd->qshd", grad_score, key_heads, preferred_element_type=jnp.float32
            )
            * score_scale
        )
        return (grad_query, carry_state[1] + bias_grad(grad_score, onehot))

    def key_grads(carry_state, query_block, first_row):
        query_heads = split_heads(query_block[0][..., :head_width], head_count)
        grad_heads = split_heads(query_block[0][..., head_width:], head_count)
        pos_rows = dealt_positions(first_row, query_heads.shape[0], ctx_count)
        score, _ = score_block(query_heads, own_keys, pos_rows, pos_query, head_table)
        weights = jnp.exp(score - query_block[1][..., None])
        grad_value = carry_state[1] + jnp.einsum(
            "qshk,qshd->kshd",
            weights.astype(jnp.bfloat16),
            grad_heads,
            preferred_element_type=jnp.float32,
        )
        grad_weights = jnp.einsum(
            "qshd,kshd->qshk", grad_heads, own_values, preferred_element_type=jnp.float32
        )
        grad_score = (weights * (grad_weights - query_block[2][..., None])).astype(jnp.bfloat16)
        grad_key = (
            carry_state[0]
            + jnp.einsum(
                "qshk,qshd->kshd", grad_score, query_heads, preferred_element_type=jnp.float32
            )
            * score_scale
        )
        return (grad_key, grad_value)

    packed = jnp.concatenate([query_flat, grad_att_flat], axis=-1)
    zero_table = jnp.zeros((MAXD, head_count), jnp.float32)
    grad_query, grad_table = over_blocks(
        query_grads, (zero_heads, zero_table), (lax.all_gather(keyval, "ctx", axis=0, tiled=True),)
    )
    grad_key, grad_value = over_blocks(
        key_grads,
        (zero_heads, zero_heads),
        (
            lax.all_gather(packed, "ctx", axis=0, tiled=True),
            lax.all_gather(log_total.astype(jnp.bfloat16), "ctx", axis=0, tiled=True).astype(
                jnp.float32
            ),
            lax.all_gather(row_inner.astype(jnp.bfloat16), "ctx", axis=0, tiled=True).astype(
                jnp.float32
            ),
        ),
    )
    grad_projected = jnp.stack(
        [member.reshape(token_count, head_width) for member in (grad_query, grad_key, grad_value)],
        axis=1,
    ).astype(jnp.bfloat16)
    grad_normed_one = lax.psum(
        jnp.einsum(
            "nce,dce->nd", grad_projected, qkv_weight, preferred_element_type=jnp.float32
        ).astype(jnp.bfloat16),
        "wsh",
    ).astype(jnp.float32)
    grad_qkv = jnp.einsum(
        "nd,nce->dce", normed_low, grad_projected, preferred_element_type=jnp.float32
    )
    grad_tokens, grad_gain_one = norm_backward(token_rows, inverse_one, gain_one, grad_normed_one)
    grad_tokens = grad_tokens + grad_resid
    grad_rel = jnp.dot(bucket_pick.T, grad_table, precision=PRECISE)
    summed_grads = lax.psum(
        (grad_qkv, grad_out_rows, grad_rel, grad_gain_one, grad_gain_two, grad_router), "ctx"
    )
    return (
        out,
        grad_tokens.reshape(row_count, seq_count, model_width),
        summed_grads[3],
        summed_grads[0],
        summed_grads[1],
        summed_grads[2],
        summed_grads[4],
        summed_grads[5],
        grad_weight_in[None],
        grad_weight_out[None],
    )


NT = (((1,), (1,)), ((), ()))
TN = (((0,), (0,)), ((), ()))
SCOPED = 16 * 1024 * 1024
LIGHT = pl.CostEstimate(flops=1_000_000, bytes_accessed=10_000, transcendentals=0)


def strip(step, side):
    width = 128 * (step + 1) if side == 0 else 128 * (8 - step)
    first = 0 if side == 0 else 128 * (step + 1)
    return (width, first)


def skewed(values, leftward):
    width = values.shape[1]
    row = lax.broadcasted_iota(jnp.int32, values.shape, 0)
    for bit in range(6):
        shift = width - (1 << bit) if leftward else 1 << bit
        moved = pltpu.roll(values, shift, 1)
        values = jnp.where((row & (1 << bit)) != 0, moved, values)
    return values


def attend_kernel(ids_ref, *refs):
    own_refs, other_refs, line_ref = refs[1:5], refs[5:9], refs[9]
    att_refs = refs[10:14]
    far_prob_ref, far_keyval_ref, far_query_ref = refs[14:17]
    bias_ref, own_ref, other_ref, all_ref, near_ref = refs[17:22]
    prob_ref, keyval_ref, query_ref, sems, out_sems = refs[22:]

    def prob_copy(step):
        return pltpu.make_async_copy(
            prob_ref.at[:, step], far_prob_ref.at[:, step], out_sems.at[step]
        )

    def other_copies():
        return (
            pltpu.make_async_copy(keyval_ref, far_keyval_ref, out_sems.at[4]),
            pltpu.make_async_copy(query_ref, far_query_ref, out_sems.at[5]),
        )

    chip = ids_ref[0]
    core = ids_ref[1]

    def gather_keys(parity):
        for place in range(16):
            owner = place if place < 8 else 15 - place
            half = 0 if place < 8 else BLK
            source = own_ref if owner % 2 == parity else other_ref
            keyval_ref[place * BLK : (place + 1) * BLK, :] = source[
                owner // 2, half : half + BLK, :
            ]

    @pl.when(pl.program_id(0) == 0)
    def _():
        fetch(list(own_refs) + list(other_refs), [near_ref.at[at] for at in range(8)], sems)
        for away in range(4):
            own_ref[chip ^ away] = near_ref[away, :, :384]
            other_ref[chip ^ away] = near_ref[4 + away, :, :384]
            query_ref[chip ^ away] = near_ref[away, :, 384:] * jnp.bfloat16(HD ** (-0.5))
        for head in range(3):
            for side in range(2):
                line = jnp.broadcast_to(line_ref[head, side : side + 1, :], (BLK, 512))
                bias_ref[head, side] = skewed(line, False)[:, 128:384]

        @pl.when(core == 0)
        def _():
            gather_keys(0)

        @pl.when(core == 1)
        def _():
            gather_keys(1)

        for copy in other_copies():
            copy.start()

    def attend_step(step):
        jobs = [(head, side) for side in range(2) for head in range(3)]
        scores = []
        for head, side in jobs:
            width, _ = strip(step, side)
            rows = slice(side * BLK, (side + 1) * BLK)
            query = query_ref[step, rows, HD * head : HD * (head + 1)]
            keys = keyval_ref[:width, HD * head : HD * (head + 1)]
            score = lax.dot_general(query, keys, NT, preferred_element_type=jnp.float32)
            near = min(width, 256)
            close = score[:, width - near :] + bias_ref[head, side, :, 256 - near :]
            if width > near:
                score = jnp.concatenate([score[:, : width - near], close], axis=1)
            else:
                score = close
            scores.append(score)
        tops = [jnp.max(score, axis=-1, keepdims=True) for score in scores]
        weights = [jnp.exp(score - top) for score, top in zip(scores, tops)]
        totals = [jnp.sum(weight, axis=-1, keepdims=True) for weight in weights]
        probs = [
            (weight * (1.0 / total)).astype(jnp.bfloat16)
            for weight, total in zip(weights, totals)
        ]
        for (head, side), prob in zip(jobs, probs):
            width, first = strip(step, side)
            prob_ref[head, step, :, first : first + width] = prob
        prob_copy(step).start()
        mixed = [
            jnp.dot(
                prob,
                keyval_ref[: prob.shape[1], 192 + HD * head : 192 + HD * (head + 1)],
                preferred_element_type=jnp.float32,
            ).astype(jnp.bfloat16)
            for (head, side), prob in zip(jobs, probs)
        ]
        for side in range(2):
            rows = slice(side * BLK, (side + 1) * BLK)
            all_ref[step, rows, :] = jnp.concatenate(
                mixed[3 * side : 3 * side + 3], axis=1
            )

    for step in range(4):
        pl.when(pl.program_id(0) == step)(functools.partial(attend_step, step))

    @pl.when(pl.program_id(0) == 3)
    def _():
        for away in range(4):
            att_refs[away][...] = all_ref[chip ^ away]
        for step in range(4):
            prob_copy(step).wait()
        for copy in other_copies():
            copy.wait()


def attend_back_kernel(ids_ref, *refs):
    far_query_ref, prob_ref, far_keyval_ref = refs[:3]
    grad_refs = refs[3:7]
    mine_ref, theirs_ref, lags_ref, tiny_ref, total_ref, near_ref, grad_ref = refs[7:14]
    query_ref, keyval_ref, sems = refs[14:]
    core = ids_ref[1]
    plane = ids_ref[2]

    @pl.when(pl.program_id(0) == 0)
    def _():
        total_ref[...] = jnp.zeros_like(total_ref)
        near_ref[...] = jnp.zeros_like(near_ref)
        fetch(
            list(grad_refs) + [far_query_ref, far_keyval_ref],
            [grad_ref.at[plane ^ away] for away in range(4)] + [query_ref, keyval_ref],
            sems,
        )

    def back_step(step):
        jobs = [(head, side) for side in range(2) for head in range(3)]
        queries, grads, probs, products = [], [], [], []
        for head, side in jobs:
            width, first = strip(step, side)
            rows = slice(side * BLK, (side + 1) * BLK)
            queries.append(query_ref[step, rows, HD * head : HD * (head + 1)])
            grad = grad_ref[step, rows, HD * head : HD * (head + 1)]
            grads.append(grad)
            values = keyval_ref[:width, 192 + HD * head : 192 + HD * (head + 1)]
            prob = prob_ref[head, 0, :, first : first + width]
            probs.append(prob)
            grad_prob = lax.dot_general(grad, values, NT, preferred_element_type=jnp.float32)
            products.append(prob.astype(jnp.float32) * grad_prob)
        inners = [jnp.sum(product, axis=-1, keepdims=True) for product in products]
        lows = [
            (product - prob.astype(jnp.float32) * inner).astype(jnp.bfloat16)
            for product, prob, inner in zip(products, probs, inners)
        ]
        dqs = [
            (
                jnp.dot(
                    low,
                    keyval_ref[: low.shape[1], HD * head : HD * (head + 1)],
                    preferred_element_type=jnp.float32,
                )
                * HD ** (-0.5)
            ).astype(jnp.bfloat16)
            for (head, side), low in zip(jobs, lows)
        ]
        for side in range(2):
            rows = slice(side * BLK, (side + 1) * BLK)
            width, _ = strip(step, side)
            mine_ref[step, rows, 384:] = jnp.concatenate(dqs[3 * side : 3 * side + 3], axis=1)
            parts = []
            for left, right in ((lows, queries), (probs, grads)):
                for head in range(3):
                    parts.append(
                        lax.dot_general(
                            left[3 * side + head],
                            right[3 * side + head],
                            TN,
                            preferred_element_type=jnp.float32,
                        )
                    )
            total_ref[:width, :] += jnp.concatenate(parts, axis=1)
        for (head, side), low in zip(jobs, lows):
            width, _ = strip(step, side)
            score = low.astype(jnp.float32)
            near_ref[head, 2 * side] += score[:, width - 128 :]
            if width >= 256:
                near_ref[head, 2 * side + 1] += score[:, width - 256 : width - 128]
            if width > 256:
                far = score[:, :128]
                for chunk in range(1, (width - 256) // 128):
                    far = far + score[:, 128 * chunk : 128 * (chunk + 1)]
                near_ref[head, 4] += far

    for step in range(4):
        pl.when(pl.program_id(0) == step)(functools.partial(back_step, step))

    def scatter_keys(parity):
        for place in range(16):
            owner = place if place < 8 else 15 - place
            half = 0 if place < 8 else BLK
            target = mine_ref if owner % 2 == parity else theirs_ref
            target[owner // 2, half : half + BLK, :384] = total_ref[
                place * BLK : (place + 1) * BLK, :
            ].astype(jnp.bfloat16)

    @pl.when(pl.program_id(0) == 3)
    def _():
        tiny_ref[...] = total_ref[:16, :128].astype(jnp.bfloat16)
        lags_ref[...] = jnp.zeros_like(lags_ref)
        for head in range(3):
            for kind in range(4):
                wide = jnp.concatenate(
                    [near_ref[head, kind], jnp.zeros((BLK, 128), jnp.float32)], axis=1
                )
                lags_ref[head, kind : kind + 1, :] = jnp.sum(
                    skewed(wide, True), axis=0, keepdims=True
                )
            lags_ref[head, 4:5, :128] = jnp.sum(near_ref[head, 4], axis=0, keepdims=True)

        @pl.when(core == 0)
        def _():
            scatter_keys(0)

        @pl.when(core == 1)
        def _():
            scatter_keys(1)


def whole(*shape):
    return pl.BlockSpec(shape, lambda at: (0,) * len(shape))


def in_hbm():
    return pl.BlockSpec(memory_space=pltpu.HBM)


def by_step():
    return pl.BlockSpec((3, 1, BLK, 1152), lambda at: (0, at, 0, 0))


def in_vmem(count):
    return [pl.BlockSpec(memory_space=pltpu.VMEM)] * count


def attend_call(ids, tiny, own, other, line):
    return pl.pallas_call(
        attend_kernel,
        grid=(4,),
        out_shape=(jax.ShapeDtypeStruct((128, 192), jnp.bfloat16),) * 4
        + (
            jax.ShapeDtypeStruct((3, 4, BLK, 1152), jnp.bfloat16),
            jax.ShapeDtypeStruct((1024, 384), jnp.bfloat16),
            jax.ShapeDtypeStruct((4, 128, 192), jnp.bfloat16),
        ),
        in_specs=[in_smem(), whole(16, 128)] + [in_hbm()] * 8 + [whole(3, 2, 512)],
        out_specs=(whole(128, 192),) * 4 + (in_hbm(),) * 3,
        scratch_shapes=[
            pltpu.VMEM((3, 2, BLK, 256), jnp.float32),
            pltpu.VMEM((4, 128, 384), jnp.bfloat16),
            pltpu.VMEM((4, 128, 384), jnp.bfloat16),
            pltpu.VMEM((4, 128, 192), jnp.bfloat16),
            pltpu.VMEM((8, 128, 576), jnp.bfloat16),
            pltpu.VMEM((3, 4, BLK, 1152), jnp.bfloat16),
            pltpu.VMEM((1024, 384), jnp.bfloat16),
            pltpu.VMEM((4, 128, 192), jnp.bfloat16),
            pltpu.SemaphoreType.DMA((8,)),
            pltpu.SemaphoreType.DMA((6,)),
        ],
        compiler_params=pltpu.CompilerParams(
            vmem_limit_bytes=SCOPED, dimension_semantics=("arbitrary",)
        ),
        cost_estimate=LIGHT,
        name="attend",
    )(ids, tiny, *own, *other, line)


def attend_back_call(ids, query, prob, keyval, grads):
    return pl.pallas_call(
        attend_back_kernel,
        grid=(4,),
        out_shape=(
            jax.ShapeDtypeStruct((4, 128, 576), jnp.bfloat16),
            jax.ShapeDtypeStruct((4, 128, 384), jnp.bfloat16),
            jax.ShapeDtypeStruct((3, 8, 256), jnp.float32),
            jax.ShapeDtypeStruct((16, 128), jnp.bfloat16),
        ),
        in_specs=[
            in_smem(),
            in_hbm(),
            by_step(),
            in_hbm(),
        ]
        + [in_hbm()] * 4,
        out_specs=(
            whole(4, 128, 576),
            whole(4, 128, 384),
            whole(3, 8, 256),
            whole(16, 128),
        ),
        scratch_shapes=[
            pltpu.VMEM((1024, 384), jnp.float32),
            pltpu.VMEM((3, 5, BLK, 128), jnp.float32),
            pltpu.VMEM((4, 128, 192), jnp.bfloat16),
            pltpu.VMEM((4, 128, 192), jnp.bfloat16),
            pltpu.VMEM((1024, 384), jnp.bfloat16),
            pltpu.SemaphoreType.DMA((6,)),
        ],
        compiler_params=pltpu.CompilerParams(
            vmem_limit_bytes=SCOPED, dimension_semantics=("arbitrary",)
        ),
        cost_estimate=LIGHT,
        name="attend_back",
    )(ids, query, prob, keyval, *grads)


def to_core(values):
    return lax.ppermute(values, "ctx", [(at, at ^ 1) for at in range(8)])


def to_chip(values, away):
    return lax.ppermute(values, "ctx", [(at, at ^ (2 * away)) for at in range(8)])


def to_plane(values, away):
    return lax.ppermute(values, "wsh", [(at, at ^ away) for at in range(4)])


def tiny_of(source):
    return to_core(source.reshape(-1, source.shape[-1])[:16, :128])


def chip_swap(blocks):
    return [blocks[0]] + [to_chip(blocks[away], away) for away in range(1, 4)]


def plane_shift(blocks):
    return [blocks[0]] + [
        lax.ppermute(blocks[step], "wsh", [(at, (at + step) % 4) for at in range(4)])
        for step in range(1, 4)
    ]


def plane_swap(blocks):
    return [blocks[0]] + [to_plane(blocks[away], away) for away in range(1, 4)]


def seat(chip, core, plane):
    return (2 * chip + core) * 4 + plane


def turn_swap(blocks):
    return [
        lax.ppermute(
            block,
            ("ctx", "wsh"),
            [
                (seat(chip, core, plane), seat(plane, core, chip ^ away))
                for chip in range(4)
                for core in range(2)
                for plane in range(4)
            ],
        )
        for away, block in enumerate(blocks)
    ]


def pick(blocks, at):
    return lax.dynamic_index_in_dim(blocks, at, 0, keepdims=False)


def bias_lines(head_table, core):
    shifted = head_table - head_table[:, MAXD - 1 :]
    turned = shifted[:, ::-1]

    def line(zeros):
        return jnp.pad(
            jnp.pad(turned, ((0, 0), (zeros, 0))),
            ((0, 0), (0, 512 - MAXD - zeros)),
            constant_values=MASKED,
        )

    even, odd = line(129), line(193)
    return jnp.where(
        core == 0, jnp.stack([even, odd], axis=1), jnp.stack([odd, even], axis=1)
    )


def table_grad(lags, core):
    offsets = lax.iota(jnp.int32, 256)
    offsets = jnp.where(offsets < 128, offsets, offsets - 256)
    base = BLK * jnp.stack([core, core + 2, 1 - core, 3 - core])
    clipped = jnp.clip(base[:, None] - offsets[None, :], 0, MAXD - 1)
    onehot = (clipped[..., None] == lax.iota(jnp.int32, MAXD)).astype(jnp.float32)
    table = jnp.einsum("hkz,kzd->dh", lags[:, :4], onehot, precision=PRECISE)
    last = (lax.iota(jnp.int32, MAXD) == MAXD - 1).astype(jnp.float32)
    return table + last[:, None] * jnp.sum(lags[:, 4], axis=-1)


def gelu_parts(values):
    cdf = 0.5 * (1.0 + lax.erf(values * (0.5**0.5)))
    density = jnp.exp(-0.5 * values * values) * ((0.5 / jnp.pi) ** 0.5)
    return (values * cdf, cdf + values * density)


def in_smem():
    return pl.BlockSpec(memory_space=pltpu.SMEM)


def split_column(column):
    high = column.astype(jnp.bfloat16)
    low = (column - high.astype(jnp.float32)).astype(jnp.bfloat16)
    lane = lax.broadcasted_iota(jnp.int32, (column.shape[0], 128), 1)
    wide = jnp.where(
        lane == 0,
        high.astype(jnp.float32),
        jnp.where(lane == 1, low.astype(jnp.float32), 0.0),
    )
    return wide.astype(jnp.bfloat16)


def project_kernel(ids_ref, hint_ref, token_ref, gain_ref, weight_ref, normed_ref, *refs):
    chip = ids_ref[0]
    tokens = token_ref[...].reshape(512, 768).astype(jnp.float32)
    inverse = lax.rsqrt(jnp.mean(tokens * tokens, axis=-1, keepdims=True) + EPSILON)
    normed = (tokens * inverse * gain_ref[...]).astype(jnp.bfloat16)
    normed_ref[...] = normed
    projected = jnp.dot(normed, weight_ref[...], preferred_element_type=jnp.float32)
    refs[4][...] = projected.astype(jnp.bfloat16).reshape(4, 128, 576)
    for away in range(4):
        refs[away][...] = refs[4][chip ^ away]


def project_call(ids, tiny, tokens, gain, weight):
    return pl.pallas_call(
        project_kernel,
        out_shape=(jax.ShapeDtypeStruct((512, 768), jnp.bfloat16),)
        + (jax.ShapeDtypeStruct((128, 576), jnp.bfloat16),) * 4,
        in_specs=[in_smem()] + in_vmem(4),
        out_specs=tuple(in_vmem(5)),
        scratch_shapes=[pltpu.VMEM((4, 128, 576), jnp.bfloat16)],
        compiler_params=pltpu.CompilerParams(vmem_limit_bytes=SCOPED),
        cost_estimate=LIGHT,
        name="project",
    )(ids, tiny, tokens, gain, weight)


def gather_rows_kernel(ids_ref, *refs):
    chip = ids_ref[0]
    for away in range(4):
        refs[4][pl.ds(pl.multiple_of(128 * (chip ^ away), 128), 128), :] = refs[away][...]


def gather_rows_call(ids, blocks):
    return pl.pallas_call(
        gather_rows_kernel,
        out_shape=jax.ShapeDtypeStruct((512, 192), jnp.bfloat16),
        in_specs=[in_smem()] + in_vmem(4),
        out_specs=in_vmem(1)[0],
        compiler_params=pltpu.CompilerParams(vmem_limit_bytes=SCOPED),
        cost_estimate=LIGHT,
        name="gather_rows",
    )(ids, *blocks)


def add_queries_kernel(ids_ref, mine_ref, theirs_ref, *sum_refs):
    chip = ids_ref[0]
    for away, sum_ref in enumerate(sum_refs):
        mine = mine_ref[chip ^ away]
        total = mine[:, :384].astype(jnp.float32) + theirs_ref[chip ^ away].astype(jnp.float32)
        sum_ref[:, :384] = total.astype(jnp.bfloat16)
        sum_ref[:, 384:] = mine[:, 384:]


def add_queries_call(ids, mine, theirs):
    return pl.pallas_call(
        add_queries_kernel,
        out_shape=(jax.ShapeDtypeStruct((128, 576), jnp.bfloat16),) * 4,
        in_specs=[in_smem()] + in_vmem(2),
        out_specs=tuple(in_vmem(4)),
        compiler_params=pltpu.CompilerParams(vmem_limit_bytes=SCOPED),
        cost_estimate=LIGHT,
        name="add_queries",
    )(ids, mine, theirs)


def fetch(sources, targets, sems):
    copies = [
        pltpu.make_async_copy(source, target, sems.at[at])
        for at, (source, target) in enumerate(zip(sources, targets))
    ]
    for copy in copies:
        copy.start()
    for copy in copies:
        copy.wait()


def join_kernel(tiny_ref, ids_ref, *refs):
    core = ids_ref[1]
    turn_ref, narrow_ref, joined_ref, rows_ref, wide_ref = refs[7:]
    for seq in range(4):
        rows_ref[seq] = turn_ref[:, seq, :]
    wide_ref[...] = jnp.concatenate(
        [narrow_ref[...], jnp.zeros((768, 124), jnp.float32)], axis=1
    )
    joined_ref[0] = refs[0][...]
    own_rows = pl.ds(pl.multiple_of(96 * core, 32), 96)
    other_rows = pl.ds(pl.multiple_of(96 - 96 * core, 32), 96)
    for away in range(1, 4):
        joined_ref[away, own_rows, :] = refs[away][...]
        joined_ref[away, other_rows, :] = refs[3 + away][...]


def join_call(tiny, ids, parts, grad, router):
    return pl.pallas_call(
        join_kernel,
        out_shape=(
            jax.ShapeDtypeStruct((4, 192, 768), jnp.bfloat16),
            jax.ShapeDtypeStruct((4, 128, 768), jnp.bfloat16),
            jax.ShapeDtypeStruct((768, 128), jnp.float32),
        ),
        in_specs=in_vmem(1) + [in_smem()] + in_vmem(9),
        out_specs=tuple(in_vmem(3)),
        compiler_params=pltpu.CompilerParams(vmem_limit_bytes=SCOPED),
        cost_estimate=LIGHT,
        name="join",
    )(tiny, ids, *parts, grad, router)


def place_slots(route, turned_ref, grad_ref, low_ref, rows_ref, slots_ref):
    lane = lax.broadcasted_iota(jnp.int32, (512, 128), 1)
    choose = lane == route
    later = lax.broadcasted_iota(jnp.int32, (512, 512), 0)
    earlier = lax.broadcasted_iota(jnp.int32, (512, 512), 1)
    filled = jnp.dot(
        (later >= earlier).astype(jnp.float32).astype(jnp.bfloat16),
        choose.astype(jnp.float32).astype(jnp.bfloat16),
        preferred_element_type=jnp.float32,
    )
    index = jnp.sum(jnp.where(choose, filled, 0.0), axis=-1, keepdims=True).astype(jnp.int32) - 1
    target = route * 256 + index
    low_ref[...] = (
        (lax.broadcasted_iota(jnp.int32, (512, 1024), 1) == target)
        .astype(jnp.float32)
        .astype(jnp.bfloat16)
        .reshape(4, 128, 1024)
    )
    turned = turned_ref[...]
    choose = lax.broadcasted_iota(jnp.int32, (8, 512), 0) == turned
    filled = jnp.dot(
        choose.astype(jnp.float32).astype(jnp.bfloat16),
        (later <= earlier).astype(jnp.float32).astype(jnp.bfloat16),
        preferred_element_type=jnp.float32,
    )
    index = jnp.sum(jnp.where(choose, filled, 0.0), axis=0, keepdims=True).astype(jnp.int32) - 1
    target = turned * 256 + index
    rows_ref[...] = (
        (lax.broadcasted_iota(jnp.int32, (1024, 512), 0) == target)
        .astype(jnp.float32)
        .astype(jnp.bfloat16)
    )
    slots_ref[...] = (
        jnp.dot(rows_ref[...], grad_ref[...], preferred_element_type=jnp.float32)
        .astype(jnp.bfloat16)
        .reshape(4, 256, 768)
    )


def route_kernel(*refs):
    ids_ref, att_refs, out_weight_ref = refs[0], refs[1:5], refs[5]
    token_ref, gain_ref, router_ref, route_ref, row_ref, grad_ref = refs[6:12]
    resid_ref, probs_ref, sent_ref, gate_ref, low_ref, slots_ref = refs[12:18]
    payload_ref, branch_ref, all_probs_ref, slot_ref = refs[18:]
    chip = ids_ref[0]
    plane = ids_ref[2]
    route = route_ref[...].reshape(512, 1)
    place_slots(route ^ chip, row_ref, grad_ref, low_ref, slot_ref, slots_ref)
    branch = token_ref[...].reshape(512, 768).astype(jnp.float32)
    for away, att_ref in enumerate(att_refs):
        branch = branch + jnp.dot(
            att_ref[...], out_weight_ref[away], preferred_element_type=jnp.float32
        )
    branch_ref[...] = branch.reshape(4, 128, 768)
    inverse = lax.rsqrt(jnp.mean(branch * branch, axis=-1, keepdims=True) + EPSILON)
    normed = branch * inverse * gain_ref[...]
    payload_ref[:, :768] = normed.astype(jnp.bfloat16)
    logits = jnp.dot(normed, router_ref[...], precision=PRECISE, preferred_element_type=jnp.float32)
    lane = lax.broadcasted_iota(jnp.int32, (512, 128), 1)
    logits = jnp.where(lane < 4, logits, MASKED)
    shifted = jnp.exp(logits - jnp.max(logits, axis=-1, keepdims=True))
    probs = shifted / jnp.sum(shifted, axis=-1, keepdims=True)
    all_probs_ref[...] = probs.reshape(4, 128, 128)
    gate = jnp.sum(jnp.where(lane == route, probs, 0.0), axis=-1, keepdims=True)
    payload_ref[:, 768:] = split_column(gate)
    resid_ref[...] = branch_ref[plane]
    probs_ref[...] = all_probs_ref[plane]
    placed = jnp.dot(slot_ref[...], payload_ref[...], preferred_element_type=jnp.float32)
    sent_ref[...] = placed[:, :768].astype(jnp.bfloat16).reshape(4, 256, 768)
    gate_ref[...] = jnp.broadcast_to(
        placed[:, 768:769] + placed[:, 769:770], (1024, 128)
    ).reshape(4, 256, 128)


def route_call(ids, att, out_weights, tokens, gain, router, route, relative, grad):
    return pl.pallas_call(
        route_kernel,
        out_shape=(
            jax.ShapeDtypeStruct((128, 768), jnp.float32),
            jax.ShapeDtypeStruct((128, 128), jnp.float32),
            jax.ShapeDtypeStruct((4, 256, 768), jnp.bfloat16),
            jax.ShapeDtypeStruct((4, 256, 128), jnp.float32),
            jax.ShapeDtypeStruct((4, 128, 1024), jnp.bfloat16),
            jax.ShapeDtypeStruct((4, 256, 768), jnp.bfloat16),
        ),
        in_specs=[in_smem()] + in_vmem(11),
        out_specs=tuple(in_vmem(6)),
        scratch_shapes=[
            pltpu.VMEM((512, 896), jnp.bfloat16),
            pltpu.VMEM((4, 128, 768), jnp.float32),
            pltpu.VMEM((4, 128, 128), jnp.float32),
            pltpu.VMEM((1024, 512), jnp.bfloat16),
        ],
        compiler_params=pltpu.CompilerParams(vmem_limit_bytes=SCOPED),
        cost_estimate=LIGHT,
        name="route",
    )(ids, *att, out_weights, tokens, gain, router, route, relative[None, :], grad)


def expert_kernel(*refs):
    ids_ref, sent_ref, grad_ref = refs[:3]
    in_refs, out_refs = refs[3:11], refs[11:19]
    pick_ref, home_refs = refs[19], refs[20:24]
    hidden_ref, grad_pre_ref, total_ref = refs[24:]
    plane = ids_ref[2]
    for expert in range(4):
        back = None
        inner = None
        for half in range(2):
            in_ref, out_ref = in_refs[2 * expert + half], out_refs[2 * expert + half]
            pre_act = jnp.dot(sent_ref[expert], in_ref[...], preferred_element_type=jnp.float32)
            grad_hidden = lax.dot_general(
                grad_ref[expert], out_ref[...], NT, preferred_element_type=jnp.float32
            )
            hidden, slope = gelu_parts(pre_act)
            hidden_ref[half, expert] = hidden.astype(jnp.bfloat16)
            grad_pre = (grad_hidden * slope).astype(jnp.bfloat16)
            grad_pre_ref[half, expert] = grad_pre
            part_inner = jnp.sum(hidden * grad_hidden, axis=-1, keepdims=True)
            part_back = lax.dot_general(
                grad_pre, in_ref[...], NT, preferred_element_type=jnp.float32
            )
            back = part_back if half == 0 else back + part_back
            inner = part_inner if half == 0 else inner + part_inner
        payload = jnp.concatenate([back.astype(jnp.bfloat16), split_column(inner)], axis=1)
        columns = slice(256 * expert, 256 * (expert + 1))
        picked = pick_ref[:, :, columns].reshape(512, 256)
        part = jnp.dot(picked, payload, preferred_element_type=jnp.float32)
        if expert == 0:
            total_ref[...] = part.reshape(4, 128, 896)
        else:
            total_ref[...] += part.reshape(4, 128, 896)
    for away in range(4):
        home_refs[away][...] = total_ref[plane ^ away].astype(jnp.bfloat16)


def expert_call(ids, sent, grad, weights_in, weights_out, slot_pick):
    return pl.pallas_call(
        expert_kernel,
        out_shape=(jax.ShapeDtypeStruct((128, 896), jnp.bfloat16),) * 4
        + (jax.ShapeDtypeStruct((2, 4, 256, 384), jnp.bfloat16),) * 2,
        in_specs=[in_smem()] + in_vmem(19),
        out_specs=tuple(in_vmem(6)),
        scratch_shapes=[pltpu.VMEM((4, 128, 896), jnp.float32)],
        compiler_params=pltpu.CompilerParams(vmem_limit_bytes=SCOPED),
        cost_estimate=LIGHT,
        name="experts",
    )(ids, sent, grad, *weights_in, *weights_out, slot_pick)


def weight_grad_kernel(*refs):
    ids_ref, sent_ref, grad_ref, gate_ref, hidden_ref, grad_pre_ref = refs[1:7]
    out_refs = refs[7:15]
    pick_ref = refs[15]
    out_grad_refs, in_grad_refs = refs[16:24], refs[24:32]
    home_refs, total_ref = refs[32:36], refs[36]
    plane = ids_ref[2]
    for expert in range(4):
        gate = gate_ref[expert][:, :1]
        rows = (grad_ref[expert].astype(jnp.float32) * gate).astype(jnp.bfloat16)
        for half in range(2):
            out_grad_refs[4 * half + expert][...] = lax.dot_general(
                hidden_ref[half, expert], rows, TN, preferred_element_type=jnp.float32
            ).astype(jnp.bfloat16)
    for expert in range(4):
        gate = gate_ref[expert][:, :1]
        part = None
        for half in range(2):
            grad_pre = (grad_pre_ref[half, expert].astype(jnp.float32) * gate).astype(jnp.bfloat16)
            in_grad_refs[4 * half + expert][...] = lax.dot_general(
                sent_ref[expert], grad_pre, TN, preferred_element_type=jnp.float32
            ).astype(jnp.bfloat16)
            product = jnp.dot(
                hidden_ref[half, expert],
                out_refs[2 * expert + half][...],
                preferred_element_type=jnp.float32,
            )
            part = product if half == 0 else part + product
        part = part.astype(jnp.bfloat16)
        columns = slice(256 * expert, 256 * (expert + 1))
        picked = pick_ref[:, :, columns].reshape(512, 256)
        placed = jnp.dot(picked, part, preferred_element_type=jnp.float32)
        if expert == 0:
            total_ref[...] = placed.reshape(4, 128, 768)
        else:
            total_ref[...] += placed.reshape(4, 128, 768)
    for away in range(4):
        home_refs[away][...] = total_ref[lax.rem(plane + away, 4)].astype(jnp.bfloat16)


def weight_grad_call(tiny, ids, sent, grad, gate, hidden, grad_pre, weights_out, slot_pick):
    return pl.pallas_call(
        weight_grad_kernel,
        out_shape=(jax.ShapeDtypeStruct((384, 768), jnp.bfloat16),) * 8
        + (jax.ShapeDtypeStruct((768, 384), jnp.bfloat16),) * 8
        + (jax.ShapeDtypeStruct((128, 768), jnp.bfloat16),) * 4,
        in_specs=in_vmem(1) + [in_smem()] + in_vmem(14),
        out_specs=tuple(in_vmem(20)),
        scratch_shapes=[pltpu.VMEM((4, 128, 768), jnp.float32)],
        compiler_params=pltpu.CompilerParams(vmem_limit_bytes=SCOPED),
        cost_estimate=LIGHT,
        name="weight_grads",
    )(tiny, ids, sent, grad, gate, hidden, grad_pre, *weights_out, slot_pick)


def project_back_kernel(ids_ref, *refs):
    grad_refs = refs[:4]
    weight_ref, token_ref, gain_two_ref, router_ref, rel_ref = refs[4:9]
    block_refs = refs[9:13]
    tiny_ref, low_ref, small_ref = refs[13:]
    chip = ids_ref[0]
    plane = ids_ref[2]
    gain = None
    for away in range(4):
        part = lax.dot_general(
            grad_refs[away][...], weight_ref[...], NT, preferred_element_type=jnp.float32
        )
        low_ref[chip ^ away] = part.astype(jnp.bfloat16)
        tokens = token_ref[chip ^ away].astype(jnp.float32)
        inverse = lax.rsqrt(jnp.mean(tokens * tokens, axis=-1, keepdims=True) + EPSILON)
        added = jnp.sum(part * tokens * inverse, axis=0, keepdims=True)
        gain = added if away == 0 else gain + added
    small_ref[...] = jnp.zeros_like(small_ref)
    small_ref[0:1, :] = gain
    small_ref[1:2, :] = gain_two_ref[...]
    small_ref[2:6, :] = router_ref[:4, :]
    small_ref[6:7, :] = rel_ref[...]
    small = small_ref[...]
    high = small.astype(jnp.bfloat16).astype(jnp.float32)
    rows = jnp.concatenate([high, small - high], axis=0).astype(jnp.bfloat16)
    for away, block_ref in enumerate(block_refs):
        block_ref[:128, :] = low_ref[lax.rem(plane + away, 4)]
        block_ref[128:, :] = rows
    tiny_ref[...] = low_ref[0, :16, :128]


def project_back_call(ids, grads, weight, tokens, gain_two, router, rel):
    return pl.pallas_call(
        project_back_kernel,
        out_shape=(jax.ShapeDtypeStruct((144, 768), jnp.bfloat16),) * 4
        + (jax.ShapeDtypeStruct((16, 128), jnp.bfloat16),),
        in_specs=[in_smem()] + in_vmem(9),
        out_specs=tuple(in_vmem(5)),
        scratch_shapes=[
            pltpu.VMEM((4, 128, 768), jnp.bfloat16),
            pltpu.VMEM((8, 768), jnp.float32),
        ],
        compiler_params=pltpu.CompilerParams(vmem_limit_bytes=SCOPED),
        cost_estimate=LIGHT,
        name="project_back",
    )(ids, *grads, weight, tokens, gain_two, router, rel)


def add_dense_kernel(ids_ref, kept_ref, *refs):
    arrived_refs = refs[4:8]
    chip = ids_ref[0]
    total = refs[12]
    small = arrived_refs[0][128:, :].astype(jnp.float32)
    for at in range(1, 4):
        small = small + arrived_refs[at][128:, :].astype(jnp.float32)
    small = small[:8] + small[8:]
    for at in range(4):
        total[at] = kept_ref[at].astype(jnp.float32) + refs[at][...].astype(jnp.float32)
        total[at, 120:, :] = small
    for away in range(4):
        refs[8 + away][...] = total[chip ^ away].astype(jnp.bfloat16)


def add_dense_call(ids, kept, theirs, arrived):
    return pl.pallas_call(
        add_dense_kernel,
        out_shape=(jax.ShapeDtypeStruct((128, 768), jnp.bfloat16),) * 4,
        in_specs=[in_smem()] + in_vmem(9),
        out_specs=tuple(in_vmem(4)),
        scratch_shapes=[pltpu.VMEM((4, 128, 768), jnp.float32)],
        compiler_params=pltpu.CompilerParams(vmem_limit_bytes=SCOPED),
        cost_estimate=LIGHT,
        name="add_dense",
    )(ids, kept, *theirs, *arrived)


def sum_dense_kernel(tiny_ref, *refs):
    total = refs[0][...].astype(jnp.float32)
    for at in range(1, 4):
        total = total + refs[at][...].astype(jnp.float32)
    refs[4][...] = total.astype(jnp.bfloat16)


def sum_dense_call(tiny, blocks):
    return pl.pallas_call(
        sum_dense_kernel,
        out_shape=jax.ShapeDtypeStruct((128, 768), jnp.bfloat16),
        in_specs=in_vmem(5),
        out_specs=in_vmem(1)[0],
        compiler_params=pltpu.CompilerParams(vmem_limit_bytes=SCOPED),
        cost_estimate=LIGHT,
        name="sum_dense",
    )(tiny, *blocks)


def pack_kernel(branch_ref, *refs):
    for at in range(3):
        refs[3 + at][:128, :] = refs[at][...]
        refs[3 + at][128:, :] = branch_ref[...]


def pack_call(branch, homes):
    return pl.pallas_call(
        pack_kernel,
        out_shape=(jax.ShapeDtypeStruct((256, 768), jnp.bfloat16),) * 3,
        in_specs=in_vmem(4),
        out_specs=tuple(in_vmem(3)),
        compiler_params=pltpu.CompilerParams(vmem_limit_bytes=SCOPED),
        cost_estimate=LIGHT,
        name="pack",
    )(branch, *homes)


def output_kernel(ids_ref, home_ref, *refs):
    plane = ids_ref[2]
    resid_ref, probs_ref, route_ref, out_ref = refs[3:]
    rows = home_ref[...].astype(jnp.float32)
    for at in range(3):
        rows = rows + refs[at][:128, :].astype(jnp.float32)
    lane = lax.broadcasted_iota(jnp.int32, (128, 128), 1)
    gate = jnp.sum(
        jnp.where(lane == route_ref[plane], probs_ref[...], 0.0), axis=-1, keepdims=True
    )
    out_ref[...] = (resid_ref[...] + gate * rows).astype(jnp.bfloat16)


def output_call(ids, home, packed, resid, probs, route):
    return pl.pallas_call(
        output_kernel,
        out_shape=jax.ShapeDtypeStruct((128, 768), jnp.bfloat16),
        in_specs=[in_smem()] + in_vmem(7),
        out_specs=in_vmem(1)[0],
        compiler_params=pltpu.CompilerParams(vmem_limit_bytes=SCOPED),
        cost_estimate=LIGHT,
        name="output",
    )(ids, home, *packed, resid, probs, route)


def finish_kernel(ids_ref, *refs):
    token_ref, gain_ref, grad_ref, out_ref = refs[4:8]
    ending_ref, tiny_ref = refs[9:]
    plane = ids_ref[2]
    gradient = refs[0][:128, :].astype(jnp.float32)
    for at in range(1, 4):
        gradient = gradient + refs[at][:128, :].astype(jnp.float32)
    tokens = token_ref[plane].astype(jnp.float32)
    inverse = lax.rsqrt(jnp.mean(tokens * tokens, axis=-1, keepdims=True) + EPSILON)
    weighted = gradient * gain_ref[...]
    inner = jnp.mean(weighted * tokens, axis=-1, keepdims=True)
    result = inverse * weighted - tokens * (inverse * inverse * inverse * inner) + grad_ref[...]
    ending = result.astype(jnp.bfloat16)
    ending_ref[:128, :] = ending
    ending_ref[128:, :] = out_ref[...]
    tiny_ref[...] = ending[:16, :128]


def finish_call(ids, arrived, tokens, gain, grad, out, ready):
    return pl.pallas_call(
        finish_kernel,
        out_shape=(
            jax.ShapeDtypeStruct((256, 768), jnp.bfloat16),
            jax.ShapeDtypeStruct((16, 128), jnp.bfloat16),
        ),
        in_specs=[in_smem()] + in_vmem(9),
        out_specs=tuple(in_vmem(2)),
        compiler_params=pltpu.CompilerParams(vmem_limit_bytes=SCOPED),
        cost_estimate=LIGHT,
        name="finish",
    )(ids, *arrived, tokens, gain, grad, out, ready)


def dense_grad_kernel(tiny_ref, ids_ref, *refs):
    grad_refs, att_ref, branch_refs = refs[:4], refs[4], refs[5:9]
    normed_ref, kept_ref = refs[9:11]
    sent_refs, total_ref = refs[11:15], refs[15]
    chip = ids_ref[0]
    core = ids_ref[1]
    plane = ids_ref[2]
    total = None
    for away in range(4):
        part = lax.dot_general(
            normed_ref[pl.ds(pl.multiple_of(128 * (chip ^ away), 128), 128), :],
            grad_refs[away][...],
            TN,
            preferred_element_type=jnp.float32,
        )
        total = part if away == 0 else total + part
    rows = None
    for away, branch_ref in enumerate(branch_refs):
        branch = branch_ref[...] if away == 0 else branch_ref[128:, :]
        part = lax.dot_general(
            att_ref[pl.ds(pl.multiple_of(128 * lax.rem(plane + 4 - away, 4), 128), 128), :],
            branch,
            TN,
            preferred_element_type=jnp.float32,
        )
        rows = part if away == 0 else rows + part
    total_ref[...] = jnp.zeros_like(total_ref)
    for half in range(2):
        for place in range(4):
            first = 384 * half + 96 * place
            total_ref[half, place, :96, :576] = total[first : first + 96]
            first = 96 * half + 24 * place
            total_ref[half, place, 96:120, :] = rows[first : first + 24]
    kept_ref[...] = total_ref[core].astype(jnp.bfloat16)
    for place in range(4):
        sent_refs[place][...] = total_ref[1 - core, place].astype(jnp.bfloat16)


def dense_grad_call(tiny, ids, grads, att, branches, normed):
    return pl.pallas_call(
        dense_grad_kernel,
        out_shape=(jax.ShapeDtypeStruct((4, 128, 768), jnp.bfloat16),)
        + (jax.ShapeDtypeStruct((128, 768), jnp.bfloat16),) * 4,
        in_specs=in_vmem(1) + [in_smem()] + in_vmem(10),
        out_specs=tuple(in_vmem(5)),
        scratch_shapes=[pltpu.VMEM((2, 4, 128, 768), jnp.float32)],
        compiler_params=pltpu.CompilerParams(vmem_limit_bytes=SCOPED),
        cost_estimate=LIGHT,
        name="dense_grads",
    )(tiny, ids, *grads, att, *branches, normed)


def tokens_kernel(ids_ref, *refs):
    grad_ref, all_ref = refs[4:]
    plane = ids_ref[2]
    for step in range(4):
        all_ref[lax.rem(plane + 4 - step, 4)] = refs[step][:128, :].astype(jnp.float32)
    for seq in range(4):
        grad_ref[:, seq, :] = all_ref[seq]


def tokens_call(ids, blocks):
    return pl.pallas_call(
        tokens_kernel,
        out_shape=jax.ShapeDtypeStruct((128, 4, 768), jnp.float32),
        in_specs=[in_smem()] + in_vmem(4),
        out_specs=in_vmem(1)[0],
        scratch_shapes=[pltpu.VMEM((4, 128, 768), jnp.float32)],
        compiler_params=pltpu.CompilerParams(vmem_limit_bytes=SCOPED),
        cost_estimate=LIGHT,
        name="tokens_back",
    )(ids, *blocks)


def add_pairs_kernel(*refs):
    blocks = refs[16:20]
    for at in range(4):
        total = refs[at][...].astype(jnp.float32) + refs[4 + at][...].astype(jnp.float32)
        blocks[at][:, :768] = total.astype(jnp.bfloat16)
        total = refs[8 + at][...].astype(jnp.float32) + refs[12 + at][...].astype(jnp.float32)
        blocks[at][:, 768:1152] = total[:384].astype(jnp.bfloat16)
        blocks[at][:, 1152:] = total[384:].astype(jnp.bfloat16)


def add_pairs_call(parts):
    return pl.pallas_call(
        add_pairs_kernel,
        out_shape=(jax.ShapeDtypeStruct((384, 1536), jnp.bfloat16),) * 4,
        in_specs=in_vmem(16),
        out_specs=tuple(in_vmem(4)),
        compiler_params=pltpu.CompilerParams(vmem_limit_bytes=SCOPED),
        cost_estimate=LIGHT,
        name="add_pairs",
    )(*parts)


def resid_back_kernel(
    ids_ref,
    home0_ref,
    home1_ref,
    home2_ref,
    home3_ref,
    resid_ref,
    probs_ref,
    route_ref,
    grad_ref,
    gain_ref,
    router_ref,
    out_weight_ref,
    grad_resid_ref,
    branch_ref,
    att0_ref,
    att1_ref,
    att2_ref,
    att3_ref,
    gain_grad_ref,
    router_grad_ref,
    all_ref,
):
    chip = ids_ref[0]
    plane = ids_ref[2]
    lane = lax.broadcasted_iota(jnp.int32, (128, 128), 1)
    collected = home0_ref[...].astype(jnp.float32)
    for home_ref in (home1_ref, home2_ref, home3_ref):
        collected = collected + home_ref[...].astype(jnp.float32)
    grad_gate = collected[:, 768:769] + collected[:, 769:770]
    probs = probs_ref[...]
    chosen = lane == route_ref[plane]
    gate = jnp.sum(jnp.where(chosen, probs, 0.0), axis=-1, keepdims=True)
    grad_sent = (collected[:, :768] * gate).astype(jnp.bfloat16).astype(jnp.float32)
    grad_logits = probs * (jnp.where(chosen, grad_gate, 0.0) - gate * grad_gate)
    resid = resid_ref[...]
    gain = gain_ref[...]
    inverse = lax.rsqrt(jnp.mean(resid * resid, axis=-1, keepdims=True) + EPSILON)
    unit = resid * inverse
    router_grad_ref[...] = lax.dot_general(
        grad_logits, unit * gain, TN, precision=PRECISE, preferred_element_type=jnp.float32
    )
    grad_normed = grad_sent + lax.dot_general(
        grad_logits, router_ref[...], NT, precision=PRECISE, preferred_element_type=jnp.float32
    )
    gain_grad_ref[...] = jnp.sum(grad_normed * unit, axis=0, keepdims=True)
    weighted = grad_normed * gain
    inner = jnp.mean(weighted * resid, axis=-1, keepdims=True)
    grad_resid = inverse * weighted - unit * (inverse * inverse * inner)
    grad_resid = grad_resid + grad_ref[plane].astype(jnp.float32)
    grad_resid_ref[...] = grad_resid
    branch = grad_resid.astype(jnp.bfloat16)
    branch_ref[...] = branch
    for away in range(4):
        all_ref[plane ^ away] = lax.dot_general(
            branch, out_weight_ref[away], NT, preferred_element_type=jnp.float32
        ).astype(jnp.bfloat16)
    for away, att_ref in enumerate((att0_ref, att1_ref, att2_ref, att3_ref)):
        att_ref[...] = all_ref[chip ^ away]


def resid_back_call(ids, homes, resid, probs, route, grad, gain, router, out_weights):
    return pl.pallas_call(
        resid_back_kernel,
        out_shape=(
            jax.ShapeDtypeStruct((128, 768), jnp.float32),
            jax.ShapeDtypeStruct((128, 768), jnp.bfloat16),
        )
        + (jax.ShapeDtypeStruct((128, 192), jnp.bfloat16),) * 4
        + (
            jax.ShapeDtypeStruct((1, 768), jnp.float32),
            jax.ShapeDtypeStruct((128, 768), jnp.float32),
        ),
        in_specs=[in_smem()] + in_vmem(11),
        out_specs=tuple(in_vmem(8)),
        scratch_shapes=[pltpu.VMEM((4, 128, 192), jnp.bfloat16)],
        compiler_params=pltpu.CompilerParams(vmem_limit_bytes=SCOPED),
        cost_estimate=LIGHT,
        name="resid_back",
    )(ids, *homes, resid, probs, route, grad, gain, router, out_weights)


def pinned(first, *others):
    tied = lax.optimization_barrier((first,) + others)
    return tied


def gather_over_ctx(block, chip, core):
    gathered = jnp.stack([block] + [to_chip(block, away) for away in range(1, 4)])
    ordered = jnp.stack([pick(gathered, at ^ chip) for at in range(4)])
    both = jnp.stack([ordered, to_core(ordered)])
    whole = jnp.stack([pick(both, core), pick(both, 1 - core)])
    return whole.reshape((8,) + block.shape)


def local_planned(
    tokens,
    gain_one,
    qkv_weight,
    out_weight,
    rel_weight,
    gain_two,
    router_weight,
    expert_in,
    expert_out,
    routes,
    bucket_table,
    grad_out,
):
    row_count, seq_count, width = tokens.shape
    token_count = row_count * seq_count
    expert_count = router_weight.shape[1]
    capacity = 2 * token_count // expert_count
    slots = expert_count * capacity
    ctx_at = lax.axis_index("ctx")
    plane = lax.axis_index("wsh")
    chip = ctx_at // 2
    core = ctx_at % 2
    ids = jnp.stack([chip, core, plane]).astype(jnp.int32)

    def by_seq(values):
        return lax.optimization_barrier(jnp.swapaxes(values, 0, 1))

    token_blocks = by_seq(tokens)
    weight_qkv = jnp.concatenate(
        lax.optimization_barrier((qkv_weight[:, 1], qkv_weight[:, 2], qkv_weight[:, 0])), axis=1
    )
    half_rows = pick(out_weight.reshape(2, 96, width), core)
    normed_low, *projected = project_call(
        ids, tiny_of(half_rows), token_blocks, gain_one[None], weight_qkv
    )
    in_one, in_two = to_chip(expert_in[0], 1), to_chip(expert_in[0], 2)
    weight_parts = plane_swap([half_rows] * 4)[1:]
    own = chip_swap(projected)
    route_blocks = by_seq(routes)
    relative = route_blocks.reshape(token_count) ^ chip
    gain_row = gain_two[None]
    *own, in_one, in_two, part_one, part_two, part_three = pinned(
        *own, in_one, in_two, *weight_parts
    )
    weight_parts = [part_one, part_two, part_three]
    own[3], weight_in, weight_out = pinned(own[3], expert_in[0], expert_out[0])
    out_one, out_two = to_chip(weight_out, 1), to_chip(weight_out, 2)
    other = [to_core(block) for block in own]

    bucket_pick = (
        bucket_table[:, None] == lax.iota(jnp.int32, rel_weight.shape[0])[None, :]
    ).astype(jnp.float32)
    head_table = jnp.dot(bucket_pick, rel_weight, precision=PRECISE).T
    line = bias_lines(head_table, core)
    *attended, prob, keyval, query = attend_call(ids, half_rows[:16, :128], own, other, line)
    attended = chip_swap(attended)
    rest = pinned(*attended, out_one, out_two, relative)
    attended, (out_one, out_two, relative) = list(rest[:4]), rest[4:]
    attended[3], late_in, late_out = pinned(attended[3], weight_in, weight_out)
    in_three, out_three = to_chip(late_in, 3), to_chip(late_out, 3)
    att_rows = gather_rows_call(ids, attended)
    att_rows, *weight_parts = pinned(att_rows, *weight_parts)
    out_weights, grad_blocks, router_wide = join_call(
        tiny_of(att_rows),
        ids,
        [out_weight] + weight_parts + [to_core(part) for part in weight_parts],
        grad_out,
        router_weight,
    )
    grad_rows = grad_blocks.reshape(token_count, width)
    att_planes = [att_rows] + [to_plane(att_rows, away) for away in range(1, 4)]
    weights_in, weights_out = [], []
    for block in (weight_in, in_one, in_two, in_three):
        weights_in += [block, to_core(block)]
    for block in (weight_out, out_one, out_two, out_three):
        weights_out += [block, to_core(block)]
    *att_planes, out_weights = pinned(*att_planes, out_weights)
    my_resid, my_probs, sent_slots, gate_slots, slot_blocks, grad_slots = route_call(
        ids,
        att_planes,
        out_weights,
        token_blocks,
        gain_row,
        router_wide,
        route_blocks,
        relative,
        grad_rows,
    )
    *homes, hidden, grad_pre = expert_call(
        ids, sent_slots, grad_slots, weights_in, weights_out, slot_blocks
    )
    tiny = tiny_of(homes[0])
    homes = plane_swap(homes)

    weight_grads = weight_grad_call(
        tiny, ids, sent_slots, grad_slots, gate_slots, hidden, grad_pre, weights_out, slot_blocks
    )
    out_parts, in_parts, expert_homes = weight_grads[:8], weight_grads[8:16], weight_grads[16:]
    *homes, expert_one, expert_two = pinned(*homes, *expert_homes[:2])
    expert_homes = [expert_one, expert_two] + list(expert_homes[2:])
    my_grad_resid, my_branch, *att_grads, grad_gain_two, grad_router = resid_back_call(
        ids,
        homes,
        my_resid,
        my_probs,
        route_blocks,
        grad_blocks,
        gain_row,
        router_wide,
        out_weights,
    )
    att_grads[0], *parts = pinned(att_grads[0], *out_parts, *in_parts)
    near = add_pairs_call(
        parts[:4]
        + [to_core(part) for part in parts[4:8]]
        + parts[8:12]
        + [to_core(part) for part in parts[12:]]
    )
    grad_mixed = turn_swap(att_grads)
    packed = pack_call(my_branch, expert_homes[1:])
    rest = pinned(*grad_mixed, *near[1:], *packed)
    grad_mixed, (near_one, near_two, near_three) = rest[:4], rest[4:7]
    packed = plane_shift([None] + list(rest[7:10]))[1:]
    near_one, near_two = to_chip(near_one, 1), to_chip(near_two, 2)
    mine_back, theirs_back, lags, tiny = attend_back_call(ids, query, prob, keyval, grad_mixed)
    theirs_back, near_one, near_two, near_three, *packed = pinned(
        theirs_back, near_one, near_two, near_three, *packed
    )
    out = output_call(ids, expert_homes[0], packed, my_resid, my_probs, route_blocks)
    grad_projected = list(add_queries_call(ids, mine_back, to_core(theirs_back)))
    grad_projected = chip_swap(grad_projected)
    def spread_planes(block):
        return jnp.stack([block] + [to_plane(block, away) for away in range(1, 4)])

    def to_tokens(gathered):
        by_place = jnp.stack([pick(gathered, (plane - at) % 4) for at in range(4)])
        return jnp.swapaxes(lax.optimization_barrier(by_place), 0, 1)

    *grad_projected, near_three = pinned(*grad_projected, near_three)
    near_three = to_chip(near_three, 3)
    grad_rel = jnp.dot(bucket_pick.T, table_grad(lags, core), precision=PRECISE)
    rel_row = jnp.where(
        (lax.iota(jnp.int32, 4) == plane)[None, :, None], grad_rel[:, None, :], 0.0
    ).reshape(-1)
    rel_row = jnp.pad(rel_row, (0, width - rel_row.shape[0]))
    *partial, tiny = project_back_call(
        ids,
        grad_projected,
        weight_qkv,
        token_blocks,
        grad_gain_two,
        grad_router,
        rel_row[None],
    )
    kept, *sent = dense_grad_call(
        to_core(tiny), ids, grad_projected, att_rows, [my_branch] + packed, normed_low
    )
    arrived = plane_shift(partial)
    *arrived, kept, sent_one, sent_two, sent_three, sent_four, near_three = pinned(
        *arrived, kept, *sent, near_three
    )
    weight_sum = 0.0
    for block in (near[0], near_one, near_two, near_three):
        weight_sum = weight_sum + block.astype(jnp.float32)
    grad_weight_out = weight_sum[None, :, :768]
    grad_weight_in = jnp.concatenate([weight_sum[:, 768:1152], weight_sum[:, 1152:]])[None]
    sent = [to_core(part) for part in (sent_one, sent_two, sent_three, sent_four)]
    dense = list(add_dense_call(ids, kept, sent, arrived))
    dense_own = dense[0]
    dense = chip_swap(dense)
    ending, tiny = finish_call(
        ids, arrived, token_blocks, gain_one[None], my_grad_resid, out, dense_own
    )
    ending = [ending] + [
        lax.ppermute(ending, "wsh", [(at, (at + step) % 4) for at in range(4)])
        for step in range(1, 4)
    ]
    summed = sum_dense_call(to_core(tiny), dense)
    gathered = chip_swap([summed] * 4)
    both = pinned(*ending, *gathered)
    ending, gathered = both[:4], both[4:]
    both = [gathered, [to_core(block) for block in gathered]]
    ordered = jnp.stack([jnp.stack(part) for part in both])
    ordered = jnp.stack([pick(ordered, core), pick(ordered, 1 - core)])
    ordered = jnp.stack([pick(jnp.swapaxes(ordered, 0, 1), at ^ chip) for at in range(4)], axis=1)
    summed = ordered.reshape(8, 128, width)
    small = summed[0, 120:].astype(jnp.float32) + summed[4, 120:].astype(jnp.float32)
    grad_out_all = summed[:, 96:120].astype(jnp.float32).reshape(192, width)
    grad_qkv = summed[:, :96, :576].astype(jnp.float32).reshape(width, 576)
    grad_qkv = jnp.stack([grad_qkv[:, 384:], grad_qkv[:, :192], grad_qkv[:, 192:384]], axis=1)
    out = to_tokens(jnp.stack([block[128:] for block in ending]))
    grad_tokens = tokens_call(ids, ending)
    rel_all = small[2 + expert_count][: 4 * grad_rel.size].reshape(-1, 4, grad_rel.shape[1])
    return (
        out,
        grad_tokens,
        small[0],
        grad_qkv,
        grad_out_all,
        pick(jnp.swapaxes(rel_all, 0, 1), plane),
        small[1],
        small[2 : 2 + expert_count].T,
        grad_weight_in,
        grad_weight_out,
    )


def solution(mesh):
    placed = (
        P("ctx", None, None),
        P(),
        P(None, None, "wsh"),
        P("wsh", None),
        P(None, "wsh"),
        P(),
        P(),
        P("ctx", None, "wsh"),
        P("ctx", "wsh", None),
        P("ctx", None, None),
        P(),
        P("ctx", None, None),
    )
    planned = mesh.shape['ctx'] == 8 and mesh.shape['wsh'] == 4
    return jax.shard_map(
        local_planned if planned else local,
        mesh=mesh,
        in_specs=placed,
        out_specs=(
            P("ctx", None, None),
            P("ctx", None, None),
            P(),
            P(None, None, "wsh"),
            P("wsh", None),
            P(None, "wsh"),
            P(),
            P(),
            P("ctx", None, "wsh"),
            P("ctx", "wsh", None),
        ),
        check_vma=False,
    )
```

```python
import functools

import jax
import jax.numpy as jnp
from jax import lax
from jax.experimental import pallas as pl
from jax.experimental.pallas import tpu as pltpu
from jax.sharding import PartitionSpec as P

HD = 64
MAXD = 128
BLK = 64


EPSILON = 1e-06
MASKED = -1e30
PRECISE = lax.Precision.HIGHEST


def norm_forward(values, gain_vec):
    inverse = lax.rsqrt(jnp.mean(values * values, axis=-1, keepdims=True) + EPSILON)
    return (values * inverse * gain_vec, inverse)


def norm_backward(values, inverse, gain_vec, gradient):
    weighted = gradient * gain_vec
    inner_mean = jnp.mean(weighted * values, axis=-1, keepdims=True)
    grad_values = inverse * weighted - values * inverse**3 * inner_mean
    grad_gain = jnp.sum(gradient * values * inverse, axis=0)
    return (grad_values, grad_gain)


def exact_gelu(values):
    return jax.nn.gelu(values, approximate=False)


def dealt_positions(first_row, row_total, devices):
    row_ids = first_row + lax.iota(jnp.int32, row_total)
    owner_dev = row_ids // (2 * BLK)
    within = row_ids % (2 * BLK)
    early_pos = owner_dev * BLK + within
    late_pos = (2 * devices - 1 - owner_dev) * BLK + within - BLK
    return jnp.where(within < BLK, early_pos, late_pos)


def block_size():
    return 512


def split_heads(packed, head_count):
    return packed.reshape(
        packed.shape[0], packed.shape[1], head_count, packed.shape[2] // head_count
    )


def run_bias(pos_query, pos_keys, head_table):
    span = 2 * BLK - 1
    starts_query = pos_query[::BLK]
    starts_keys = pos_keys[::BLK]
    query_runs = starts_query.shape[0]
    key_runs = starts_keys.shape[0]
    head_count = head_table.shape[0]
    offsets = lax.iota(jnp.int32, span) - (BLK - 1)
    distance = starts_query[:, None, None] - starts_keys[None, :, None] + offsets[None, None, :]
    clipped = jnp.clip(distance, 0, MAXD - 1)
    onehot = (clipped.reshape(-1)[:, None] == lax.iota(jnp.int32, MAXD)[None, :]).astype(
        jnp.float32
    )
    diag_values = jnp.dot(onehot, head_table.T, precision=PRECISE)
    diag_values = jnp.transpose(
        diag_values.reshape(query_runs, key_runs, span, head_count), (3, 0, 1, 2)
    )
    tiled = jnp.tile(diag_values, (1, 1, 1, BLK + 1))[..., : BLK * (span + 1)]
    tiled = tiled.reshape(head_count, query_runs, key_runs, BLK, span + 1)[..., :BLK][..., ::-1]
    bias = jnp.transpose(tiled, (1, 3, 0, 2, 4)).reshape(
        query_runs * BLK, head_count, key_runs * BLK
    )
    return (bias[:, None], onehot)


def score_block(query, key_heads, pos_query, pos_keys, head_table):
    raw_score = jnp.einsum(
        "qshd,kshd->qshk", query, key_heads, preferred_element_type=jnp.float32
    ) * HD ** (-0.5)
    distance = pos_query[:, None] - pos_keys[None, :]
    score_bias, onehot = run_bias(pos_query, pos_keys, head_table)
    score = jnp.where((distance >= 0)[:, None, None, :], raw_score + score_bias, MASKED)
    return (score, onehot)


def bias_grad(grad_score, onehot):
    span = 2 * BLK - 1
    summed = jnp.sum(grad_score.astype(jnp.float32), axis=1)
    query_rows, head_count, key_rows = summed.shape
    query_runs = query_rows // BLK
    key_runs = key_rows // BLK
    tiles = jnp.transpose(
        summed.reshape(query_runs, BLK, head_count, key_runs, BLK), (2, 0, 3, 1, 4)
    )[..., ::-1]
    widened = jnp.pad(tiles, ((0, 0), (0, 0), (0, 0), (0, 0), (0, span + 1 - BLK)))
    flat = widened.reshape(head_count, query_runs, key_runs, BLK * (span + 1))
    flat = jnp.pad(flat, ((0, 0), (0, 0), (0, 0), (0, (BLK + 1) * span - BLK * (span + 1))))
    diag_sums = jnp.sum(flat.reshape(head_count, query_runs, key_runs, BLK + 1, span), axis=3)
    diag_rows = jnp.transpose(diag_sums, (1, 2, 3, 0)).reshape(-1, head_count)
    return jnp.dot(onehot.T, diag_rows, precision=PRECISE)


def over_blocks(step_fn, carried, piece):
    piece_rows = piece[0].shape[0]
    step_rows = block_size()
    block_count = piece_rows // step_rows
    blocks = tuple(
        (member.reshape((block_count, step_rows) + member.shape[1:]) for member in piece)
    )
    firsts = step_rows * lax.iota(jnp.int32, block_count)

    def advance(carry_state, scan_item):
        return (step_fn(carry_state, scan_item[0], scan_item[1]), None)

    carried, _ = lax.scan(advance, carried, (blocks, firsts))
    return carried


def local(
    tokens,
    gain_one,
    qkv_weight,
    out_weight,
    rel_weight,
    gain_two,
    router_weight,
    expert_in,
    expert_out,
    routes,
    bucket_table,
    grad_out,
):
    ctx_count = lax.axis_size("ctx")
    row_count, seq_count, model_width = tokens.shape
    token_count = row_count * seq_count
    head_count = qkv_weight.shape[2] // HD
    head_width = head_count * HD
    score_scale = HD ** (-0.5)
    pos_query = dealt_positions(lax.axis_index("ctx") * row_count, row_count, ctx_count)
    token_rows = tokens.astype(jnp.float32).reshape(token_count, model_width)
    normed_one, inverse_one = norm_forward(token_rows, gain_one)
    normed_low = normed_one.astype(jnp.bfloat16)
    projected = jnp.einsum(
        "nd,dce->nce", normed_low, qkv_weight, preferred_element_type=jnp.float32
    ).astype(jnp.bfloat16)
    query_flat = projected[:, 0].reshape(row_count, seq_count, head_width)
    query = split_heads(query_flat, head_count)
    keyval = projected[:, 1:].reshape(row_count, seq_count, 2 * head_width)
    own_keys = split_heads(keyval[..., :head_width], head_count)
    own_values = split_heads(keyval[..., head_width:], head_count)
    bucket_pick = (
        bucket_table[:, None] == lax.iota(jnp.int32, rel_weight.shape[0])[None, :]
    ).astype(jnp.float32)
    head_table = jnp.dot(bucket_pick, rel_weight, precision=PRECISE).T

    def attend(carry_state, key_block, first_row):
        key_heads = split_heads(key_block[0][..., :head_width], head_count)
        value_heads = split_heads(key_block[0][..., head_width:], head_count)
        pos_keys = dealt_positions(first_row, key_heads.shape[0], ctx_count)
        score, _ = score_block(query, key_heads, pos_query, pos_keys, head_table)
        row_max, denominator, weighted = carry_state
        new_max = jnp.maximum(row_max, jnp.max(score, axis=-1))
        rescale = jnp.exp(row_max - new_max)
        weights = jnp.exp(score - new_max[..., None])
        denominator = rescale * denominator + jnp.sum(weights, axis=-1)
        weighted = rescale[..., None] * weighted + jnp.einsum(
            "qshk,kshd->qshd",
            weights.astype(jnp.bfloat16),
            value_heads,
            preferred_element_type=jnp.float32,
        )
        return (new_max, denominator, weighted)

    stat_shape = (row_count, seq_count, head_count)
    zero_heads = jnp.zeros((row_count, seq_count, head_count, HD), jnp.float32)
    initial = (
        jnp.full(stat_shape, MASKED, jnp.float32),
        jnp.zeros(stat_shape, jnp.float32),
        zero_heads,
    )
    row_max, denominator, weighted = over_blocks(
        attend, initial, (lax.all_gather(keyval, "ctx", axis=0, tiled=True),)
    )
    attended = weighted / denominator[..., None]
    log_total = row_max + jnp.log(denominator)
    attended_low = attended.reshape(token_count, head_width).astype(jnp.bfloat16)
    branch = lax.psum(
        jnp.dot(attended_low, out_weight, preferred_element_type=jnp.float32).astype(jnp.bfloat16),
        "wsh",
    ).astype(jnp.float32)
    resid = token_rows + branch
    normed_two, inverse_two = norm_forward(resid, gain_two)
    logits = jnp.dot(normed_two, router_weight, precision=PRECISE)
    shifted = jnp.exp(logits - jnp.max(logits, axis=-1, keepdims=True))
    gate_probs = shifted / jnp.sum(shifted, axis=-1, keepdims=True)
    expert_count = router_weight.shape[1]
    expert_ids = routes.reshape(token_count)
    choose = expert_ids[:, None] == lax.iota(jnp.int32, expert_count)[None, :]
    gate_value = jnp.sum(jnp.where(choose, gate_probs, 0.0), axis=1)
    lower_ones = (
        lax.iota(jnp.int32, token_count)[:, None] >= lax.iota(jnp.int32, token_count)[None, :]
    ).astype(jnp.bfloat16)
    filled = jnp.dot(
        lower_ones, choose.astype(jnp.bfloat16), preferred_element_type=jnp.float32
    ).astype(jnp.int32)
    slot_index = jnp.sum(jnp.where(choose, filled - 1, 0), axis=1)
    capacity = max(2, 2 * token_count // expert_count)
    target = expert_ids * capacity + slot_index
    slot_pick = target[:, None] == lax.iota(jnp.int32, expert_count * capacity)[None, :]
    slot_low = slot_pick.astype(jnp.bfloat16)
    slot_full = slot_pick.astype(jnp.float32)
    weight_in = expert_in[0]
    weight_out = expert_out[0]

    def spread(values):
        buffer = jnp.einsum(
            "nm,nd->md", slot_low, values, preferred_element_type=jnp.float32
        ).astype(jnp.bfloat16)
        doubled = jnp.broadcast_to(
            buffer.reshape(expert_count, 1, capacity, model_width),
            (expert_count, 2, capacity, model_width),
        )
        return doubled.reshape(2 * expert_count, capacity, model_width)

    def collect(returned):
        row_width = returned.shape[-1]
        paired = jnp.sum(returned.reshape(expert_count, 2, capacity, row_width), axis=1)
        return jnp.dot(
            slot_full, paired.reshape(expert_count * capacity, row_width), precision=PRECISE
        )

    arrived_rows = lax.all_to_all(
        spread(normed_two.astype(jnp.bfloat16)), "ctx", split_axis=0, concat_axis=0, tiled=True
    )
    flat_rows = arrived_rows.reshape(-1, model_width)
    pre_act = jnp.dot(flat_rows, weight_in, preferred_element_type=jnp.float32)
    hidden = exact_gelu(pre_act).astype(jnp.bfloat16)
    returned = lax.all_to_all(
        jnp.dot(hidden, weight_out, preferred_element_type=jnp.float32)
        .reshape(arrived_rows.shape)
        .astype(jnp.bfloat16),
        "ctx",
        split_axis=0,
        concat_axis=0,
        tiled=True,
    ).astype(jnp.float32)
    expert_rows = lax.psum(collect(returned).astype(jnp.bfloat16), "wsh").astype(jnp.float32)
    result = resid + gate_value[:, None] * expert_rows
    out = result.astype(jnp.bfloat16).reshape(row_count, seq_count, model_width)
    grad_rows_f = grad_out.astype(jnp.float32).reshape(token_count, model_width)
    grad_gate = jnp.sum(grad_rows_f * expert_rows, axis=1)
    grad_expert_rows = (gate_value[:, None] * grad_rows_f).astype(jnp.bfloat16)
    arrived_grad = lax.all_to_all(
        spread(grad_expert_rows), "ctx", split_axis=0, concat_axis=0, tiled=True
    )
    flat_rows = arrived_rows.reshape(-1, model_width)
    flat_grad = arrived_grad.reshape(-1, model_width)
    pre_act = jnp.dot(flat_rows, weight_in, preferred_element_type=jnp.float32)
    hidden, gelu_pull = jax.vjp(exact_gelu, pre_act)
    hidden_low = hidden.astype(jnp.bfloat16)
    grad_weight_out = jnp.einsum(
        "rf,rd->fd", hidden_low, flat_grad, preferred_element_type=jnp.float32
    )
    grad_hidden = jnp.einsum("rd,fd->rf", flat_grad, weight_out, preferred_element_type=jnp.float32)
    grad_pre = gelu_pull(grad_hidden)[0].astype(jnp.bfloat16)
    grad_weight_in = jnp.einsum(
        "rd,rf->df", flat_rows, grad_pre, preferred_element_type=jnp.float32
    )
    partial_back = jnp.einsum(
        "rf,df->rd", grad_pre, weight_in, preferred_element_type=jnp.float32
    ).reshape(arrived_rows.shape)
    returned_grad = lax.all_to_all(
        partial_back.astype(jnp.bfloat16), "ctx", split_axis=0, concat_axis=0, tiled=True
    ).astype(partial_back.dtype)
    grad_sent = lax.psum(collect(returned_grad).astype(jnp.bfloat16), "wsh").astype(jnp.float32)
    grad_sent = lax.optimization_barrier(grad_sent.astype(jnp.bfloat16)).astype(jnp.float32)
    grad_logits = gate_probs * (
        jnp.where(choose, grad_gate[:, None], 0.0) - (gate_value * grad_gate)[:, None]
    )
    grad_router = jnp.dot(normed_two.T, grad_logits, precision=PRECISE)
    grad_normed_two = grad_sent + jnp.dot(grad_logits, router_weight.T, precision=PRECISE)
    grad_resid, grad_gain_two = norm_backward(resid, inverse_two, gain_two, grad_normed_two)
    grad_resid = grad_resid + grad_rows_f
    grad_branch = grad_resid.astype(jnp.bfloat16)
    grad_out_rows = jnp.einsum(
        "nw,nd->wd", attended_low, grad_branch, preferred_element_type=jnp.float32
    )
    grad_att = jnp.einsum(
        "nd,wd->nw", grad_branch, out_weight, preferred_element_type=jnp.float32
    ).astype(jnp.bfloat16)
    grad_att_flat = grad_att.reshape(row_count, seq_count, head_width)
    grad_att_heads = split_heads(grad_att_flat, head_count)
    row_inner = jnp.sum(grad_att_heads.astype(jnp.float32) * attended, axis=-1)

    def query_grads(carry_state, key_block, first_row):
        key_heads = split_heads(key_block[0][..., :head_width], head_count)
        value_heads = split_heads(key_block[0][..., head_width:], head_count)
        pos_keys = dealt_positions(first_row, key_heads.shape[0], ctx_count)
        score, onehot = score_block(query, key_heads, pos_query, pos_keys, head_table)
        weights = jnp.exp(score - log_total[..., None])
        grad_weights = jnp.einsum(
            "qshd,kshd->qshk", grad_att_heads, value_heads, preferred_element_type=jnp.float32
        )
        grad_score = (weights * (grad_weights - row_inner[..., None])).astype(jnp.bfloat16)
        grad_query = (
            carry_state[0]
            + jnp.einsum(
                "qshk,kshd->qshd", grad_score, key_heads, preferred_element_type=jnp.float32
            )
            * score_scale
        )
        return (grad_query, carry_state[1] + bias_grad(grad_score, onehot))

    def key_grads(carry_state, query_block, first_row):
        query_heads = split_heads(query_block[0][..., :head_width], head_count)
        grad_heads = split_heads(query_block[0][..., head_width:], head_count)
        pos_rows = dealt_positions(first_row, query_heads.shape[0], ctx_count)
        score, _ = score_block(query_heads, own_keys, pos_rows, pos_query, head_table)
        weights = jnp.exp(score - query_block[1][..., None])
        grad_value = carry_state[1] + jnp.einsum(
            "qshk,qshd->kshd",
            weights.astype(jnp.bfloat16),
            grad_heads,
            preferred_element_type=jnp.float32,
        )
        grad_weights = jnp.einsum(
            "qshd,kshd->qshk", grad_heads, own_values, preferred_element_type=jnp.float32
        )
        grad_score = (weights * (grad_weights - query_block[2][..., None])).astype(jnp.bfloat16)
        grad_key = (
            carry_state[0]
            + jnp.einsum(
                "qshk,qshd->kshd", grad_score, query_heads, preferred_element_type=jnp.float32
            )
            * score_scale
        )
        return (grad_key, grad_value)

    packed = jnp.concatenate([query_flat, grad_att_flat], axis=-1)
    zero_table = jnp.zeros((MAXD, head_count), jnp.float32)
    grad_query, grad_table = over_blocks(
        query_grads, (zero_heads, zero_table), (lax.all_gather(keyval, "ctx", axis=0, tiled=True),)
    )
    grad_key, grad_value = over_blocks(
        key_grads,
        (zero_heads, zero_heads),
        (
            lax.all_gather(packed, "ctx", axis=0, tiled=True),
            lax.all_gather(log_total.astype(jnp.bfloat16), "ctx", axis=0, tiled=True).astype(
                jnp.float32
            ),
            lax.all_gather(row_inner.astype(jnp.bfloat16), "ctx", axis=0, tiled=True).astype(
                jnp.float32
            ),
        ),
    )
    grad_projected = jnp.stack(
        [member.reshape(token_count, head_width) for member in (grad_query, grad_key, grad_value)],
        axis=1,
    ).astype(jnp.bfloat16)
    grad_normed_one = lax.psum(
        jnp.einsum(
            "nce,dce->nd", grad_projected, qkv_weight, preferred_element_type=jnp.float32
        ).astype(jnp.bfloat16),
        "wsh",
    ).astype(jnp.float32)
    grad_qkv = jnp.einsum(
        "nd,nce->dce", normed_low, grad_projected, preferred_element_type=jnp.float32
    )
    grad_tokens, grad_gain_one = norm_backward(token_rows, inverse_one, gain_one, grad_normed_one)
    grad_tokens = grad_tokens + grad_resid
    grad_rel = jnp.dot(bucket_pick.T, grad_table, precision=PRECISE)
    summed_grads = lax.psum(
        (grad_qkv, grad_out_rows, grad_rel, grad_gain_one, grad_gain_two, grad_router), "ctx"
    )
    return (
        out,
        grad_tokens.reshape(row_count, seq_count, model_width),
        summed_grads[3],
        summed_grads[0],
        summed_grads[1],
        summed_grads[2],
        summed_grads[4],
        summed_grads[5],
        grad_weight_in[None],
        grad_weight_out[None],
    )


NT = (((1,), (1,)), ((), ()))
TN = (((0,), (0,)), ((), ()))
SCOPED = 16 * 1024 * 1024
LIGHT = pl.CostEstimate(flops=1_000_000, bytes_accessed=10_000, transcendentals=0)


def strip(step, side):
    width = 128 * (step + 1) if side == 0 else 128 * (8 - step)
    first = 0 if side == 0 else 128 * (step + 1)
    return (width, first)


def skewed(values, leftward):
    width = values.shape[1]
    row = lax.broadcasted_iota(jnp.int32, values.shape, 0)
    for bit in range(6):
        shift = width - (1 << bit) if leftward else 1 << bit
        moved = pltpu.roll(values, shift, 1)
        values = jnp.where((row & (1 << bit)) != 0, moved, values)
    return values


def attend_kernel(ids_ref, *refs):
    own_refs, other_refs, line_ref = refs[1:5], refs[5:9], refs[9]
    att_refs = refs[10:14]
    far_prob_ref, far_keyval_ref, far_query_ref = refs[14:17]
    bias_ref, own_ref, other_ref, all_ref, near_ref = refs[17:22]
    prob_ref, keyval_ref, query_ref, sems, out_sems = refs[22:]

    def prob_copy(step):
        return pltpu.make_async_copy(
            prob_ref.at[:, step], far_prob_ref.at[:, step], out_sems.at[step]
        )

    def other_copies():
        return (
            pltpu.make_async_copy(keyval_ref, far_keyval_ref, out_sems.at[4]),
            pltpu.make_async_copy(query_ref, far_query_ref, out_sems.at[5]),
        )

    chip = ids_ref[0]
    core = ids_ref[1]

    def gather_keys(parity):
        for place in range(16):
            owner = place if place < 8 else 15 - place
            half = 0 if place < 8 else BLK
            source = own_ref if owner % 2 == parity else other_ref
            keyval_ref[place * BLK : (place + 1) * BLK, :] = source[
                owner // 2, half : half + BLK, :
            ]

    @pl.when(pl.program_id(0) == 0)
    def _():
        fetch(list(own_refs) + list(other_refs), [near_ref.at[at] for at in range(8)], sems)
        for away in range(4):
            own_ref[chip ^ away] = near_ref[away, :, :384]
            other_ref[chip ^ away] = near_ref[4 + away, :, :384]
            query_ref[chip ^ away] = near_ref[away, :, 384:] * jnp.bfloat16(HD ** (-0.5))
        for head in range(3):
            for side in range(2):
                line = jnp.broadcast_to(line_ref[head, side : side + 1, :], (BLK, 512))
                bias_ref[head, side] = skewed(line, False)[:, 128:384]

        @pl.when(core == 0)
        def _():
            gather_keys(0)

        @pl.when(core == 1)
        def _():
            gather_keys(1)

        for copy in other_copies():
            copy.start()

    def attend_step(step):
        jobs = [(head, side) for side in range(2) for head in range(3)]
        scores = []
        for head, side in jobs:
            width, _ = strip(step, side)
            rows = slice(side * BLK, (side + 1) * BLK)
            query = query_ref[step, rows, HD * head : HD * (head + 1)]
            keys = keyval_ref[:width, HD * head : HD * (head + 1)]
            score = lax.dot_general(query, keys, NT, preferred_element_type=jnp.float32)
            near = min(width, 256)
            close = score[:, width - near :] + bias_ref[head, side, :, 256 - near :]
            if width > near:
                score = jnp.concatenate([score[:, : width - near], close], axis=1)
            else:
                score = close
            scores.append(score)
        tops = [jnp.max(score, axis=-1, keepdims=True) for score in scores]
        weights = [jnp.exp(score - top) for score, top in zip(scores, tops)]
        totals = [jnp.sum(weight, axis=-1, keepdims=True) for weight in weights]
        probs = [
            (weight * (1.0 / total)).astype(jnp.bfloat16)
            for weight, total in zip(weights, totals)
        ]
        for (head, side), prob in zip(jobs, probs):
            width, first = strip(step, side)
            prob_ref[head, step, :, first : first + width] = prob
        prob_copy(step).start()
        mixed = [
            jnp.dot(
                prob,
                keyval_ref[: prob.shape[1], 192 + HD * head : 192 + HD * (head + 1)],
                preferred_element_type=jnp.float32,
            ).astype(jnp.bfloat16)
            for (head, side), prob in zip(jobs, probs)
        ]
        for side in range(2):
            rows = slice(side * BLK, (side + 1) * BLK)
            all_ref[step, rows, :] = jnp.concatenate(
                mixed[3 * side : 3 * side + 3], axis=1
            )

    for step in range(4):
        pl.when(pl.program_id(0) == step)(functools.partial(attend_step, step))

    @pl.when(pl.program_id(0) == 3)
    def _():
        for away in range(4):
            att_refs[away][...] = all_ref[chip ^ away]
        for step in range(4):
            prob_copy(step).wait()
        for copy in other_copies():
            copy.wait()


def attend_back_kernel(ids_ref, *refs):
    far_query_ref, prob_ref, far_keyval_ref = refs[:3]
    grad_refs = refs[3:7]
    mine_ref, theirs_ref, lags_ref, tiny_ref, total_ref, near_ref, grad_ref = refs[7:14]
    query_ref, keyval_ref, sems = refs[14:]
    core = ids_ref[1]
    plane = ids_ref[2]

    @pl.when(pl.program_id(0) == 0)
    def _():
        total_ref[...] = jnp.zeros_like(total_ref)
        near_ref[...] = jnp.zeros_like(near_ref)
        fetch(
            list(grad_refs) + [far_query_ref, far_keyval_ref],
            [grad_ref.at[plane ^ away] for away in range(4)] + [query_ref, keyval_ref],
            sems,
        )

    def back_step(step):
        jobs = [(head, side) for side in range(2) for head in range(3)]
        queries, grads, probs, products = [], [], [], []
        for head, side in jobs:
            width, first = strip(step, side)
            rows = slice(side * BLK, (side + 1) * BLK)
            queries.append(query_ref[step, rows, HD * head : HD * (head + 1)])
            grad = grad_ref[step, rows, HD * head : HD * (head + 1)]
            grads.append(grad)
            values = keyval_ref[:width, 192 + HD * head : 192 + HD * (head + 1)]
            prob = prob_ref[head, 0, :, first : first + width]
            probs.append(prob)
            grad_prob = lax.dot_general(grad, values, NT, preferred_element_type=jnp.float32)
            products.append(prob.astype(jnp.float32) * grad_prob)
        inners = [jnp.sum(product, axis=-1, keepdims=True) for product in products]
        lows = [
            (product - prob.astype(jnp.float32) * inner).astype(jnp.bfloat16)
            for product, prob, inner in zip(products, probs, inners)
        ]
        dqs = [
            (
                jnp.dot(
                    low,
                    keyval_ref[: low.shape[1], HD * head : HD * (head + 1)],
                    preferred_element_type=jnp.float32,
                )
                * HD ** (-0.5)
            ).astype(jnp.bfloat16)
            for (head, side), low in zip(jobs, lows)
        ]
        for side in range(2):
            rows = slice(side * BLK, (side + 1) * BLK)
            width, _ = strip(step, side)
            mine_ref[step, rows, 384:] = jnp.concatenate(dqs[3 * side : 3 * side + 3], axis=1)
            parts = []
            for left, right in ((lows, queries), (probs, grads)):
                for head in range(3):
                    parts.append(
                        lax.dot_general(
                            left[3 * side + head],
                            right[3 * side + head],
                            TN,
                            preferred_element_type=jnp.float32,
                        )
                    )
            total_ref[:width, :] += jnp.concatenate(parts, axis=1)
        for (head, side), low in zip(jobs, lows):
            width, _ = strip(step, side)
            score = low.astype(jnp.float32)
            near_ref[head, 2 * side] += score[:, width - 128 :]
            if width >= 256:
                near_ref[head, 2 * side + 1] += score[:, width - 256 : width - 128]
            if width > 256:
                far = score[:, :128]
                for chunk in range(1, (width - 256) // 128):
                    far = far + score[:, 128 * chunk : 128 * (chunk + 1)]
                near_ref[head, 4] += far

    for step in range(4):
        pl.when(pl.program_id(0) == step)(functools.partial(back_step, step))

    def scatter_keys(parity):
        for place in range(16):
            owner = place if place < 8 else 15 - place
            half = 0 if place < 8 else BLK
            target = mine_ref if owner % 2 == parity else theirs_ref
            target[owner // 2, half : half + BLK, :384] = total_ref[
                place * BLK : (place + 1) * BLK, :
            ].astype(jnp.bfloat16)

    @pl.when(pl.program_id(0) == 3)
    def _():
        tiny_ref[...] = total_ref[:16, :128].astype(jnp.bfloat16)
        lags_ref[...] = jnp.zeros_like(lags_ref)
        for head in range(3):
            for kind in range(4):
                wide = jnp.concatenate(
                    [near_ref[head, kind], jnp.zeros((BLK, 128), jnp.float32)], axis=1
                )
                lags_ref[head, kind : kind + 1, :] = jnp.sum(
                    skewed(wide, True), axis=0, keepdims=True
                )
            lags_ref[head, 4:5, :128] = jnp.sum(near_ref[head, 4], axis=0, keepdims=True)

        @pl.when(core == 0)
        def _():
            scatter_keys(0)

        @pl.when(core == 1)
        def _():
            scatter_keys(1)


def whole(*shape):
    return pl.BlockSpec(shape, lambda at: (0,) * len(shape))


def in_hbm():
    return pl.BlockSpec(memory_space=pltpu.HBM)


def by_step():
    return pl.BlockSpec((3, 1, BLK, 1152), lambda at: (0, at, 0, 0))


def in_vmem(count):
    return [pl.BlockSpec(memory_space=pltpu.VMEM)] * count


def attend_call(ids, tiny, own, other, line):
    return pl.pallas_call(
        attend_kernel,
        grid=(4,),
        out_shape=(jax.ShapeDtypeStruct((128, 192), jnp.bfloat16),) * 4
        + (
            jax.ShapeDtypeStruct((3, 4, BLK, 1152), jnp.bfloat16),
            jax.ShapeDtypeStruct((1024, 384), jnp.bfloat16),
            jax.ShapeDtypeStruct((4, 128, 192), jnp.bfloat16),
        ),
        in_specs=[in_smem(), whole(16, 128)] + [in_hbm()] * 8 + [whole(3, 2, 512)],
        out_specs=(whole(128, 192),) * 4 + (in_hbm(),) * 3,
        scratch_shapes=[
            pltpu.VMEM((3, 2, BLK, 256), jnp.float32),
            pltpu.VMEM((4, 128, 384), jnp.bfloat16),
            pltpu.VMEM((4, 128, 384), jnp.bfloat16),
            pltpu.VMEM((4, 128, 192), jnp.bfloat16),
            pltpu.VMEM((8, 128, 576), jnp.bfloat16),
            pltpu.VMEM((3, 4, BLK, 1152), jnp.bfloat16),
            pltpu.VMEM((1024, 384), jnp.bfloat16),
            pltpu.VMEM((4, 128, 192), jnp.bfloat16),
            pltpu.SemaphoreType.DMA((8,)),
            pltpu.SemaphoreType.DMA((6,)),
        ],
        compiler_params=pltpu.CompilerParams(
            vmem_limit_bytes=SCOPED, dimension_semantics=("arbitrary",)
        ),
        cost_estimate=LIGHT,
        name="attend",
    )(ids, tiny, *own, *other, line)


def attend_back_call(ids, query, prob, keyval, grads):
    return pl.pallas_call(
        attend_back_kernel,
        grid=(4,),
        out_shape=(
            jax.ShapeDtypeStruct((4, 128, 576), jnp.bfloat16),
            jax.ShapeDtypeStruct((4, 128, 384), jnp.bfloat16),
            jax.ShapeDtypeStruct((3, 8, 256), jnp.float32),
            jax.ShapeDtypeStruct((16, 128), jnp.bfloat16),
        ),
        in_specs=[
            in_smem(),
            in_hbm(),
            by_step(),
            in_hbm(),
        ]
        + [in_hbm()] * 4,
        out_specs=(
            whole(4, 128, 576),
            whole(4, 128, 384),
            whole(3, 8, 256),
            whole(16, 128),
        ),
        scratch_shapes=[
            pltpu.VMEM((1024, 384), jnp.float32),
            pltpu.VMEM((3, 5, BLK, 128), jnp.float32),
            pltpu.VMEM((4, 128, 192), jnp.bfloat16),
            pltpu.VMEM((4, 128, 192), jnp.bfloat16),
            pltpu.VMEM((1024, 384), jnp.bfloat16),
            pltpu.SemaphoreType.DMA((6,)),
        ],
        compiler_params=pltpu.CompilerParams(
            vmem_limit_bytes=SCOPED, dimension_semantics=("arbitrary",)
        ),
        cost_estimate=LIGHT,
        name="attend_back",
    )(ids, query, prob, keyval, *grads)


def to_core(values):
    return lax.ppermute(values, "ctx", [(at, at ^ 1) for at in range(8)])


def to_chip(values, away):
    return lax.ppermute(values, "ctx", [(at, at ^ (2 * away)) for at in range(8)])


def to_plane(values, away):
    return lax.ppermute(values, "wsh", [(at, at ^ away) for at in range(4)])


def tiny_of(source):
    return to_core(source.reshape(-1, source.shape[-1])[:16, :128])


def chip_swap(blocks):
    return [blocks[0]] + [to_chip(blocks[away], away) for away in range(1, 4)]


def plane_shift(blocks):
    return [blocks[0]] + [
        lax.ppermute(blocks[step], "wsh", [(at, (at + step) % 4) for at in range(4)])
        for step in range(1, 4)
    ]


def plane_swap(blocks):
    return [blocks[0]] + [to_plane(blocks[away], away) for away in range(1, 4)]


def seat(chip, core, plane):
    return (2 * chip + core) * 4 + plane


def turn_swap(blocks):
    return [
        lax.ppermute(
            block,
            ("ctx", "wsh"),
            [
                (seat(chip, core, plane), seat(plane, core, chip ^ away))
                for chip in range(4)
                for core in range(2)
                for plane in range(4)
            ],
        )
        for away, block in enumerate(blocks)
    ]


def pick(blocks, at):
    return lax.dynamic_index_in_dim(blocks, at, 0, keepdims=False)


def bias_lines(head_table, core):
    shifted = head_table - head_table[:, MAXD - 1 :]
    turned = shifted[:, ::-1]

    def line(zeros):
        return jnp.pad(
            jnp.pad(turned, ((0, 0), (zeros, 0))),
            ((0, 0), (0, 512 - MAXD - zeros)),
            constant_values=MASKED,
        )

    even, odd = line(129), line(193)
    return jnp.where(
        core == 0, jnp.stack([even, odd], axis=1), jnp.stack([odd, even], axis=1)
    )


def table_grad(lags, core):
    offsets = lax.iota(jnp.int32, 256)
    offsets = jnp.where(offsets < 128, offsets, offsets - 256)
    base = BLK * jnp.stack([core, core + 2, 1 - core, 3 - core])
    clipped = jnp.clip(base[:, None] - offsets[None, :], 0, MAXD - 1)
    onehot = (clipped[..., None] == lax.iota(jnp.int32, MAXD)).astype(jnp.float32)
    table = jnp.einsum("hkz,kzd->dh", lags[:, :4], onehot, precision=PRECISE)
    last = (lax.iota(jnp.int32, MAXD) == MAXD - 1).astype(jnp.float32)
    return table + last[:, None] * jnp.sum(lags[:, 4], axis=-1)


def gelu_parts(values):
    cdf = 0.5 * (1.0 + lax.erf(values * (0.5**0.5)))
    density = jnp.exp(-0.5 * values * values) * ((0.5 / jnp.pi) ** 0.5)
    return (values * cdf, cdf + values * density)


def in_smem():
    return pl.BlockSpec(memory_space=pltpu.SMEM)


def split_column(column):
    high = column.astype(jnp.bfloat16)
    low = (column - high.astype(jnp.float32)).astype(jnp.bfloat16)
    lane = lax.broadcasted_iota(jnp.int32, (column.shape[0], 128), 1)
    wide = jnp.where(
        lane == 0,
        high.astype(jnp.float32),
        jnp.where(lane == 1, low.astype(jnp.float32), 0.0),
    )
    return wide.astype(jnp.bfloat16)


def project_kernel(ids_ref, token_ref, gain_ref, weight_ref, normed_ref, *refs):
    chip = ids_ref[0]
    tokens = token_ref[...].reshape(512, 768).astype(jnp.float32)
    inverse = lax.rsqrt(jnp.mean(tokens * tokens, axis=-1, keepdims=True) + EPSILON)
    normed = (tokens * inverse * gain_ref[...]).astype(jnp.bfloat16)
    normed_ref[...] = normed
    projected = jnp.dot(normed, weight_ref[...], preferred_element_type=jnp.float32)
    refs[4][...] = projected.astype(jnp.bfloat16).reshape(4, 128, 576)
    for away in range(4):
        refs[away][...] = refs[4][chip ^ away]


def project_call(ids, tokens, gain, weight):
    return pl.pallas_call(
        project_kernel,
        out_shape=(jax.ShapeDtypeStruct((512, 768), jnp.bfloat16),)
        + (jax.ShapeDtypeStruct((128, 576), jnp.bfloat16),) * 4,
        in_specs=[in_smem()] + in_vmem(3),
        out_specs=tuple(in_vmem(5)),
        scratch_shapes=[pltpu.VMEM((4, 128, 576), jnp.bfloat16)],
        compiler_params=pltpu.CompilerParams(vmem_limit_bytes=SCOPED),
        cost_estimate=LIGHT,
        name="project",
    )(ids, tokens, gain, weight)


def gather_rows_kernel(ids_ref, *refs):
    chip = ids_ref[0]
    for away in range(4):
        refs[4][pl.ds(pl.multiple_of(128 * (chip ^ away), 128), 128), :] = refs[away][...]


def gather_rows_call(ids, blocks):
    return pl.pallas_call(
        gather_rows_kernel,
        out_shape=jax.ShapeDtypeStruct((512, 192), jnp.bfloat16),
        in_specs=[in_smem()] + in_vmem(4),
        out_specs=in_vmem(1)[0],
        compiler_params=pltpu.CompilerParams(vmem_limit_bytes=SCOPED),
        cost_estimate=LIGHT,
        name="gather_rows",
    )(ids, *blocks)


def add_queries_kernel(ids_ref, mine_ref, theirs_ref, *sum_refs):
    chip = ids_ref[0]
    for away, sum_ref in enumerate(sum_refs):
        mine = mine_ref[chip ^ away]
        total = mine[:, :384].astype(jnp.float32) + theirs_ref[chip ^ away].astype(jnp.float32)
        sum_ref[:, :384] = total.astype(jnp.bfloat16)
        sum_ref[:, 384:] = mine[:, 384:]


def add_queries_call(ids, mine, theirs):
    return pl.pallas_call(
        add_queries_kernel,
        out_shape=(jax.ShapeDtypeStruct((128, 576), jnp.bfloat16),) * 4,
        in_specs=[in_smem()] + in_vmem(2),
        out_specs=tuple(in_vmem(4)),
        compiler_params=pltpu.CompilerParams(vmem_limit_bytes=SCOPED),
        cost_estimate=LIGHT,
        name="add_queries",
    )(ids, mine, theirs)


def fetch(sources, targets, sems):
    copies = [
        pltpu.make_async_copy(source, target, sems.at[at])
        for at, (source, target) in enumerate(zip(sources, targets))
    ]
    for copy in copies:
        copy.start()
    for copy in copies:
        copy.wait()


def route_kernel(*refs):
    ids_ref = refs[0]
    att_refs, part_refs = refs[1:5], refs[5:12]
    token_ref, gain_ref, router_ref, route_ref, slot_ref = refs[12:17]
    resid_ref, probs_ref, sent_ref, gate_ref, out_weight_ref = refs[17:22]
    payload_ref, branch_ref, all_probs_ref, att_ref, own_ref, half_ref, sems = refs[22:]
    fetch(
        list(att_refs) + list(part_refs),
        [att_ref.at[at] for at in range(4)] + [own_ref] + [half_ref.at[at] for at in range(6)],
        sems,
    )
    att_refs = [att_ref.at[at] for at in range(4)]
    part_refs = [own_ref] + [half_ref.at[at] for at in range(6)]
    core = ids_ref[1]
    plane = ids_ref[2]
    out_weight_ref[0] = part_refs[0][...]
    own_rows = pl.ds(pl.multiple_of(96 * core, 32), 96)
    other_rows = pl.ds(pl.multiple_of(96 - 96 * core, 32), 96)
    for away in range(1, 4):
        out_weight_ref[away, own_rows, :] = part_refs[away][...]
        out_weight_ref[away, other_rows, :] = part_refs[3 + away][...]
    branch = token_ref[...].reshape(512, 768).astype(jnp.float32)
    for away, att_ref in enumerate(att_refs):
        branch = branch + jnp.dot(
            att_ref[...], out_weight_ref[away], preferred_element_type=jnp.float32
        )
    branch_ref[...] = branch.reshape(4, 128, 768)
    inverse = lax.rsqrt(jnp.mean(branch * branch, axis=-1, keepdims=True) + EPSILON)
    normed = branch * inverse * gain_ref[...]
    payload_ref[:, :768] = normed.astype(jnp.bfloat16)
    logits = jnp.dot(normed, router_ref[...], precision=PRECISE, preferred_element_type=jnp.float32)
    lane = lax.broadcasted_iota(jnp.int32, (512, 128), 1)
    logits = jnp.where(lane < 4, logits, MASKED)
    shifted = jnp.exp(logits - jnp.max(logits, axis=-1, keepdims=True))
    probs = shifted / jnp.sum(shifted, axis=-1, keepdims=True)
    all_probs_ref[...] = probs.reshape(4, 128, 128)
    gate = jnp.sum(
        jnp.where(lane == route_ref[...].reshape(512, 1), probs, 0.0), axis=-1, keepdims=True
    )
    payload_ref[:, 768:] = split_column(gate)
    resid_ref[...] = branch_ref[plane]
    probs_ref[...] = all_probs_ref[plane]
    placed = jnp.dot(slot_ref[...], payload_ref[...], preferred_element_type=jnp.float32)
    sent_ref[...] = placed[:, :768].astype(jnp.bfloat16).reshape(4, 256, 768)
    gate_ref[...] = jnp.broadcast_to(
        placed[:, 768:769] + placed[:, 769:770], (1024, 128)
    ).reshape(4, 256, 128)


def route_call(ids, att, parts, tokens, gain, router, route, slot_rows):
    return pl.pallas_call(
        route_kernel,
        out_shape=(
            jax.ShapeDtypeStruct((128, 768), jnp.float32),
            jax.ShapeDtypeStruct((128, 128), jnp.float32),
            jax.ShapeDtypeStruct((4, 256, 768), jnp.bfloat16),
            jax.ShapeDtypeStruct((4, 256, 128), jnp.float32),
            jax.ShapeDtypeStruct((4, 192, 768), jnp.bfloat16),
        ),
        in_specs=[in_smem()] + [pl.BlockSpec(memory_space=pltpu.HBM)] * 11 + in_vmem(5),
        out_specs=tuple(in_vmem(5)),
        scratch_shapes=[
            pltpu.VMEM((512, 896), jnp.bfloat16),
            pltpu.VMEM((4, 128, 768), jnp.float32),
            pltpu.VMEM((4, 128, 128), jnp.float32),
            pltpu.VMEM((4, 512, 192), jnp.bfloat16),
            pltpu.VMEM((192, 768), jnp.bfloat16),
            pltpu.VMEM((6, 96, 768), jnp.bfloat16),
            pltpu.SemaphoreType.DMA((11,)),
        ],
        compiler_params=pltpu.CompilerParams(vmem_limit_bytes=SCOPED),
        cost_estimate=LIGHT,
        name="route",
    )(ids, *att, *parts, tokens, gain, router, route, slot_rows)


def slot_kernel(tiny_ref, route_ref, turned_ref, grad_ref, low_ref, rows_ref, slots_ref):
    route = route_ref[...]
    lane = lax.broadcasted_iota(jnp.int32, (512, 128), 1)
    choose = lane == route
    later = lax.broadcasted_iota(jnp.int32, (512, 512), 0)
    earlier = lax.broadcasted_iota(jnp.int32, (512, 512), 1)
    filled = jnp.dot(
        (later >= earlier).astype(jnp.float32).astype(jnp.bfloat16),
        choose.astype(jnp.float32).astype(jnp.bfloat16),
        preferred_element_type=jnp.float32,
    )
    index = jnp.sum(jnp.where(choose, filled, 0.0), axis=-1, keepdims=True).astype(jnp.int32) - 1
    target = route * 256 + index
    low_ref[...] = (
        (lax.broadcasted_iota(jnp.int32, (512, 1024), 1) == target)
        .astype(jnp.float32)
        .astype(jnp.bfloat16)
        .reshape(4, 128, 1024)
    )
    turned = turned_ref[...]
    choose = lax.broadcasted_iota(jnp.int32, (8, 512), 0) == turned
    filled = jnp.dot(
        choose.astype(jnp.float32).astype(jnp.bfloat16),
        (later <= earlier).astype(jnp.float32).astype(jnp.bfloat16),
        preferred_element_type=jnp.float32,
    )
    index = jnp.sum(jnp.where(choose, filled, 0.0), axis=0, keepdims=True).astype(jnp.int32) - 1
    target = turned * 256 + index
    rows = (
        (lax.broadcasted_iota(jnp.int32, (1024, 512), 0) == target)
        .astype(jnp.float32)
        .astype(jnp.bfloat16)
    )
    rows_ref[...] = rows
    slots_ref[...] = (
        jnp.dot(rows, grad_ref[...], preferred_element_type=jnp.float32)
        .astype(jnp.bfloat16)
        .reshape(4, 256, 768)
    )


def slot_call(tiny, route, grad):
    return pl.pallas_call(
        slot_kernel,
        out_shape=(
            jax.ShapeDtypeStruct((4, 128, 1024), jnp.bfloat16),
            jax.ShapeDtypeStruct((1024, 512), jnp.bfloat16),
            jax.ShapeDtypeStruct((4, 256, 768), jnp.bfloat16),
        ),
        in_specs=in_vmem(4),
        out_specs=tuple(in_vmem(3)),
        compiler_params=pltpu.CompilerParams(vmem_limit_bytes=SCOPED),
        cost_estimate=LIGHT,
        name="slots",
    )(tiny, route[:, None], route[None, :], grad)


def expert_kernel(*refs):
    ids_ref, sent_ref, grad_ref = refs[:3]
    in_refs, out_refs = refs[3:11], refs[11:19]
    pick_ref, home_refs = refs[19], refs[20:24]
    hidden_ref, grad_pre_ref, total_ref = refs[24:]
    plane = ids_ref[2]
    for expert in range(4):
        back = None
        inner = None
        for half in range(2):
            in_ref, out_ref = in_refs[2 * expert + half], out_refs[2 * expert + half]
            pre_act = jnp.dot(sent_ref[expert], in_ref[...], preferred_element_type=jnp.float32)
            grad_hidden = lax.dot_general(
                grad_ref[expert], out_ref[...], NT, preferred_element_type=jnp.float32
            )
            hidden, slope = gelu_parts(pre_act)
            hidden_ref[half, expert] = hidden.astype(jnp.bfloat16)
            grad_pre = (grad_hidden * slope).astype(jnp.bfloat16)
            grad_pre_ref[half, expert] = grad_pre
            part_inner = jnp.sum(hidden * grad_hidden, axis=-1, keepdims=True)
            part_back = lax.dot_general(
                grad_pre, in_ref[...], NT, preferred_element_type=jnp.float32
            )
            back = part_back if half == 0 else back + part_back
            inner = part_inner if half == 0 else inner + part_inner
        payload = jnp.concatenate([back.astype(jnp.bfloat16), split_column(inner)], axis=1)
        columns = slice(256 * expert, 256 * (expert + 1))
        picked = pick_ref[:, :, columns].reshape(512, 256)
        part = jnp.dot(picked, payload, preferred_element_type=jnp.float32)
        if expert == 0:
            total_ref[...] = part.reshape(4, 128, 896)
        else:
            total_ref[...] += part.reshape(4, 128, 896)
    for away in range(4):
        home_refs[away][...] = total_ref[plane ^ away].astype(jnp.bfloat16)


def expert_call(ids, sent, grad, weights_in, weights_out, slot_pick):
    return pl.pallas_call(
        expert_kernel,
        out_shape=(jax.ShapeDtypeStruct((128, 896), jnp.bfloat16),) * 4
        + (jax.ShapeDtypeStruct((2, 4, 256, 384), jnp.bfloat16),) * 2,
        in_specs=[in_smem()] + in_vmem(19),
        out_specs=tuple(in_vmem(6)),
        scratch_shapes=[pltpu.VMEM((4, 128, 896), jnp.float32)],
        compiler_params=pltpu.CompilerParams(vmem_limit_bytes=SCOPED),
        cost_estimate=LIGHT,
        name="experts",
    )(ids, sent, grad, *weights_in, *weights_out, slot_pick)


def weight_grad_kernel(*refs):
    ids_ref, sent_ref, grad_ref, gate_ref, hidden_ref, grad_pre_ref = refs[1:7]
    out_refs = refs[7:15]
    pick_ref = refs[15]
    out_grad_refs, in_grad_refs = refs[16:24], refs[24:32]
    home_refs, total_ref = refs[32:36], refs[36]
    plane = ids_ref[2]
    for expert in range(4):
        gate = gate_ref[expert][:, :1]
        rows = (grad_ref[expert].astype(jnp.float32) * gate).astype(jnp.bfloat16)
        for half in range(2):
            out_grad_refs[4 * half + expert][...] = lax.dot_general(
                hidden_ref[half, expert], rows, TN, preferred_element_type=jnp.float32
            ).astype(jnp.bfloat16)
    for expert in range(4):
        gate = gate_ref[expert][:, :1]
        part = None
        for half in range(2):
            grad_pre = (grad_pre_ref[half, expert].astype(jnp.float32) * gate).astype(jnp.bfloat16)
            in_grad_refs[4 * half + expert][...] = lax.dot_general(
                sent_ref[expert], grad_pre, TN, preferred_element_type=jnp.float32
            ).astype(jnp.bfloat16)
            product = jnp.dot(
                hidden_ref[half, expert],
                out_refs[2 * expert + half][...],
                preferred_element_type=jnp.float32,
            )
            part = product if half == 0 else part + product
        part = part.astype(jnp.bfloat16)
        columns = slice(256 * expert, 256 * (expert + 1))
        picked = pick_ref[:, :, columns].reshape(512, 256)
        placed = jnp.dot(picked, part, preferred_element_type=jnp.float32)
        if expert == 0:
            total_ref[...] = placed.reshape(4, 128, 768)
        else:
            total_ref[...] += placed.reshape(4, 128, 768)
    for away in range(4):
        home_refs[away][...] = total_ref[lax.rem(plane + away, 4)].astype(jnp.bfloat16)


def weight_grad_call(tiny, ids, sent, grad, gate, hidden, grad_pre, weights_out, slot_pick):
    return pl.pallas_call(
        weight_grad_kernel,
        out_shape=(jax.ShapeDtypeStruct((384, 768), jnp.bfloat16),) * 8
        + (jax.ShapeDtypeStruct((768, 384), jnp.bfloat16),) * 8
        + (jax.ShapeDtypeStruct((128, 768), jnp.bfloat16),) * 4,
        in_specs=in_vmem(1) + [in_smem()] + in_vmem(14),
        out_specs=tuple(in_vmem(20)),
        scratch_shapes=[pltpu.VMEM((4, 128, 768), jnp.float32)],
        compiler_params=pltpu.CompilerParams(vmem_limit_bytes=SCOPED),
        cost_estimate=LIGHT,
        name="weight_grads",
    )(tiny, ids, sent, grad, gate, hidden, grad_pre, *weights_out, slot_pick)


def project_back_kernel(ids_ref, *refs):
    grad_refs = refs[:4]
    weight_ref, token_ref, gain_two_ref, router_ref = refs[4:8]
    block_refs = refs[8:12]
    tiny_ref, low_ref, small_ref = refs[12:]
    chip = ids_ref[0]
    plane = ids_ref[2]
    gain = None
    for away in range(4):
        part = lax.dot_general(
            grad_refs[away][...], weight_ref[...], NT, preferred_element_type=jnp.float32
        )
        low_ref[chip ^ away] = part.astype(jnp.bfloat16)
        tokens = token_ref[chip ^ away].astype(jnp.float32)
        inverse = lax.rsqrt(jnp.mean(tokens * tokens, axis=-1, keepdims=True) + EPSILON)
        added = jnp.sum(part * tokens * inverse, axis=0, keepdims=True)
        gain = added if away == 0 else gain + added
    small_ref[...] = jnp.zeros_like(small_ref)
    small_ref[0:1, :] = gain
    small_ref[1:2, :] = gain_two_ref[...]
    small_ref[2:6, :] = router_ref[:4, :]
    small = small_ref[...]
    high = small.astype(jnp.bfloat16).astype(jnp.float32)
    rows = jnp.concatenate([high, small - high], axis=0).astype(jnp.bfloat16)
    for away, block_ref in enumerate(block_refs):
        block_ref[:128, :] = low_ref[lax.rem(plane + away, 4)]
        block_ref[128:, :] = rows
    tiny_ref[...] = low_ref[0, :16, :128]


def project_back_call(ids, grads, weight, tokens, gain_two, router):
    return pl.pallas_call(
        project_back_kernel,
        out_shape=(jax.ShapeDtypeStruct((144, 768), jnp.bfloat16),) * 4
        + (jax.ShapeDtypeStruct((16, 128), jnp.bfloat16),),
        in_specs=[in_smem()] + in_vmem(8),
        out_specs=tuple(in_vmem(5)),
        scratch_shapes=[
            pltpu.VMEM((4, 128, 768), jnp.bfloat16),
            pltpu.VMEM((8, 768), jnp.float32),
        ],
        compiler_params=pltpu.CompilerParams(vmem_limit_bytes=SCOPED),
        cost_estimate=LIGHT,
        name="project_back",
    )(ids, *grads, weight, tokens, gain_two, router)


def add_dense_kernel(ids_ref, kept_ref, *refs):
    arrived_refs, rel_ref, home_refs, total = refs[4:8], refs[8], refs[9:13], refs[13]
    chip = ids_ref[0]
    small = arrived_refs[0][128:, :].astype(jnp.float32)
    for at in range(1, 4):
        small = small + arrived_refs[at][128:, :].astype(jnp.float32)
    small = small[:8] + small[8:]
    for at in range(4):
        total[at] = kept_ref[at].astype(jnp.float32) + refs[at][...].astype(jnp.float32)
        total[at, 120:, :] = small
        total[at, 126:127, :] = rel_ref[...]
    for away in range(4):
        home_refs[away][...] = total[chip ^ away].astype(jnp.bfloat16)


def add_dense_call(ids, kept, theirs, arrived, rel):
    return pl.pallas_call(
        add_dense_kernel,
        out_shape=(jax.ShapeDtypeStruct((128, 768), jnp.bfloat16),) * 4,
        in_specs=[in_smem()] + in_vmem(10),
        out_specs=tuple(in_vmem(4)),
        scratch_shapes=[pltpu.VMEM((4, 128, 768), jnp.float32)],
        compiler_params=pltpu.CompilerParams(vmem_limit_bytes=SCOPED),
        cost_estimate=LIGHT,
        name="add_dense",
    )(ids, kept, *theirs, *arrived, rel)


def sum_dense_kernel(tiny_ref, *refs):
    total = refs[0][...].astype(jnp.float32)
    for at in range(1, 4):
        total = total + refs[at][...].astype(jnp.float32)
    refs[4][...] = total.astype(jnp.bfloat16)


def sum_dense_call(tiny, blocks):
    return pl.pallas_call(
        sum_dense_kernel,
        out_shape=jax.ShapeDtypeStruct((128, 768), jnp.bfloat16),
        in_specs=in_vmem(5),
        out_specs=in_vmem(1)[0],
        compiler_params=pltpu.CompilerParams(vmem_limit_bytes=SCOPED),
        cost_estimate=LIGHT,
        name="sum_dense",
    )(tiny, *blocks)


def pack_kernel(branch_ref, *refs):
    for at in range(3):
        refs[3 + at][:128, :] = refs[at][...]
        refs[3 + at][128:, :] = branch_ref[...]


def pack_call(branch, homes):
    return pl.pallas_call(
        pack_kernel,
        out_shape=(jax.ShapeDtypeStruct((256, 768), jnp.bfloat16),) * 3,
        in_specs=in_vmem(4),
        out_specs=tuple(in_vmem(3)),
        compiler_params=pltpu.CompilerParams(vmem_limit_bytes=SCOPED),
        cost_estimate=LIGHT,
        name="pack",
    )(branch, *homes)


def output_kernel(ids_ref, home_ref, *refs):
    plane = ids_ref[2]
    resid_ref, probs_ref, route_ref, out_ref = refs[3:]
    rows = home_ref[...].astype(jnp.float32)
    for at in range(3):
        rows = rows + refs[at][:128, :].astype(jnp.float32)
    lane = lax.broadcasted_iota(jnp.int32, (128, 128), 1)
    gate = jnp.sum(
        jnp.where(lane == route_ref[plane], probs_ref[...], 0.0), axis=-1, keepdims=True
    )
    out_ref[...] = (resid_ref[...] + gate * rows).astype(jnp.bfloat16)


def output_call(ids, home, packed, resid, probs, route):
    return pl.pallas_call(
        output_kernel,
        out_shape=jax.ShapeDtypeStruct((128, 768), jnp.bfloat16),
        in_specs=[in_smem()] + in_vmem(7),
        out_specs=in_vmem(1)[0],
        compiler_params=pltpu.CompilerParams(vmem_limit_bytes=SCOPED),
        cost_estimate=LIGHT,
        name="output",
    )(ids, home, *packed, resid, probs, route)


def finish_kernel(ids_ref, *refs):
    token_ref, gain_ref, grad_ref, out_ref = refs[4:8]
    ending_ref, tiny_ref = refs[9:]
    plane = ids_ref[2]
    gradient = refs[0][:128, :].astype(jnp.float32)
    for at in range(1, 4):
        gradient = gradient + refs[at][:128, :].astype(jnp.float32)
    tokens = token_ref[plane].astype(jnp.float32)
    inverse = lax.rsqrt(jnp.mean(tokens * tokens, axis=-1, keepdims=True) + EPSILON)
    weighted = gradient * gain_ref[...]
    inner = jnp.mean(weighted * tokens, axis=-1, keepdims=True)
    result = inverse * weighted - tokens * (inverse * inverse * inverse * inner) + grad_ref[...]
    ending = result.astype(jnp.bfloat16)
    ending_ref[:128, :] = ending
    ending_ref[128:, :] = out_ref[...]
    tiny_ref[...] = ending[:16, :128]


def finish_call(ids, arrived, tokens, gain, grad, out, ready):
    return pl.pallas_call(
        finish_kernel,
        out_shape=(
            jax.ShapeDtypeStruct((256, 768), jnp.bfloat16),
            jax.ShapeDtypeStruct((16, 128), jnp.bfloat16),
        ),
        in_specs=[in_smem()] + in_vmem(9),
        out_specs=tuple(in_vmem(2)),
        compiler_params=pltpu.CompilerParams(vmem_limit_bytes=SCOPED),
        cost_estimate=LIGHT,
        name="finish",
    )(ids, *arrived, tokens, gain, grad, out, ready)


def dense_grad_kernel(tiny_ref, ids_ref, *refs):
    grad_refs, att_ref, branch_refs = refs[:4], refs[4], refs[5:9]
    normed_ref, kept_ref = refs[9:11]
    sent_refs, total_ref = refs[11:15], refs[15]
    chip = ids_ref[0]
    core = ids_ref[1]
    plane = ids_ref[2]
    total = None
    for away in range(4):
        part = lax.dot_general(
            normed_ref[pl.ds(pl.multiple_of(128 * (chip ^ away), 128), 128), :],
            grad_refs[away][...],
            TN,
            preferred_element_type=jnp.float32,
        )
        total = part if away == 0 else total + part
    rows = None
    for away, branch_ref in enumerate(branch_refs):
        branch = branch_ref[...] if away == 0 else branch_ref[128:, :]
        part = lax.dot_general(
            att_ref[pl.ds(pl.multiple_of(128 * lax.rem(plane + 4 - away, 4), 128), 128), :],
            branch,
            TN,
            preferred_element_type=jnp.float32,
        )
        rows = part if away == 0 else rows + part
    total_ref[...] = jnp.zeros_like(total_ref)
    for half in range(2):
        for place in range(4):
            first = 384 * half + 96 * place
            total_ref[half, place, :96, :576] = total[first : first + 96]
            first = 96 * half + 24 * place
            total_ref[half, place, 96:120, :] = rows[first : first + 24]
    kept_ref[...] = total_ref[core].astype(jnp.bfloat16)
    for place in range(4):
        sent_refs[place][...] = total_ref[1 - core, place].astype(jnp.bfloat16)


def dense_grad_call(tiny, ids, grads, att, branches, normed):
    return pl.pallas_call(
        dense_grad_kernel,
        out_shape=(jax.ShapeDtypeStruct((4, 128, 768), jnp.bfloat16),)
        + (jax.ShapeDtypeStruct((128, 768), jnp.bfloat16),) * 4,
        in_specs=in_vmem(1) + [in_smem()] + in_vmem(10),
        out_specs=tuple(in_vmem(5)),
        scratch_shapes=[pltpu.VMEM((2, 4, 128, 768), jnp.float32)],
        compiler_params=pltpu.CompilerParams(vmem_limit_bytes=SCOPED),
        cost_estimate=LIGHT,
        name="dense_grads",
    )(tiny, ids, *grads, att, *branches, normed)


def tokens_kernel(ids_ref, *refs):
    grad_ref, all_ref = refs[4:]
    plane = ids_ref[2]
    for step in range(4):
        all_ref[lax.rem(plane + 4 - step, 4)] = refs[step][:128, :].astype(jnp.float32)
    for seq in range(4):
        grad_ref[:, seq, :] = all_ref[seq]


def tokens_call(ids, blocks):
    return pl.pallas_call(
        tokens_kernel,
        out_shape=jax.ShapeDtypeStruct((128, 4, 768), jnp.float32),
        in_specs=[in_smem()] + in_vmem(4),
        out_specs=in_vmem(1)[0],
        scratch_shapes=[pltpu.VMEM((4, 128, 768), jnp.float32)],
        compiler_params=pltpu.CompilerParams(vmem_limit_bytes=SCOPED),
        cost_estimate=LIGHT,
        name="tokens_back",
    )(ids, *blocks)


def add_pairs_kernel(*refs):
    blocks = refs[16:20]
    for at in range(4):
        total = refs[at][...].astype(jnp.float32) + refs[4 + at][...].astype(jnp.float32)
        blocks[at][:, :768] = total.astype(jnp.bfloat16)
        total = refs[8 + at][...].astype(jnp.float32) + refs[12 + at][...].astype(jnp.float32)
        blocks[at][:, 768:1152] = total[:384].astype(jnp.bfloat16)
        blocks[at][:, 1152:] = total[384:].astype(jnp.bfloat16)


def add_pairs_call(parts):
    return pl.pallas_call(
        add_pairs_kernel,
        out_shape=(jax.ShapeDtypeStruct((384, 1536), jnp.bfloat16),) * 4,
        in_specs=in_vmem(16),
        out_specs=tuple(in_vmem(4)),
        compiler_params=pltpu.CompilerParams(vmem_limit_bytes=SCOPED),
        cost_estimate=LIGHT,
        name="add_pairs",
    )(*parts)


def resid_back_kernel(
    ids_ref,
    home0_ref,
    home1_ref,
    home2_ref,
    home3_ref,
    resid_ref,
    probs_ref,
    route_ref,
    grad_ref,
    gain_ref,
    router_ref,
    out_weight_ref,
    grad_resid_ref,
    branch_ref,
    att0_ref,
    att1_ref,
    att2_ref,
    att3_ref,
    gain_grad_ref,
    router_grad_ref,
    all_ref,
):
    chip = ids_ref[0]
    plane = ids_ref[2]
    lane = lax.broadcasted_iota(jnp.int32, (128, 128), 1)
    collected = home0_ref[...].astype(jnp.float32)
    for home_ref in (home1_ref, home2_ref, home3_ref):
        collected = collected + home_ref[...].astype(jnp.float32)
    grad_gate = collected[:, 768:769] + collected[:, 769:770]
    probs = probs_ref[...]
    chosen = lane == route_ref[plane]
    gate = jnp.sum(jnp.where(chosen, probs, 0.0), axis=-1, keepdims=True)
    grad_sent = (collected[:, :768] * gate).astype(jnp.bfloat16).astype(jnp.float32)
    grad_logits = probs * (jnp.where(chosen, grad_gate, 0.0) - gate * grad_gate)
    resid = resid_ref[...]
    gain = gain_ref[...]
    inverse = lax.rsqrt(jnp.mean(resid * resid, axis=-1, keepdims=True) + EPSILON)
    unit = resid * inverse
    router_grad = lax.dot_general(
        grad_logits, unit * gain, TN, precision=PRECISE, preferred_element_type=jnp.float32
    )
    router_grad_ref[...] = router_grad[:8]
    grad_normed = grad_sent + lax.dot_general(
        grad_logits, router_ref[...], NT, precision=PRECISE, preferred_element_type=jnp.float32
    )
    gain_grad_ref[...] = jnp.sum(grad_normed * unit, axis=0, keepdims=True)
    weighted = grad_normed * gain
    inner = jnp.mean(weighted * resid, axis=-1, keepdims=True)
    grad_resid = inverse * weighted - unit * (inverse * inverse * inner)
    grad_resid = grad_resid + grad_ref[plane].astype(jnp.float32)
    grad_resid_ref[...] = grad_resid
    branch = grad_resid.astype(jnp.bfloat16)
    branch_ref[...] = branch
    for away in range(4):
        all_ref[plane ^ away] = lax.dot_general(
            branch, out_weight_ref[away], NT, preferred_element_type=jnp.float32
        ).astype(jnp.bfloat16)
    for away, att_ref in enumerate((att0_ref, att1_ref, att2_ref, att3_ref)):
        att_ref[...] = all_ref[chip ^ away]


def resid_back_call(ids, homes, resid, probs, route, grad, gain, router, out_weights):
    return pl.pallas_call(
        resid_back_kernel,
        out_shape=(
            jax.ShapeDtypeStruct((128, 768), jnp.float32),
            jax.ShapeDtypeStruct((128, 768), jnp.bfloat16),
        )
        + (jax.ShapeDtypeStruct((128, 192), jnp.bfloat16),) * 4
        + (
            jax.ShapeDtypeStruct((1, 768), jnp.float32),
            jax.ShapeDtypeStruct((8, 768), jnp.float32),
        ),
        in_specs=[in_smem()] + in_vmem(11),
        out_specs=tuple(in_vmem(8)),
        scratch_shapes=[pltpu.VMEM((4, 128, 192), jnp.bfloat16)],
        compiler_params=pltpu.CompilerParams(vmem_limit_bytes=SCOPED),
        cost_estimate=LIGHT,
        name="resid_back",
    )(ids, *homes, resid, probs, route, grad, gain, router, out_weights)


def pinned(first, *others):
    tied = lax.optimization_barrier((first,) + others)
    return tied


def gather_over_ctx(block, chip, core):
    gathered = jnp.stack([block] + [to_chip(block, away) for away in range(1, 4)])
    ordered = jnp.stack([pick(gathered, at ^ chip) for at in range(4)])
    both = jnp.stack([ordered, to_core(ordered)])
    whole = jnp.stack([pick(both, core), pick(both, 1 - core)])
    return whole.reshape((8,) + block.shape)


def local_planned(
    tokens,
    gain_one,
    qkv_weight,
    out_weight,
    rel_weight,
    gain_two,
    router_weight,
    expert_in,
    expert_out,
    routes,
    bucket_table,
    grad_out,
):
    row_count, seq_count, width = tokens.shape
    token_count = row_count * seq_count
    expert_count = router_weight.shape[1]
    capacity = 2 * token_count // expert_count
    slots = expert_count * capacity
    ctx_at = lax.axis_index("ctx")
    plane = lax.axis_index("wsh")
    chip = ctx_at // 2
    core = ctx_at % 2
    ids = jnp.stack([chip, core, plane]).astype(jnp.int32)

    def by_seq(values):
        return lax.optimization_barrier(jnp.swapaxes(values, 0, 1))

    token_blocks = by_seq(tokens)
    weight_qkv = jnp.concatenate(
        lax.optimization_barrier((qkv_weight[:, 1], qkv_weight[:, 2], qkv_weight[:, 0])), axis=1
    )
    normed_low, *projected = project_call(ids, token_blocks, gain_one[None], weight_qkv)
    in_one, in_two = to_chip(expert_in[0], 1), to_chip(expert_in[0], 2)
    half_rows = pick(out_weight.reshape(2, 96, width), core)
    weight_parts = plane_swap([half_rows] * 4)[1:]
    own = chip_swap(projected)
    route_blocks = by_seq(routes)
    grad_blocks = by_seq(grad_out)
    slot_blocks, slot_rows, grad_slots = slot_call(
        tiny_of(projected[0]),
        route_blocks.reshape(token_count) ^ chip,
        grad_blocks.reshape(token_count, width),
    )
    gain_row = gain_two[None]
    router_wide = jnp.pad(router_weight, ((0, 0), (0, 128 - expert_count)))
    *own, in_one, in_two, slot_blocks, slot_rows, grad_slots, router_wide = pinned(
        *own, in_one, in_two, slot_blocks, slot_rows, grad_slots, router_wide
    )
    own[3], weight_in, weight_out = pinned(own[3], expert_in[0], expert_out[0])
    out_one, out_two = to_chip(weight_out, 1), to_chip(weight_out, 2)
    other = [to_core(block) for block in own]

    bucket_pick = (
        bucket_table[:, None] == lax.iota(jnp.int32, rel_weight.shape[0])[None, :]
    ).astype(jnp.float32)
    head_table = jnp.dot(bucket_pick, rel_weight, precision=PRECISE).T
    line = bias_lines(head_table, core)
    *attended, prob, keyval, query = attend_call(ids, tiny_of(half_rows), own, other, line)
    attended[3], *weight_parts = pinned(attended[3], *weight_parts)
    weight_parts = [out_weight] + weight_parts + [to_core(part) for part in weight_parts]
    attended = chip_swap(attended)
    *attended, out_one, out_two = pinned(*attended, out_one, out_two)
    attended[3], late_in, late_out = pinned(attended[3], weight_in, weight_out)
    in_three, out_three = to_chip(late_in, 3), to_chip(late_out, 3)
    att_rows = gather_rows_call(ids, attended)
    att_planes = [att_rows] + [to_plane(att_rows, away) for away in range(1, 4)]
    weights_in, weights_out = [], []
    for block in (weight_in, in_one, in_two, in_three):
        weights_in += [block, to_core(block)]
    for block in (weight_out, out_one, out_two, out_three):
        weights_out += [block, to_core(block)]
    my_resid, my_probs, sent_slots, gate_slots, out_weights = route_call(
        ids, att_planes, weight_parts, token_blocks, gain_row, router_wide, route_blocks, slot_rows
    )
    *homes, hidden, grad_pre = expert_call(
        ids, sent_slots, grad_slots, weights_in, weights_out, slot_blocks
    )
    tiny = tiny_of(homes[0])
    homes = plane_swap(homes)

    weight_grads = weight_grad_call(
        tiny, ids, sent_slots, grad_slots, gate_slots, hidden, grad_pre, weights_out, slot_blocks
    )
    out_parts, in_parts, expert_homes = weight_grads[:8], weight_grads[8:16], weight_grads[16:]
    *homes, expert_one, expert_two = pinned(*homes, *expert_homes[:2])
    expert_homes = [expert_one, expert_two] + list(expert_homes[2:])
    my_grad_resid, my_branch, *att_grads, grad_gain_two, grad_router = resid_back_call(
        ids,
        homes,
        my_resid,
        my_probs,
        route_blocks,
        grad_blocks,
        gain_row,
        router_wide,
        out_weights,
    )
    att_grads[0], *parts = pinned(att_grads[0], *out_parts, *in_parts)
    near = add_pairs_call(
        parts[:4]
        + [to_core(part) for part in parts[4:8]]
        + parts[8:12]
        + [to_core(part) for part in parts[12:]]
    )
    grad_mixed = turn_swap(att_grads)
    packed = pack_call(my_branch, expert_homes[1:])
    rest = pinned(*grad_mixed, *near[1:], *packed)
    grad_mixed, (near_one, near_two, near_three) = rest[:4], rest[4:7]
    packed = plane_shift([None] + list(rest[7:10]))[1:]
    near_one, near_two = to_chip(near_one, 1), to_chip(near_two, 2)
    mine_back, theirs_back, lags, tiny = attend_back_call(ids, query, prob, keyval, grad_mixed)
    theirs_back, near_one, near_two, near_three, *packed = pinned(
        theirs_back, near_one, near_two, near_three, *packed
    )
    out = output_call(ids, expert_homes[0], packed, my_resid, my_probs, route_blocks)
    grad_projected = list(add_queries_call(ids, mine_back, to_core(theirs_back)))
    grad_projected = chip_swap(grad_projected)
    def spread_planes(block):
        return jnp.stack([block] + [to_plane(block, away) for away in range(1, 4)])

    def to_tokens(gathered):
        by_place = jnp.stack([pick(gathered, (plane - at) % 4) for at in range(4)])
        return jnp.swapaxes(lax.optimization_barrier(by_place), 0, 1)

    *grad_projected, near_three = pinned(*grad_projected, near_three)
    near_three = to_chip(near_three, 3)
    grad_rel = jnp.dot(bucket_pick.T, table_grad(lags, core), precision=PRECISE)
    rel_row = jnp.where(
        (lax.iota(jnp.int32, 4) == plane)[None, :, None], grad_rel[:, None, :], 0.0
    ).reshape(-1)
    rel_row = jnp.pad(rel_row, (0, width - rel_row.shape[0]))
    *partial, tiny = project_back_call(
        ids,
        grad_projected,
        weight_qkv,
        token_blocks,
        grad_gain_two,
        grad_router,
    )
    kept, *sent = dense_grad_call(
        to_core(tiny), ids, grad_projected, att_rows, [my_branch] + packed, normed_low
    )
    arrived = plane_shift(partial)
    *arrived, kept, sent_one, sent_two, sent_three, sent_four, near_three = pinned(
        *arrived, kept, *sent, near_three
    )
    weight_sum = 0.0
    for block in (near[0], near_one, near_two, near_three):
        weight_sum = weight_sum + block.astype(jnp.float32)
    grad_weight_out = weight_sum[None, :, :768]
    grad_weight_in = jnp.concatenate([weight_sum[:, 768:1152], weight_sum[:, 1152:]])[None]
    sent = [to_core(part) for part in (sent_one, sent_two, sent_three, sent_four)]
    dense = list(add_dense_call(ids, kept, sent, arrived, rel_row[None]))
    dense_own = dense[0]
    dense = chip_swap(dense)
    ending, tiny = finish_call(
        ids, arrived, token_blocks, gain_one[None], my_grad_resid, out, dense_own
    )
    ending = [ending] + [
        lax.ppermute(ending, "wsh", [(at, (at + step) % 4) for at in range(4)])
        for step in range(1, 4)
    ]
    summed = sum_dense_call(to_core(tiny), dense)
    gathered = chip_swap([summed] * 4)
    both = pinned(*ending, *gathered)
    ending, gathered = both[:4], both[4:]
    both = [gathered, [to_core(block) for block in gathered]]
    ordered = jnp.stack([jnp.stack(part) for part in both])
    ordered = jnp.stack([pick(ordered, core), pick(ordered, 1 - core)])
    ordered = jnp.stack([pick(jnp.swapaxes(ordered, 0, 1), at ^ chip) for at in range(4)], axis=1)
    summed = ordered.reshape(8, 128, width)
    small = summed[0, 120:].astype(jnp.float32) + summed[4, 120:].astype(jnp.float32)
    grad_out_all = summed[:, 96:120].astype(jnp.float32).reshape(192, width)
    grad_qkv = summed[:, :96, :576].astype(jnp.float32).reshape(width, 576)
    grad_qkv = jnp.stack([grad_qkv[:, 384:], grad_qkv[:, :192], grad_qkv[:, 192:384]], axis=1)
    out = to_tokens(jnp.stack([block[128:] for block in ending]))
    grad_tokens = tokens_call(ids, ending)
    rel_all = small[2 + expert_count][: 4 * grad_rel.size].reshape(-1, 4, grad_rel.shape[1])
    return (
        out,
        grad_tokens,
        small[0],
        grad_qkv,
        grad_out_all,
        pick(jnp.swapaxes(rel_all, 0, 1), plane),
        small[1],
        small[2 : 2 + expert_count].T,
        grad_weight_in,
        grad_weight_out,
    )


def solution(mesh):
    placed = (
        P("ctx", None, None),
        P(),
        P(None, None, "wsh"),
        P("wsh", None),
        P(None, "wsh"),
        P(),
        P(),
        P("ctx", None, "wsh"),
        P("ctx", "wsh", None),
        P("ctx", None, None),
        P(),
        P("ctx", None, None),
    )
    planned = mesh.shape['ctx'] == 8 and mesh.shape['wsh'] == 4
    return jax.shard_map(
        local_planned if planned else local,
        mesh=mesh,
        in_specs=placed,
        out_specs=(
            P("ctx", None, None),
            P("ctx", None, None),
            P(),
            P(None, None, "wsh"),
            P("wsh", None),
            P(None, "wsh"),
            P(),
            P(),
            P("ctx", None, "wsh"),
            P("ctx", "wsh", None),
        ),
        check_vma=False,
    )
```

```python
import functools

import jax
import jax.numpy as jnp
from jax import lax
from jax.experimental import pallas as pl
from jax.experimental.pallas import tpu as pltpu
from jax.sharding import PartitionSpec as P

HD = 64
MAXD = 128
BLK = 64


EPSILON = 1e-06
MASKED = -1e30
PRECISE = lax.Precision.HIGHEST


def norm_forward(values, gain_vec):
    inverse = lax.rsqrt(jnp.mean(values * values, axis=-1, keepdims=True) + EPSILON)
    return (values * inverse * gain_vec, inverse)


def norm_backward(values, inverse, gain_vec, gradient):
    weighted = gradient * gain_vec
    inner_mean = jnp.mean(weighted * values, axis=-1, keepdims=True)
    grad_values = inverse * weighted - values * inverse**3 * inner_mean
    grad_gain = jnp.sum(gradient * values * inverse, axis=0)
    return (grad_values, grad_gain)


def exact_gelu(values):
    return jax.nn.gelu(values, approximate=False)


def dealt_positions(first_row, row_total, devices):
    row_ids = first_row + lax.iota(jnp.int32, row_total)
    owner_dev = row_ids // (2 * BLK)
    within = row_ids % (2 * BLK)
    early_pos = owner_dev * BLK + within
    late_pos = (2 * devices - 1 - owner_dev) * BLK + within - BLK
    return jnp.where(within < BLK, early_pos, late_pos)


def block_size():
    return 512


def split_heads(packed, head_count):
    return packed.reshape(
        packed.shape[0], packed.shape[1], head_count, packed.shape[2] // head_count
    )


def run_bias(pos_query, pos_keys, head_table):
    span = 2 * BLK - 1
    starts_query = pos_query[::BLK]
    starts_keys = pos_keys[::BLK]
    query_runs = starts_query.shape[0]
    key_runs = starts_keys.shape[0]
    head_count = head_table.shape[0]
    offsets = lax.iota(jnp.int32, span) - (BLK - 1)
    distance = starts_query[:, None, None] - starts_keys[None, :, None] + offsets[None, None, :]
    clipped = jnp.clip(distance, 0, MAXD - 1)
    onehot = (clipped.reshape(-1)[:, None] == lax.iota(jnp.int32, MAXD)[None, :]).astype(
        jnp.float32
    )
    diag_values = jnp.dot(onehot, head_table.T, precision=PRECISE)
    diag_values = jnp.transpose(
        diag_values.reshape(query_runs, key_runs, span, head_count), (3, 0, 1, 2)
    )
    tiled = jnp.tile(diag_values, (1, 1, 1, BLK + 1))[..., : BLK * (span + 1)]
    tiled = tiled.reshape(head_count, query_runs, key_runs, BLK, span + 1)[..., :BLK][..., ::-1]
    bias = jnp.transpose(tiled, (1, 3, 0, 2, 4)).reshape(
        query_runs * BLK, head_count, key_runs * BLK
    )
    return (bias[:, None], onehot)


def score_block(query, key_heads, pos_query, pos_keys, head_table):
    raw_score = jnp.einsum(
        "qshd,kshd->qshk", query, key_heads, preferred_element_type=jnp.float32
    ) * HD ** (-0.5)
    distance = pos_query[:, None] - pos_keys[None, :]
    score_bias, onehot = run_bias(pos_query, pos_keys, head_table)
    score = jnp.where((distance >= 0)[:, None, None, :], raw_score + score_bias, MASKED)
    return (score, onehot)


def bias_grad(grad_score, onehot):
    span = 2 * BLK - 1
    summed = jnp.sum(grad_score.astype(jnp.float32), axis=1)
    query_rows, head_count, key_rows = summed.shape
    query_runs = query_rows // BLK
    key_runs = key_rows // BLK
    tiles = jnp.transpose(
        summed.reshape(query_runs, BLK, head_count, key_runs, BLK), (2, 0, 3, 1, 4)
    )[..., ::-1]
    widened = jnp.pad(tiles, ((0, 0), (0, 0), (0, 0), (0, 0), (0, span + 1 - BLK)))
    flat = widened.reshape(head_count, query_runs, key_runs, BLK * (span + 1))
    flat = jnp.pad(flat, ((0, 0), (0, 0), (0, 0), (0, (BLK + 1) * span - BLK * (span + 1))))
    diag_sums = jnp.sum(flat.reshape(head_count, query_runs, key_runs, BLK + 1, span), axis=3)
    diag_rows = jnp.transpose(diag_sums, (1, 2, 3, 0)).reshape(-1, head_count)
    return jnp.dot(onehot.T, diag_rows, precision=PRECISE)


def over_blocks(step_fn, carried, piece):
    piece_rows = piece[0].shape[0]
    step_rows = block_size()
    block_count = piece_rows // step_rows
    blocks = tuple(
        (member.reshape((block_count, step_rows) + member.shape[1:]) for member in piece)
    )
    firsts = step_rows * lax.iota(jnp.int32, block_count)

    def advance(carry_state, scan_item):
        return (step_fn(carry_state, scan_item[0], scan_item[1]), None)

    carried, _ = lax.scan(advance, carried, (blocks, firsts))
    return carried


def local(
    tokens,
    gain_one,
    qkv_weight,
    out_weight,
    rel_weight,
    gain_two,
    router_weight,
    expert_in,
    expert_out,
    routes,
    bucket_table,
    grad_out,
):
    ctx_count = lax.axis_size("ctx")
    row_count, seq_count, model_width = tokens.shape
    token_count = row_count * seq_count
    head_count = qkv_weight.shape[2] // HD
    head_width = head_count * HD
    score_scale = HD ** (-0.5)
    pos_query = dealt_positions(lax.axis_index("ctx") * row_count, row_count, ctx_count)
    token_rows = tokens.astype(jnp.float32).reshape(token_count, model_width)
    normed_one, inverse_one = norm_forward(token_rows, gain_one)
    normed_low = normed_one.astype(jnp.bfloat16)
    projected = jnp.einsum(
        "nd,dce->nce", normed_low, qkv_weight, preferred_element_type=jnp.float32
    ).astype(jnp.bfloat16)
    query_flat = projected[:, 0].reshape(row_count, seq_count, head_width)
    query = split_heads(query_flat, head_count)
    keyval = projected[:, 1:].reshape(row_count, seq_count, 2 * head_width)
    own_keys = split_heads(keyval[..., :head_width], head_count)
    own_values = split_heads(keyval[..., head_width:], head_count)
    bucket_pick = (
        bucket_table[:, None] == lax.iota(jnp.int32, rel_weight.shape[0])[None, :]
    ).astype(jnp.float32)
    head_table = jnp.dot(bucket_pick, rel_weight, precision=PRECISE).T

    def attend(carry_state, key_block, first_row):
        key_heads = split_heads(key_block[0][..., :head_width], head_count)
        value_heads = split_heads(key_block[0][..., head_width:], head_count)
        pos_keys = dealt_positions(first_row, key_heads.shape[0], ctx_count)
        score, _ = score_block(query, key_heads, pos_query, pos_keys, head_table)
        row_max, denominator, weighted = carry_state
        new_max = jnp.maximum(row_max, jnp.max(score, axis=-1))
        rescale = jnp.exp(row_max - new_max)
        weights = jnp.exp(score - new_max[..., None])
        denominator = rescale * denominator + jnp.sum(weights, axis=-1)
        weighted = rescale[..., None] * weighted + jnp.einsum(
            "qshk,kshd->qshd",
            weights.astype(jnp.bfloat16),
            value_heads,
            preferred_element_type=jnp.float32,
        )
        return (new_max, denominator, weighted)

    stat_shape = (row_count, seq_count, head_count)
    zero_heads = jnp.zeros((row_count, seq_count, head_count, HD), jnp.float32)
    initial = (
        jnp.full(stat_shape, MASKED, jnp.float32),
        jnp.zeros(stat_shape, jnp.float32),
        zero_heads,
    )
    row_max, denominator, weighted = over_blocks(
        attend, initial, (lax.all_gather(keyval, "ctx", axis=0, tiled=True),)
    )
    attended = weighted / denominator[..., None]
    log_total = row_max + jnp.log(denominator)
    attended_low = attended.reshape(token_count, head_width).astype(jnp.bfloat16)
    branch = lax.psum(
        jnp.dot(attended_low, out_weight, preferred_element_type=jnp.float32).astype(jnp.bfloat16),
        "wsh",
    ).astype(jnp.float32)
    resid = token_rows + branch
    normed_two, inverse_two = norm_forward(resid, gain_two)
    logits = jnp.dot(normed_two, router_weight, precision=PRECISE)
    shifted = jnp.exp(logits - jnp.max(logits, axis=-1, keepdims=True))
    gate_probs = shifted / jnp.sum(shifted, axis=-1, keepdims=True)
    expert_count = router_weight.shape[1]
    expert_ids = routes.reshape(token_count)
    choose = expert_ids[:, None] == lax.iota(jnp.int32, expert_count)[None, :]
    gate_value = jnp.sum(jnp.where(choose, gate_probs, 0.0), axis=1)
    lower_ones = (
        lax.iota(jnp.int32, token_count)[:, None] >= lax.iota(jnp.int32, token_count)[None, :]
    ).astype(jnp.bfloat16)
    filled = jnp.dot(
        lower_ones, choose.astype(jnp.bfloat16), preferred_element_type=jnp.float32
    ).astype(jnp.int32)
    slot_index = jnp.sum(jnp.where(choose, filled - 1, 0), axis=1)
    capacity = max(2, 2 * token_count // expert_count)
    target = expert_ids * capacity + slot_index
    slot_pick = target[:, None] == lax.iota(jnp.int32, expert_count * capacity)[None, :]
    slot_low = slot_pick.astype(jnp.bfloat16)
    slot_full = slot_pick.astype(jnp.float32)
    weight_in = expert_in[0]
    weight_out = expert_out[0]

    def spread(values):
        buffer = jnp.einsum(
            "nm,nd->md", slot_low, values, preferred_element_type=jnp.float32
        ).astype(jnp.bfloat16)
        doubled = jnp.broadcast_to(
            buffer.reshape(expert_count, 1, capacity, model_width),
            (expert_count, 2, capacity, model_width),
        )
        return doubled.reshape(2 * expert_count, capacity, model_width)

    def collect(returned):
        row_width = returned.shape[-1]
        paired = jnp.sum(returned.reshape(expert_count, 2, capacity, row_width), axis=1)
        return jnp.dot(
            slot_full, paired.reshape(expert_count * capacity, row_width), precision=PRECISE
        )

    arrived_rows = lax.all_to_all(
        spread(normed_two.astype(jnp.bfloat16)), "ctx", split_axis=0, concat_axis=0, tiled=True
    )
    flat_rows = arrived_rows.reshape(-1, model_width)
    pre_act = jnp.dot(flat_rows, weight_in, preferred_element_type=jnp.float32)
    hidden = exact_gelu(pre_act).astype(jnp.bfloat16)
    returned = lax.all_to_all(
        jnp.dot(hidden, weight_out, preferred_element_type=jnp.float32)
        .reshape(arrived_rows.shape)
        .astype(jnp.bfloat16),
        "ctx",
        split_axis=0,
        concat_axis=0,
        tiled=True,
    ).astype(jnp.float32)
    expert_rows = lax.psum(collect(returned).astype(jnp.bfloat16), "wsh").astype(jnp.float32)
    result = resid + gate_value[:, None] * expert_rows
    out = result.astype(jnp.bfloat16).reshape(row_count, seq_count, model_width)
    grad_rows_f = grad_out.astype(jnp.float32).reshape(token_count, model_width)
    grad_gate = jnp.sum(grad_rows_f * expert_rows, axis=1)
    grad_expert_rows = (gate_value[:, None] * grad_rows_f).astype(jnp.bfloat16)
    arrived_grad = lax.all_to_all(
        spread(grad_expert_rows), "ctx", split_axis=0, concat_axis=0, tiled=True
    )
    flat_rows = arrived_rows.reshape(-1, model_width)
    flat_grad = arrived_grad.reshape(-1, model_width)
    pre_act = jnp.dot(flat_rows, weight_in, preferred_element_type=jnp.float32)
    hidden, gelu_pull = jax.vjp(exact_gelu, pre_act)
    hidden_low = hidden.astype(jnp.bfloat16)
    grad_weight_out = jnp.einsum(
        "rf,rd->fd", hidden_low, flat_grad, preferred_element_type=jnp.float32
    )
    grad_hidden = jnp.einsum("rd,fd->rf", flat_grad, weight_out, preferred_element_type=jnp.float32)
    grad_pre = gelu_pull(grad_hidden)[0].astype(jnp.bfloat16)
    grad_weight_in = jnp.einsum(
        "rd,rf->df", flat_rows, grad_pre, preferred_element_type=jnp.float32
    )
    partial_back = jnp.einsum(
        "rf,df->rd", grad_pre, weight_in, preferred_element_type=jnp.float32
    ).reshape(arrived_rows.shape)
    returned_grad = lax.all_to_all(
        partial_back.astype(jnp.bfloat16), "ctx", split_axis=0, concat_axis=0, tiled=True
    ).astype(partial_back.dtype)
    grad_sent = lax.psum(collect(returned_grad).astype(jnp.bfloat16), "wsh").astype(jnp.float32)
    grad_sent = lax.optimization_barrier(grad_sent.astype(jnp.bfloat16)).astype(jnp.float32)
    grad_logits = gate_probs * (
        jnp.where(choose, grad_gate[:, None], 0.0) - (gate_value * grad_gate)[:, None]
    )
    grad_router = jnp.dot(normed_two.T, grad_logits, precision=PRECISE)
    grad_normed_two = grad_sent + jnp.dot(grad_logits, router_weight.T, precision=PRECISE)
    grad_resid, grad_gain_two = norm_backward(resid, inverse_two, gain_two, grad_normed_two)
    grad_resid = grad_resid + grad_rows_f
    grad_branch = grad_resid.astype(jnp.bfloat16)
    grad_out_rows = jnp.einsum(
        "nw,nd->wd", attended_low, grad_branch, preferred_element_type=jnp.float32
    )
    grad_att = jnp.einsum(
        "nd,wd->nw", grad_branch, out_weight, preferred_element_type=jnp.float32
    ).astype(jnp.bfloat16)
    grad_att_flat = grad_att.reshape(row_count, seq_count, head_width)
    grad_att_heads = split_heads(grad_att_flat, head_count)
    row_inner = jnp.sum(grad_att_heads.astype(jnp.float32) * attended, axis=-1)

    def query_grads(carry_state, key_block, first_row):
        key_heads = split_heads(key_block[0][..., :head_width], head_count)
        value_heads = split_heads(key_block[0][..., head_width:], head_count)
        pos_keys = dealt_positions(first_row, key_heads.shape[0], ctx_count)
        score, onehot = score_block(query, key_heads, pos_query, pos_keys, head_table)
        weights = jnp.exp(score - log_total[..., None])
        grad_weights = jnp.einsum(
            "qshd,kshd->qshk", grad_att_heads, value_heads, preferred_element_type=jnp.float32
        )
        grad_score = (weights * (grad_weights - row_inner[..., None])).astype(jnp.bfloat16)
        grad_query = (
            carry_state[0]
            + jnp.einsum(
                "qshk,kshd->qshd", grad_score, key_heads, preferred_element_type=jnp.float32
            )
            * score_scale
        )
        return (grad_query, carry_state[1] + bias_grad(grad_score, onehot))

    def key_grads(carry_state, query_block, first_row):
        query_heads = split_heads(query_block[0][..., :head_width], head_count)
        grad_heads = split_heads(query_block[0][..., head_width:], head_count)
        pos_rows = dealt_positions(first_row, query_heads.shape[0], ctx_count)
        score, _ = score_block(query_heads, own_keys, pos_rows, pos_query, head_table)
        weights = jnp.exp(score - query_block[1][..., None])
        grad_value = carry_state[1] + jnp.einsum(
            "qshk,qshd->kshd",
            weights.astype(jnp.bfloat16),
            grad_heads,
            preferred_element_type=jnp.float32,
        )
        grad_weights = jnp.einsum(
            "qshd,kshd->qshk", grad_heads, own_values, preferred_element_type=jnp.float32
        )
        grad_score = (weights * (grad_weights - query_block[2][..., None])).astype(jnp.bfloat16)
        grad_key = (
            carry_state[0]
            + jnp.einsum(
                "qshk,qshd->kshd", grad_score, query_heads, preferred_element_type=jnp.float32
            )
            * score_scale
        )
        return (grad_key, grad_value)

    packed = jnp.concatenate([query_flat, grad_att_flat], axis=-1)
    zero_table = jnp.zeros((MAXD, head_count), jnp.float32)
    grad_query, grad_table = over_blocks(
        query_grads, (zero_heads, zero_table), (lax.all_gather(keyval, "ctx", axis=0, tiled=True),)
    )
    grad_key, grad_value = over_blocks(
        key_grads,
        (zero_heads, zero_heads),
        (
            lax.all_gather(packed, "ctx", axis=0, tiled=True),
            lax.all_gather(log_total.astype(jnp.bfloat16), "ctx", axis=0, tiled=True).astype(
                jnp.float32
            ),
            lax.all_gather(row_inner.astype(jnp.bfloat16), "ctx", axis=0, tiled=True).astype(
                jnp.float32
            ),
        ),
    )
    grad_projected = jnp.stack(
        [member.reshape(token_count, head_width) for member in (grad_query, grad_key, grad_value)],
        axis=1,
    ).astype(jnp.bfloat16)
    grad_normed_one = lax.psum(
        jnp.einsum(
            "nce,dce->nd", grad_projected, qkv_weight, preferred_element_type=jnp.float32
        ).astype(jnp.bfloat16),
        "wsh",
    ).astype(jnp.float32)
    grad_qkv = jnp.einsum(
        "nd,nce->dce", normed_low, grad_projected, preferred_element_type=jnp.float32
    )
    grad_tokens, grad_gain_one = norm_backward(token_rows, inverse_one, gain_one, grad_normed_one)
    grad_tokens = grad_tokens + grad_resid
    grad_rel = jnp.dot(bucket_pick.T, grad_table, precision=PRECISE)
    summed_grads = lax.psum(
        (grad_qkv, grad_out_rows, grad_rel, grad_gain_one, grad_gain_two, grad_router), "ctx"
    )
    return (
        out,
        grad_tokens.reshape(row_count, seq_count, model_width),
        summed_grads[3],
        summed_grads[0],
        summed_grads[1],
        summed_grads[2],
        summed_grads[4],
        summed_grads[5],
        grad_weight_in[None],
        grad_weight_out[None],
    )


NT = (((1,), (1,)), ((), ()))
TN = (((0,), (0,)), ((), ()))
SCOPED = 16 * 1024 * 1024
LIGHT = pl.CostEstimate(flops=1_000_000, bytes_accessed=10_000, transcendentals=0)


def strip(step, side):
    width = 128 * (step + 1) if side == 0 else 128 * (8 - step)
    first = 0 if side == 0 else 128 * (step + 1)
    return (width, first)


def skewed(values, leftward):
    width = values.shape[1]
    row = lax.broadcasted_iota(jnp.int32, values.shape, 0)
    for bit in range(6):
        shift = width - (1 << bit) if leftward else 1 << bit
        moved = pltpu.roll(values, shift, 1)
        values = jnp.where((row & (1 << bit)) != 0, moved, values)
    return values


def attend_kernel(ids_ref, *refs):
    own_refs, other_refs, line_ref = refs[1:5], refs[5:9], refs[9]
    att_refs = refs[10:14]
    far_prob_ref, far_keyval_ref, far_query_ref = refs[14:17]
    bias_ref, own_ref, other_ref, all_ref, near_ref = refs[17:22]
    prob_ref, keyval_ref, query_ref, sems, out_sems = refs[22:]

    def prob_copy(step):
        return pltpu.make_async_copy(
            prob_ref.at[:, step], far_prob_ref.at[:, step], out_sems.at[step]
        )

    def other_copies():
        return (
            pltpu.make_async_copy(keyval_ref, far_keyval_ref, out_sems.at[4]),
            pltpu.make_async_copy(query_ref, far_query_ref, out_sems.at[5]),
        )

    chip = ids_ref[0]
    core = ids_ref[1]

    def gather_keys(parity):
        for place in range(16):
            owner = place if place < 8 else 15 - place
            half = 0 if place < 8 else BLK
            source = own_ref if owner % 2 == parity else other_ref
            keyval_ref[place * BLK : (place + 1) * BLK, :] = source[
                owner // 2, half : half + BLK, :
            ]

    @pl.when(pl.program_id(0) == 0)
    def _():
        fetch(list(own_refs) + list(other_refs), [near_ref.at[at] for at in range(8)], sems)
        for away in range(4):
            own_ref[chip ^ away] = near_ref[away, :, :384]
            other_ref[chip ^ away] = near_ref[4 + away, :, :384]
            query_ref[chip ^ away] = near_ref[away, :, 384:] * jnp.bfloat16(HD ** (-0.5))
        for head in range(3):
            for side in range(2):
                line = jnp.broadcast_to(line_ref[head, side : side + 1, :], (BLK, 512))
                bias_ref[head, side] = skewed(line, False)[:, 128:384]

        @pl.when(core == 0)
        def _():
            gather_keys(0)

        @pl.when(core == 1)
        def _():
            gather_keys(1)

        for copy in other_copies():
            copy.start()

    def attend_step(step):
        jobs = [(head, side) for side in range(2) for head in range(3)]
        scores = []
        for head, side in jobs:
            width, _ = strip(step, side)
            rows = slice(side * BLK, (side + 1) * BLK)
            query = query_ref[step, rows, HD * head : HD * (head + 1)]
            keys = keyval_ref[:width, HD * head : HD * (head + 1)]
            score = lax.dot_general(query, keys, NT, preferred_element_type=jnp.float32)
            near = min(width, 256)
            close = score[:, width - near :] + bias_ref[head, side, :, 256 - near :]
            if width > near:
                score = jnp.concatenate([score[:, : width - near], close], axis=1)
            else:
                score = close
            scores.append(score)
        tops = [jnp.max(score, axis=-1, keepdims=True) for score in scores]
        weights = [jnp.exp(score - top) for score, top in zip(scores, tops)]
        totals = [jnp.sum(weight, axis=-1, keepdims=True) for weight in weights]
        probs = [
            (weight * (1.0 / total)).astype(jnp.bfloat16)
            for weight, total in zip(weights, totals)
        ]
        for (head, side), prob in zip(jobs, probs):
            width, first = strip(step, side)
            prob_ref[head, step, :, first : first + width] = prob
        prob_copy(step).start()
        mixed = [
            jnp.dot(
                prob,
                keyval_ref[: prob.shape[1], 192 + HD * head : 192 + HD * (head + 1)],
                preferred_element_type=jnp.float32,
            ).astype(jnp.bfloat16)
            for (head, side), prob in zip(jobs, probs)
        ]
        for side in range(2):
            rows = slice(side * BLK, (side + 1) * BLK)
            all_ref[step, rows, :] = jnp.concatenate(
                mixed[3 * side : 3 * side + 3], axis=1
            )

    for step in range(4):
        pl.when(pl.program_id(0) == step)(functools.partial(attend_step, step))

    @pl.when(pl.program_id(0) == 3)
    def _():
        for away in range(4):
            att_refs[away][...] = all_ref[chip ^ away]
        for step in range(4):
            prob_copy(step).wait()
        for copy in other_copies():
            copy.wait()


def attend_back_kernel(ids_ref, *refs):
    far_query_ref, prob_ref, far_keyval_ref = refs[:3]
    grad_refs = refs[3:7]
    mine_ref, theirs_ref, lags_ref, tiny_ref, total_ref, near_ref, grad_ref = refs[7:14]
    query_ref, keyval_ref, sems = refs[14:]
    core = ids_ref[1]
    plane = ids_ref[2]

    @pl.when(pl.program_id(0) == 0)
    def _():
        total_ref[...] = jnp.zeros_like(total_ref)
        near_ref[...] = jnp.zeros_like(near_ref)
        fetch(
            list(grad_refs) + [far_query_ref, far_keyval_ref],
            [grad_ref.at[plane ^ away] for away in range(4)] + [query_ref, keyval_ref],
            sems,
        )

    def back_step(step):
        jobs = [(head, side) for side in range(2) for head in range(3)]
        queries, grads, probs, products = [], [], [], []
        for head, side in jobs:
            width, first = strip(step, side)
            rows = slice(side * BLK, (side + 1) * BLK)
            queries.append(query_ref[step, rows, HD * head : HD * (head + 1)])
            grad = grad_ref[step, rows, HD * head : HD * (head + 1)]
            grads.append(grad)
            values = keyval_ref[:width, 192 + HD * head : 192 + HD * (head + 1)]
            prob = prob_ref[head, 0, :, first : first + width]
            probs.append(prob)
            grad_prob = lax.dot_general(grad, values, NT, preferred_element_type=jnp.float32)
            products.append(prob.astype(jnp.float32) * grad_prob)
        inners = [jnp.sum(product, axis=-1, keepdims=True) for product in products]
        lows = [
            (product - prob.astype(jnp.float32) * inner).astype(jnp.bfloat16)
            for product, prob, inner in zip(products, probs, inners)
        ]
        dqs = [
            (
                jnp.dot(
                    low,
                    keyval_ref[: low.shape[1], HD * head : HD * (head + 1)],
                    preferred_element_type=jnp.float32,
                )
                * HD ** (-0.5)
            ).astype(jnp.bfloat16)
            for (head, side), low in zip(jobs, lows)
        ]
        for side in range(2):
            rows = slice(side * BLK, (side + 1) * BLK)
            width, _ = strip(step, side)
            mine_ref[step, rows, 384:] = jnp.concatenate(dqs[3 * side : 3 * side + 3], axis=1)
            parts = []
            for left, right in ((lows, queries), (probs, grads)):
                for head in range(3):
                    parts.append(
                        lax.dot_general(
                            left[3 * side + head],
                            right[3 * side + head],
                            TN,
                            preferred_element_type=jnp.float32,
                        )
                    )
            total_ref[:width, :] += jnp.concatenate(parts, axis=1)
        for (head, side), low in zip(jobs, lows):
            width, _ = strip(step, side)
            score = low.astype(jnp.float32)
            near_ref[head, 2 * side] += score[:, width - 128 :]
            if width >= 256:
                near_ref[head, 2 * side + 1] += score[:, width - 256 : width - 128]
            if width > 256:
                far = score[:, :128]
                for chunk in range(1, (width - 256) // 128):
                    far = far + score[:, 128 * chunk : 128 * (chunk + 1)]
                near_ref[head, 4] += far

    for step in range(4):
        pl.when(pl.program_id(0) == step)(functools.partial(back_step, step))

    def scatter_keys(parity):
        for place in range(16):
            owner = place if place < 8 else 15 - place
            half = 0 if place < 8 else BLK
            target = mine_ref if owner % 2 == parity else theirs_ref
            target[owner // 2, half : half + BLK, :384] = total_ref[
                place * BLK : (place + 1) * BLK, :
            ].astype(jnp.bfloat16)

    @pl.when(pl.program_id(0) == 3)
    def _():
        tiny_ref[...] = total_ref[:16, :128].astype(jnp.bfloat16)
        lags_ref[...] = jnp.zeros_like(lags_ref)
        for head in range(3):
            for kind in range(4):
                wide = jnp.concatenate(
                    [near_ref[head, kind], jnp.zeros((BLK, 128), jnp.float32)], axis=1
                )
                lags_ref[head, kind : kind + 1, :] = jnp.sum(
                    skewed(wide, True), axis=0, keepdims=True
                )
            lags_ref[head, 4:5, :128] = jnp.sum(near_ref[head, 4], axis=0, keepdims=True)

        @pl.when(core == 0)
        def _():
            scatter_keys(0)

        @pl.when(core == 1)
        def _():
            scatter_keys(1)


def whole(*shape):
    return pl.BlockSpec(shape, lambda at: (0,) * len(shape))


def in_hbm():
    return pl.BlockSpec(memory_space=pltpu.HBM)


def by_step():
    return pl.BlockSpec((3, 1, BLK, 1152), lambda at: (0, at, 0, 0))


def in_vmem(count):
    return [pl.BlockSpec(memory_space=pltpu.VMEM)] * count


def attend_call(ids, tiny, own, other, line):
    return pl.pallas_call(
        attend_kernel,
        grid=(4,),
        out_shape=(jax.ShapeDtypeStruct((128, 192), jnp.bfloat16),) * 4
        + (
            jax.ShapeDtypeStruct((3, 4, BLK, 1152), jnp.bfloat16),
            jax.ShapeDtypeStruct((1024, 384), jnp.bfloat16),
            jax.ShapeDtypeStruct((4, 128, 192), jnp.bfloat16),
        ),
        in_specs=[in_smem(), whole(16, 128)] + [in_hbm()] * 8 + [whole(3, 2, 512)],
        out_specs=(whole(128, 192),) * 4 + (in_hbm(),) * 3,
        scratch_shapes=[
            pltpu.VMEM((3, 2, BLK, 256), jnp.float32),
            pltpu.VMEM((4, 128, 384), jnp.bfloat16),
            pltpu.VMEM((4, 128, 384), jnp.bfloat16),
            pltpu.VMEM((4, 128, 192), jnp.bfloat16),
            pltpu.VMEM((8, 128, 576), jnp.bfloat16),
            pltpu.VMEM((3, 4, BLK, 1152), jnp.bfloat16),
            pltpu.VMEM((1024, 384), jnp.bfloat16),
            pltpu.VMEM((4, 128, 192), jnp.bfloat16),
            pltpu.SemaphoreType.DMA((8,)),
            pltpu.SemaphoreType.DMA((6,)),
        ],
        compiler_params=pltpu.CompilerParams(
            vmem_limit_bytes=SCOPED, dimension_semantics=("arbitrary",)
        ),
        cost_estimate=LIGHT,
        name="attend",
    )(ids, tiny, *own, *other, line)


def attend_back_call(ids, query, prob, keyval, grads):
    return pl.pallas_call(
        attend_back_kernel,
        grid=(4,),
        out_shape=(
            jax.ShapeDtypeStruct((4, 128, 576), jnp.bfloat16),
            jax.ShapeDtypeStruct((4, 128, 384), jnp.bfloat16),
            jax.ShapeDtypeStruct((3, 8, 256), jnp.float32),
            jax.ShapeDtypeStruct((16, 128), jnp.bfloat16),
        ),
        in_specs=[
            in_smem(),
            in_hbm(),
            by_step(),
            in_hbm(),
        ]
        + [in_hbm()] * 4,
        out_specs=(
            whole(4, 128, 576),
            whole(4, 128, 384),
            whole(3, 8, 256),
            whole(16, 128),
        ),
        scratch_shapes=[
            pltpu.VMEM((1024, 384), jnp.float32),
            pltpu.VMEM((3, 5, BLK, 128), jnp.float32),
            pltpu.VMEM((4, 128, 192), jnp.bfloat16),
            pltpu.VMEM((4, 128, 192), jnp.bfloat16),
            pltpu.VMEM((1024, 384), jnp.bfloat16),
            pltpu.SemaphoreType.DMA((6,)),
        ],
        compiler_params=pltpu.CompilerParams(
            vmem_limit_bytes=SCOPED, dimension_semantics=("arbitrary",)
        ),
        cost_estimate=LIGHT,
        name="attend_back",
    )(ids, query, prob, keyval, *grads)


def to_core(values):
    return lax.ppermute(values, "ctx", [(at, at ^ 1) for at in range(8)])


def to_chip(values, away):
    return lax.ppermute(values, "ctx", [(at, at ^ (2 * away)) for at in range(8)])


def to_plane(values, away):
    return lax.ppermute(values, "wsh", [(at, at ^ away) for at in range(4)])


def tiny_of(source):
    return to_core(source.reshape(-1, source.shape[-1])[:16, :128])


def chip_swap(blocks):
    return [blocks[0]] + [to_chip(blocks[away], away) for away in range(1, 4)]


def plane_shift(blocks):
    return [blocks[0]] + [
        lax.ppermute(blocks[step], "wsh", [(at, (at + step) % 4) for at in range(4)])
        for step in range(1, 4)
    ]


def plane_swap(blocks):
    return [blocks[0]] + [to_plane(blocks[away], away) for away in range(1, 4)]


def seat(chip, core, plane):
    return (2 * chip + core) * 4 + plane


def turn_swap(blocks):
    return [
        lax.ppermute(
            block,
            ("ctx", "wsh"),
            [
                (seat(chip, core, plane), seat(plane, core, chip ^ away))
                for chip in range(4)
                for core in range(2)
                for plane in range(4)
            ],
        )
        for away, block in enumerate(blocks)
    ]


def pick(blocks, at):
    return lax.dynamic_index_in_dim(blocks, at, 0, keepdims=False)


def bias_lines(head_table, core):
    shifted = head_table - head_table[:, MAXD - 1 :]
    turned = shifted[:, ::-1]

    def line(zeros):
        return jnp.pad(
            jnp.pad(turned, ((0, 0), (zeros, 0))),
            ((0, 0), (0, 512 - MAXD - zeros)),
            constant_values=MASKED,
        )

    even, odd = line(129), line(193)
    return jnp.where(
        core == 0, jnp.stack([even, odd], axis=1), jnp.stack([odd, even], axis=1)
    )


def table_grad(lags, core):
    offsets = lax.iota(jnp.int32, 256)
    offsets = jnp.where(offsets < 128, offsets, offsets - 256)
    base = BLK * jnp.stack([core, core + 2, 1 - core, 3 - core])
    clipped = jnp.clip(base[:, None] - offsets[None, :], 0, MAXD - 1)
    onehot = (clipped[..., None] == lax.iota(jnp.int32, MAXD)).astype(jnp.float32)
    table = jnp.einsum("hkz,kzd->dh", lags[:, :4], onehot, precision=PRECISE)
    last = (lax.iota(jnp.int32, MAXD) == MAXD - 1).astype(jnp.float32)
    return table + last[:, None] * jnp.sum(lags[:, 4], axis=-1)


def gelu_parts(values):
    cdf = 0.5 * (1.0 + lax.erf(values * (0.5**0.5)))
    density = jnp.exp(-0.5 * values * values) * ((0.5 / jnp.pi) ** 0.5)
    return (values * cdf, cdf + values * density)


def in_smem():
    return pl.BlockSpec(memory_space=pltpu.SMEM)


def split_column(column):
    high = column.astype(jnp.bfloat16)
    low = (column - high.astype(jnp.float32)).astype(jnp.bfloat16)
    lane = lax.broadcasted_iota(jnp.int32, (column.shape[0], 128), 1)
    wide = jnp.where(
        lane == 0,
        high.astype(jnp.float32),
        jnp.where(lane == 1, low.astype(jnp.float32), 0.0),
    )
    return wide.astype(jnp.bfloat16)


def project_kernel(ids_ref, token_ref, gain_ref, weight_ref, turn_ref, *refs):
    normed_ref, rows_ref, refs = refs[0], refs[1], refs[2:]
    for seq in range(4):
        rows_ref[seq] = turn_ref[:, seq, :]
    chip = ids_ref[0]
    tokens = token_ref[...].reshape(512, 768).astype(jnp.float32)
    inverse = lax.rsqrt(jnp.mean(tokens * tokens, axis=-1, keepdims=True) + EPSILON)
    normed = (tokens * inverse * gain_ref[...]).astype(jnp.bfloat16)
    normed_ref[...] = normed
    projected = jnp.dot(normed, weight_ref[...], preferred_element_type=jnp.float32)
    refs[4][...] = projected.astype(jnp.bfloat16).reshape(4, 128, 576)
    for away in range(4):
        refs[away][...] = refs[4][chip ^ away]


def project_call(ids, tokens, gain, weight, grad):
    return pl.pallas_call(
        project_kernel,
        out_shape=(
            jax.ShapeDtypeStruct((512, 768), jnp.bfloat16),
            jax.ShapeDtypeStruct((4, 128, 768), jnp.bfloat16),
        )
        + (jax.ShapeDtypeStruct((128, 576), jnp.bfloat16),) * 4,
        in_specs=[in_smem()] + in_vmem(4),
        out_specs=tuple(in_vmem(6)),
        scratch_shapes=[pltpu.VMEM((4, 128, 576), jnp.bfloat16)],
        compiler_params=pltpu.CompilerParams(vmem_limit_bytes=SCOPED),
        cost_estimate=LIGHT,
        name="project",
    )(ids, tokens, gain, weight, grad)


def gather_rows_kernel(ids_ref, *refs):
    chip = ids_ref[0]
    for away in range(4):
        refs[4][pl.ds(pl.multiple_of(128 * (chip ^ away), 128), 128), :] = refs[away][...]


def gather_rows_call(ids, blocks):
    return pl.pallas_call(
        gather_rows_kernel,
        out_shape=jax.ShapeDtypeStruct((512, 192), jnp.bfloat16),
        in_specs=[in_smem()] + in_vmem(4),
        out_specs=in_vmem(1)[0],
        compiler_params=pltpu.CompilerParams(vmem_limit_bytes=SCOPED),
        cost_estimate=LIGHT,
        name="gather_rows",
    )(ids, *blocks)


def add_queries_kernel(ids_ref, mine_ref, theirs_ref, *sum_refs):
    chip = ids_ref[0]
    for away, sum_ref in enumerate(sum_refs):
        mine = mine_ref[chip ^ away]
        total = mine[:, :384].astype(jnp.float32) + theirs_ref[chip ^ away].astype(jnp.float32)
        sum_ref[:, :384] = total.astype(jnp.bfloat16)
        sum_ref[:, 384:] = mine[:, 384:]


def add_queries_call(ids, mine, theirs):
    return pl.pallas_call(
        add_queries_kernel,
        out_shape=(jax.ShapeDtypeStruct((128, 576), jnp.bfloat16),) * 4,
        in_specs=[in_smem()] + in_vmem(2),
        out_specs=tuple(in_vmem(4)),
        compiler_params=pltpu.CompilerParams(vmem_limit_bytes=SCOPED),
        cost_estimate=LIGHT,
        name="add_queries",
    )(ids, mine, theirs)


def fetch(sources, targets, sems):
    copies = [
        pltpu.make_async_copy(source, target, sems.at[at])
        for at, (source, target) in enumerate(zip(sources, targets))
    ]
    for copy in copies:
        copy.start()
    for copy in copies:
        copy.wait()


def route_kernel(*refs):
    ids_ref = refs[0]
    att_refs, part_refs = refs[1:5], refs[5:12]
    token_ref, gain_ref, router_ref, route_ref, slot_ref = refs[12:17]
    resid_ref, probs_ref, sent_ref, gate_ref, out_weight_ref = refs[17:22]
    payload_ref, branch_ref, all_probs_ref, att_ref, own_ref, half_ref, sems = refs[22:]
    fetch(
        list(att_refs) + list(part_refs),
        [att_ref.at[at] for at in range(4)] + [own_ref] + [half_ref.at[at] for at in range(6)],
        sems,
    )
    att_refs = [att_ref.at[at] for at in range(4)]
    part_refs = [own_ref] + [half_ref.at[at] for at in range(6)]
    core = ids_ref[1]
    plane = ids_ref[2]
    out_weight_ref[0] = part_refs[0][...]
    own_rows = pl.ds(pl.multiple_of(96 * core, 32), 96)
    other_rows = pl.ds(pl.multiple_of(96 - 96 * core, 32), 96)
    for away in range(1, 4):
        out_weight_ref[away, own_rows, :] = part_refs[away][...]
        out_weight_ref[away, other_rows, :] = part_refs[3 + away][...]
    branch = token_ref[...].reshape(512, 768).astype(jnp.float32)
    for away, att_ref in enumerate(att_refs):
        branch = branch + jnp.dot(
            att_ref[...], out_weight_ref[away], preferred_element_type=jnp.float32
        )
    branch_ref[...] = branch.reshape(4, 128, 768)
    inverse = lax.rsqrt(jnp.mean(branch * branch, axis=-1, keepdims=True) + EPSILON)
    normed = branch * inverse * gain_ref[...]
    payload_ref[:, :768] = normed.astype(jnp.bfloat16)
    router = jnp.concatenate([router_ref[...], jnp.zeros((124, 768), jnp.float32)], axis=0)
    logits = lax.dot_general(
        normed, router, NT, precision=PRECISE, preferred_element_type=jnp.float32
    )
    lane = lax.broadcasted_iota(jnp.int32, (512, 128), 1)
    logits = jnp.where(lane < 4, logits, MASKED)
    shifted = jnp.exp(logits - jnp.max(logits, axis=-1, keepdims=True))
    probs = shifted / jnp.sum(shifted, axis=-1, keepdims=True)
    all_probs_ref[...] = probs.reshape(4, 128, 128)
    gate = jnp.sum(
        jnp.where(lane == route_ref[...].reshape(512, 1), probs, 0.0), axis=-1, keepdims=True
    )
    payload_ref[:, 768:] = split_column(gate)
    resid_ref[...] = branch_ref[plane]
    probs_ref[...] = all_probs_ref[plane]
    placed = jnp.dot(slot_ref[...], payload_ref[...], preferred_element_type=jnp.float32)
    sent_ref[...] = placed[:, :768].astype(jnp.bfloat16).reshape(4, 256, 768)
    gate_ref[...] = jnp.broadcast_to(
        placed[:, 768:769] + placed[:, 769:770], (1024, 128)
    ).reshape(4, 256, 128)


def route_call(ids, att, parts, tokens, gain, router, route, slot_rows):
    return pl.pallas_call(
        route_kernel,
        out_shape=(
            jax.ShapeDtypeStruct((128, 768), jnp.float32),
            jax.ShapeDtypeStruct((128, 128), jnp.float32),
            jax.ShapeDtypeStruct((4, 256, 768), jnp.bfloat16),
            jax.ShapeDtypeStruct((4, 256, 128), jnp.float32),
            jax.ShapeDtypeStruct((4, 192, 768), jnp.bfloat16),
        ),
        in_specs=[in_smem()] + [pl.BlockSpec(memory_space=pltpu.HBM)] * 11 + in_vmem(5),
        out_specs=tuple(in_vmem(5)),
        scratch_shapes=[
            pltpu.VMEM((512, 896), jnp.bfloat16),
            pltpu.VMEM((4, 128, 768), jnp.float32),
            pltpu.VMEM((4, 128, 128), jnp.float32),
            pltpu.VMEM((4, 512, 192), jnp.bfloat16),
            pltpu.VMEM((192, 768), jnp.bfloat16),
            pltpu.VMEM((6, 96, 768), jnp.bfloat16),
            pltpu.SemaphoreType.DMA((11,)),
        ],
        compiler_params=pltpu.CompilerParams(vmem_limit_bytes=SCOPED),
        cost_estimate=LIGHT,
        name="route",
    )(ids, *att, *parts, tokens, gain, router, route, slot_rows)


def slot_kernel(tiny_ref, route_ref, turned_ref, grad_ref, low_ref, rows_ref, slots_ref):
    route = route_ref[...]
    lane = lax.broadcasted_iota(jnp.int32, (512, 128), 1)
    choose = lane == route
    later = lax.broadcasted_iota(jnp.int32, (512, 512), 0)
    earlier = lax.broadcasted_iota(jnp.int32, (512, 512), 1)
    filled = jnp.dot(
        (later >= earlier).astype(jnp.float32).astype(jnp.bfloat16),
        choose.astype(jnp.float32).astype(jnp.bfloat16),
        preferred_element_type=jnp.float32,
    )
    index = jnp.sum(jnp.where(choose, filled, 0.0), axis=-1, keepdims=True).astype(jnp.int32) - 1
    target = route * 256 + index
    low_ref[...] = (
        (lax.broadcasted_iota(jnp.int32, (512, 1024), 1) == target)
        .astype(jnp.float32)
        .astype(jnp.bfloat16)
        .reshape(4, 128, 1024)
    )
    turned = turned_ref[...]
    choose = lax.broadcasted_iota(jnp.int32, (8, 512), 0) == turned
    filled = jnp.dot(
        choose.astype(jnp.float32).astype(jnp.bfloat16),
        (later <= earlier).astype(jnp.float32).astype(jnp.bfloat16),
        preferred_element_type=jnp.float32,
    )
    index = jnp.sum(jnp.where(choose, filled, 0.0), axis=0, keepdims=True).astype(jnp.int32) - 1
    target = turned * 256 + index
    rows = (
        (lax.broadcasted_iota(jnp.int32, (1024, 512), 0) == target)
        .astype(jnp.float32)
        .astype(jnp.bfloat16)
    )
    rows_ref[...] = rows
    slots_ref[...] = (
        jnp.dot(rows, grad_ref[...], preferred_element_type=jnp.float32)
        .astype(jnp.bfloat16)
        .reshape(4, 256, 768)
    )


def slot_call(tiny, route, grad):
    return pl.pallas_call(
        slot_kernel,
        out_shape=(
            jax.ShapeDtypeStruct((4, 128, 1024), jnp.bfloat16),
            jax.ShapeDtypeStruct((1024, 512), jnp.bfloat16),
            jax.ShapeDtypeStruct((4, 256, 768), jnp.bfloat16),
        ),
        in_specs=in_vmem(4),
        out_specs=tuple(in_vmem(3)),
        compiler_params=pltpu.CompilerParams(vmem_limit_bytes=SCOPED),
        cost_estimate=LIGHT,
        name="slots",
    )(tiny, route[:, None], route[None, :], grad)


def expert_kernel(*refs):
    ids_ref, sent_ref, grad_ref = refs[:3]
    in_refs, out_refs = refs[3:11], refs[11:19]
    pick_ref, home_refs = refs[19], refs[20:24]
    hidden_ref, grad_pre_ref, total_ref = refs[24:]
    plane = ids_ref[2]
    for expert in range(4):
        back = None
        inner = None
        for half in range(2):
            in_ref, out_ref = in_refs[2 * expert + half], out_refs[2 * expert + half]
            pre_act = jnp.dot(sent_ref[expert], in_ref[...], preferred_element_type=jnp.float32)
            grad_hidden = lax.dot_general(
                grad_ref[expert], out_ref[...], NT, preferred_element_type=jnp.float32
            )
            hidden, slope = gelu_parts(pre_act)
            hidden_ref[half, expert] = hidden.astype(jnp.bfloat16)
            grad_pre = (grad_hidden * slope).astype(jnp.bfloat16)
            grad_pre_ref[half, expert] = grad_pre
            part_inner = jnp.sum(hidden * grad_hidden, axis=-1, keepdims=True)
            part_back = lax.dot_general(
                grad_pre, in_ref[...], NT, preferred_element_type=jnp.float32
            )
            back = part_back if half == 0 else back + part_back
            inner = part_inner if half == 0 else inner + part_inner
        payload = jnp.concatenate([back.astype(jnp.bfloat16), split_column(inner)], axis=1)
        columns = slice(256 * expert, 256 * (expert + 1))
        picked = pick_ref[:, :, columns].reshape(512, 256)
        part = jnp.dot(picked, payload, preferred_element_type=jnp.float32)
        if expert == 0:
            total_ref[...] = part.reshape(4, 128, 896)
        else:
            total_ref[...] += part.reshape(4, 128, 896)
    for away in range(4):
        home_refs[away][...] = total_ref[plane ^ away].astype(jnp.bfloat16)


def expert_call(ids, sent, grad, weights_in, weights_out, slot_pick):
    return pl.pallas_call(
        expert_kernel,
        out_shape=(jax.ShapeDtypeStruct((128, 896), jnp.bfloat16),) * 4
        + (jax.ShapeDtypeStruct((2, 4, 256, 384), jnp.bfloat16),) * 2,
        in_specs=[in_smem()] + in_vmem(19),
        out_specs=tuple(in_vmem(6)),
        scratch_shapes=[pltpu.VMEM((4, 128, 896), jnp.float32)],
        compiler_params=pltpu.CompilerParams(vmem_limit_bytes=SCOPED),
        cost_estimate=LIGHT,
        name="experts",
    )(ids, sent, grad, *weights_in, *weights_out, slot_pick)


def weight_grad_kernel(*refs):
    ids_ref, sent_ref, grad_ref, gate_ref, hidden_ref, grad_pre_ref = refs[1:7]
    out_refs = refs[7:15]
    pick_ref = refs[15]
    grad_refs = refs[16:24]
    home_refs, total_ref = refs[24:28], refs[28]
    plane = ids_ref[2]
    for expert in range(4):
        gate = gate_ref[expert][:, :1]
        rows = (grad_ref[expert].astype(jnp.float32) * gate).astype(jnp.bfloat16)
        for half in range(2):
            grad_refs[4 * half + expert][:, :768] = lax.dot_general(
                hidden_ref[half, expert], rows, TN, preferred_element_type=jnp.float32
            ).astype(jnp.bfloat16)
    for expert in range(4):
        gate = gate_ref[expert][:, :1]
        part = None
        for half in range(2):
            grad_pre = (grad_pre_ref[half, expert].astype(jnp.float32) * gate).astype(jnp.bfloat16)
            in_grad = lax.dot_general(
                sent_ref[expert], grad_pre, TN, preferred_element_type=jnp.float32
            ).astype(jnp.bfloat16)
            grad_refs[4 * half + expert][:, 768:1152] = in_grad[:384]
            grad_refs[4 * half + expert][:, 1152:] = in_grad[384:]
            product = jnp.dot(
                hidden_ref[half, expert],
                out_refs[2 * expert + half][...],
                preferred_element_type=jnp.float32,
            )
            part = product if half == 0 else part + product
        part = part.astype(jnp.bfloat16)
        columns = slice(256 * expert, 256 * (expert + 1))
        picked = pick_ref[:, :, columns].reshape(512, 256)
        placed = jnp.dot(picked, part, preferred_element_type=jnp.float32)
        if expert == 0:
            total_ref[...] = placed.reshape(4, 128, 768)
        else:
            total_ref[...] += placed.reshape(4, 128, 768)
    for away in range(4):
        home_refs[away][...] = total_ref[lax.rem(plane + away, 4)].astype(jnp.bfloat16)


def weight_grad_call(tiny, ids, sent, grad, gate, hidden, grad_pre, weights_out, slot_pick):
    return pl.pallas_call(
        weight_grad_kernel,
        out_shape=(jax.ShapeDtypeStruct((384, 1536), jnp.bfloat16),) * 8
        + (jax.ShapeDtypeStruct((128, 768), jnp.bfloat16),) * 4,
        in_specs=in_vmem(1) + [in_smem()] + in_vmem(14),
        out_specs=tuple(in_vmem(12)),
        scratch_shapes=[pltpu.VMEM((4, 128, 768), jnp.float32)],
        compiler_params=pltpu.CompilerParams(vmem_limit_bytes=SCOPED),
        cost_estimate=LIGHT,
        name="weight_grads",
    )(tiny, ids, sent, grad, gate, hidden, grad_pre, *weights_out, slot_pick)


def project_back_kernel(ids_ref, *refs):
    grad_refs = refs[:4]
    weight_ref, token_ref, gain_two_ref, router_ref = refs[4:8]
    block_refs = refs[8:12]
    tiny_ref, low_ref, small_ref = refs[12:]
    chip = ids_ref[0]
    plane = ids_ref[2]
    gain = None
    for away in range(4):
        part = lax.dot_general(
            grad_refs[away][...], weight_ref[...], NT, preferred_element_type=jnp.float32
        )
        low_ref[chip ^ away] = part.astype(jnp.bfloat16)
        tokens = token_ref[chip ^ away].astype(jnp.float32)
        inverse = lax.rsqrt(jnp.mean(tokens * tokens, axis=-1, keepdims=True) + EPSILON)
        added = jnp.sum(part * tokens * inverse, axis=0, keepdims=True)
        gain = added if away == 0 else gain + added
    small_ref[...] = jnp.zeros_like(small_ref)
    small_ref[0:1, :] = gain
    small_ref[1:2, :] = gain_two_ref[...]
    small_ref[2:6, :] = router_ref[:4, :]
    small = small_ref[...]
    high = small.astype(jnp.bfloat16).astype(jnp.float32)
    rows = jnp.concatenate([high, small - high], axis=0).astype(jnp.bfloat16)
    for away, block_ref in enumerate(block_refs):
        block_ref[:128, :] = low_ref[lax.rem(plane + away, 4)]
        block_ref[128:, :] = rows
    tiny_ref[...] = low_ref[0, :16, :128]


def project_back_call(ids, grads, weight, tokens, gain_two, router):
    return pl.pallas_call(
        project_back_kernel,
        out_shape=(jax.ShapeDtypeStruct((144, 768), jnp.bfloat16),) * 4
        + (jax.ShapeDtypeStruct((16, 128), jnp.bfloat16),),
        in_specs=[in_smem()] + in_vmem(8),
        out_specs=tuple(in_vmem(5)),
        scratch_shapes=[
            pltpu.VMEM((4, 128, 768), jnp.bfloat16),
            pltpu.VMEM((8, 768), jnp.float32),
        ],
        compiler_params=pltpu.CompilerParams(vmem_limit_bytes=SCOPED),
        cost_estimate=LIGHT,
        name="project_back",
    )(ids, *grads, weight, tokens, gain_two, router)


def add_dense_kernel(ids_ref, kept_ref, *refs):
    arrived_refs, rel_ref, home_refs, total = refs[4:8], refs[8], refs[9:13], refs[13]
    chip = ids_ref[0]
    small = arrived_refs[0][128:, :].astype(jnp.float32)
    for at in range(1, 4):
        small = small + arrived_refs[at][128:, :].astype(jnp.float32)
    small = small[:8] + small[8:]
    for at in range(4):
        total[at] = kept_ref[at].astype(jnp.float32) + refs[at][...].astype(jnp.float32)
        total[at, 120:, :] = small
        total[at, 126:127, :] = rel_ref[...]
    for away in range(4):
        home_refs[away][...] = total[chip ^ away].astype(jnp.bfloat16)


def add_dense_call(ids, kept, theirs, arrived, rel):
    return pl.pallas_call(
        add_dense_kernel,
        out_shape=(jax.ShapeDtypeStruct((128, 768), jnp.bfloat16),) * 4,
        in_specs=[in_smem()] + in_vmem(10),
        out_specs=tuple(in_vmem(4)),
        scratch_shapes=[pltpu.VMEM((4, 128, 768), jnp.float32)],
        compiler_params=pltpu.CompilerParams(vmem_limit_bytes=SCOPED),
        cost_estimate=LIGHT,
        name="add_dense",
    )(ids, kept, *theirs, *arrived, rel)


def sum_dense_kernel(tiny_ref, *refs):
    total = refs[0][...].astype(jnp.float32)
    for at in range(1, 4):
        total = total + refs[at][...].astype(jnp.float32)
    refs[4][...] = total.astype(jnp.bfloat16)


def sum_dense_call(tiny, blocks):
    return pl.pallas_call(
        sum_dense_kernel,
        out_shape=jax.ShapeDtypeStruct((128, 768), jnp.bfloat16),
        in_specs=in_vmem(5),
        out_specs=in_vmem(1)[0],
        compiler_params=pltpu.CompilerParams(vmem_limit_bytes=SCOPED),
        cost_estimate=LIGHT,
        name="sum_dense",
    )(tiny, *blocks)


def pack_kernel(branch_ref, *refs):
    for at in range(3):
        refs[3 + at][:128, :] = refs[at][...]
        refs[3 + at][128:, :] = branch_ref[...]


def pack_call(branch, homes):
    return pl.pallas_call(
        pack_kernel,
        out_shape=(jax.ShapeDtypeStruct((256, 768), jnp.bfloat16),) * 3,
        in_specs=in_vmem(4),
        out_specs=tuple(in_vmem(3)),
        compiler_params=pltpu.CompilerParams(vmem_limit_bytes=SCOPED),
        cost_estimate=LIGHT,
        name="pack",
    )(branch, *homes)


def output_kernel(ids_ref, home_ref, *refs):
    plane = ids_ref[2]
    resid_ref, probs_ref, route_ref, out_ref = refs[3:]
    rows = home_ref[...].astype(jnp.float32)
    for at in range(3):
        rows = rows + refs[at][:128, :].astype(jnp.float32)
    lane = lax.broadcasted_iota(jnp.int32, (128, 128), 1)
    gate = jnp.sum(
        jnp.where(lane == route_ref[plane], probs_ref[...], 0.0), axis=-1, keepdims=True
    )
    out_ref[...] = (resid_ref[...] + gate * rows).astype(jnp.bfloat16)


def output_call(ids, home, packed, resid, probs, route):
    return pl.pallas_call(
        output_kernel,
        out_shape=jax.ShapeDtypeStruct((128, 768), jnp.bfloat16),
        in_specs=[in_smem()] + in_vmem(7),
        out_specs=in_vmem(1)[0],
        compiler_params=pltpu.CompilerParams(vmem_limit_bytes=SCOPED),
        cost_estimate=LIGHT,
        name="output",
    )(ids, home, *packed, resid, probs, route)


def finish_kernel(ids_ref, *refs):
    token_ref, gain_ref, grad_ref, out_ref = refs[4:8]
    ending_ref, tiny_ref = refs[9:]
    plane = ids_ref[2]
    gradient = refs[0][:128, :].astype(jnp.float32)
    for at in range(1, 4):
        gradient = gradient + refs[at][:128, :].astype(jnp.float32)
    tokens = token_ref[plane].astype(jnp.float32)
    inverse = lax.rsqrt(jnp.mean(tokens * tokens, axis=-1, keepdims=True) + EPSILON)
    weighted = gradient * gain_ref[...]
    inner = jnp.mean(weighted * tokens, axis=-1, keepdims=True)
    result = inverse * weighted - tokens * (inverse * inverse * inverse * inner) + grad_ref[...]
    ending = result.astype(jnp.bfloat16)
    ending_ref[:128, :] = ending
    ending_ref[128:, :] = out_ref[...]
    tiny_ref[...] = ending[:16, :128]


def finish_call(ids, arrived, tokens, gain, grad, out, ready):
    return pl.pallas_call(
        finish_kernel,
        out_shape=(
            jax.ShapeDtypeStruct((256, 768), jnp.bfloat16),
            jax.ShapeDtypeStruct((16, 128), jnp.bfloat16),
        ),
        in_specs=[in_smem()] + in_vmem(9),
        out_specs=tuple(in_vmem(2)),
        compiler_params=pltpu.CompilerParams(vmem_limit_bytes=SCOPED),
        cost_estimate=LIGHT,
        name="finish",
    )(ids, *arrived, tokens, gain, grad, out, ready)


def dense_grad_kernel(tiny_ref, ids_ref, *refs):
    grad_refs, att_ref, branch_refs = refs[:4], refs[4], refs[5:9]
    normed_ref, kept_ref = refs[9:11]
    sent_refs, total_ref = refs[11:15], refs[15]
    chip = ids_ref[0]
    core = ids_ref[1]
    plane = ids_ref[2]
    total = None
    for away in range(4):
        part = lax.dot_general(
            normed_ref[pl.ds(pl.multiple_of(128 * (chip ^ away), 128), 128), :],
            grad_refs[away][...],
            TN,
            preferred_element_type=jnp.float32,
        )
        total = part if away == 0 else total + part
    rows = None
    for away, branch_ref in enumerate(branch_refs):
        branch = branch_ref[...] if away == 0 else branch_ref[128:, :]
        part = lax.dot_general(
            att_ref[pl.ds(pl.multiple_of(128 * lax.rem(plane + 4 - away, 4), 128), 128), :],
            branch,
            TN,
            preferred_element_type=jnp.float32,
        )
        rows = part if away == 0 else rows + part
    total_ref[...] = jnp.zeros_like(total_ref)
    for half in range(2):
        for place in range(4):
            first = 384 * half + 96 * place
            total_ref[half, place, :96, :576] = total[first : first + 96]
            first = 96 * half + 24 * place
            total_ref[half, place, 96:120, :] = rows[first : first + 24]
    kept_ref[...] = total_ref[core].astype(jnp.bfloat16)
    for place in range(4):
        sent_refs[place][...] = total_ref[1 - core, place].astype(jnp.bfloat16)


def dense_grad_call(tiny, ids, grads, att, branches, normed):
    return pl.pallas_call(
        dense_grad_kernel,
        out_shape=(jax.ShapeDtypeStruct((4, 128, 768), jnp.bfloat16),)
        + (jax.ShapeDtypeStruct((128, 768), jnp.bfloat16),) * 4,
        in_specs=in_vmem(1) + [in_smem()] + in_vmem(10),
        out_specs=tuple(in_vmem(5)),
        scratch_shapes=[pltpu.VMEM((2, 4, 128, 768), jnp.float32)],
        compiler_params=pltpu.CompilerParams(vmem_limit_bytes=SCOPED),
        cost_estimate=LIGHT,
        name="dense_grads",
    )(tiny, ids, *grads, att, *branches, normed)


def tokens_kernel(ids_ref, *refs):
    grad_ref, all_ref = refs[4:]
    plane = ids_ref[2]
    for step in range(4):
        all_ref[lax.rem(plane + 4 - step, 4)] = refs[step][:128, :].astype(jnp.float32)
    for seq in range(4):
        grad_ref[:, seq, :] = all_ref[seq]


def tokens_call(ids, blocks):
    return pl.pallas_call(
        tokens_kernel,
        out_shape=jax.ShapeDtypeStruct((128, 4, 768), jnp.float32),
        in_specs=[in_smem()] + in_vmem(4),
        out_specs=in_vmem(1)[0],
        scratch_shapes=[pltpu.VMEM((4, 128, 768), jnp.float32)],
        compiler_params=pltpu.CompilerParams(vmem_limit_bytes=SCOPED),
        cost_estimate=LIGHT,
        name="tokens_back",
    )(ids, *blocks)


def add_pairs_kernel(*refs):
    for at in range(4):
        total = refs[at][...].astype(jnp.float32) + refs[4 + at][...].astype(jnp.float32)
        refs[8 + at][...] = total.astype(jnp.bfloat16)


def add_pairs_call(parts):
    return pl.pallas_call(
        add_pairs_kernel,
        out_shape=(jax.ShapeDtypeStruct((384, 1536), jnp.bfloat16),) * 4,
        in_specs=in_vmem(8),
        out_specs=tuple(in_vmem(4)),
        compiler_params=pltpu.CompilerParams(vmem_limit_bytes=SCOPED),
        cost_estimate=LIGHT,
        name="add_pairs",
    )(*parts)


def resid_back_kernel(
    ids_ref,
    home0_ref,
    home1_ref,
    home2_ref,
    home3_ref,
    resid_ref,
    probs_ref,
    route_ref,
    grad_ref,
    gain_ref,
    router_ref,
    out_weight_ref,
    grad_resid_ref,
    branch_ref,
    att0_ref,
    att1_ref,
    att2_ref,
    att3_ref,
    gain_grad_ref,
    router_grad_ref,
    all_ref,
):
    chip = ids_ref[0]
    plane = ids_ref[2]
    lane = lax.broadcasted_iota(jnp.int32, (128, 128), 1)
    collected = home0_ref[...].astype(jnp.float32)
    for home_ref in (home1_ref, home2_ref, home3_ref):
        collected = collected + home_ref[...].astype(jnp.float32)
    grad_gate = collected[:, 768:769] + collected[:, 769:770]
    probs = probs_ref[...]
    chosen = lane == route_ref[plane]
    gate = jnp.sum(jnp.where(chosen, probs, 0.0), axis=-1, keepdims=True)
    grad_sent = (collected[:, :768] * gate).astype(jnp.bfloat16).astype(jnp.float32)
    grad_logits = probs * (jnp.where(chosen, grad_gate, 0.0) - gate * grad_gate)
    resid = resid_ref[...]
    gain = gain_ref[...]
    inverse = lax.rsqrt(jnp.mean(resid * resid, axis=-1, keepdims=True) + EPSILON)
    unit = resid * inverse
    router_grad = lax.dot_general(
        grad_logits, unit * gain, TN, precision=PRECISE, preferred_element_type=jnp.float32
    )
    router_grad_ref[...] = router_grad[:8]
    router = jnp.concatenate([router_ref[...], jnp.zeros((124, 768), jnp.float32)], axis=0)
    grad_normed = grad_sent + jnp.dot(
        grad_logits, router, precision=PRECISE, preferred_element_type=jnp.float32
    )
    gain_grad_ref[...] = jnp.sum(grad_normed * unit, axis=0, keepdims=True)
    weighted = grad_normed * gain
    inner = jnp.mean(weighted * resid, axis=-1, keepdims=True)
    grad_resid = inverse * weighted - unit * (inverse * inverse * inner)
    grad_resid = grad_resid + grad_ref[plane].astype(jnp.float32)
    grad_resid_ref[...] = grad_resid
    branch = grad_resid.astype(jnp.bfloat16)
    branch_ref[...] = branch
    for away in range(4):
        all_ref[plane ^ away] = lax.dot_general(
            branch, out_weight_ref[away], NT, preferred_element_type=jnp.float32
        ).astype(jnp.bfloat16)
    for away, att_ref in enumerate((att0_ref, att1_ref, att2_ref, att3_ref)):
        att_ref[...] = all_ref[chip ^ away]


def resid_back_call(ids, homes, resid, probs, route, grad, gain, router, out_weights):
    return pl.pallas_call(
        resid_back_kernel,
        out_shape=(
            jax.ShapeDtypeStruct((128, 768), jnp.float32),
            jax.ShapeDtypeStruct((128, 768), jnp.bfloat16),
        )
        + (jax.ShapeDtypeStruct((128, 192), jnp.bfloat16),) * 4
        + (
            jax.ShapeDtypeStruct((1, 768), jnp.float32),
            jax.ShapeDtypeStruct((8, 768), jnp.float32),
        ),
        in_specs=[in_smem()] + in_vmem(11),
        out_specs=tuple(in_vmem(8)),
        scratch_shapes=[pltpu.VMEM((4, 128, 192), jnp.bfloat16)],
        compiler_params=pltpu.CompilerParams(vmem_limit_bytes=SCOPED),
        cost_estimate=LIGHT,
        name="resid_back",
    )(ids, *homes, resid, probs, route, grad, gain, router, out_weights)


def pinned(first, *others):
    tied = lax.optimization_barrier((first,) + others)
    return tied


def gather_over_ctx(block, chip, core):
    gathered = jnp.stack([block] + [to_chip(block, away) for away in range(1, 4)])
    ordered = jnp.stack([pick(gathered, at ^ chip) for at in range(4)])
    both = jnp.stack([ordered, to_core(ordered)])
    whole = jnp.stack([pick(both, core), pick(both, 1 - core)])
    return whole.reshape((8,) + block.shape)


def local_planned(
    tokens,
    gain_one,
    qkv_weight,
    out_weight,
    rel_weight,
    gain_two,
    router_weight,
    expert_in,
    expert_out,
    routes,
    bucket_table,
    grad_out,
):
    row_count, seq_count, width = tokens.shape
    token_count = row_count * seq_count
    expert_count = router_weight.shape[1]
    capacity = 2 * token_count // expert_count
    slots = expert_count * capacity
    ctx_at = lax.axis_index("ctx")
    plane = lax.axis_index("wsh")
    chip = ctx_at // 2
    core = ctx_at % 2
    ids = jnp.stack([chip, core, plane]).astype(jnp.int32)

    def by_seq(values):
        return lax.optimization_barrier(jnp.swapaxes(values, 0, 1))

    token_blocks = by_seq(tokens)
    weight_qkv = jnp.concatenate(
        lax.optimization_barrier((qkv_weight[:, 1], qkv_weight[:, 2], qkv_weight[:, 0])), axis=1
    )
    normed_low, grad_blocks, *projected = project_call(
        ids, token_blocks, gain_one[None], weight_qkv, grad_out
    )
    in_one, in_two = to_chip(expert_in[0], 1), to_chip(expert_in[0], 2)
    half_rows = pick(out_weight.reshape(2, 96, width), core)
    weight_parts = plane_swap([half_rows] * 4)[1:]
    own = chip_swap(projected)
    route_blocks = by_seq(routes)
    slot_blocks, slot_rows, grad_slots = slot_call(
        tiny_of(projected[0]),
        route_blocks.reshape(token_count) ^ chip,
        grad_blocks.reshape(token_count, width),
    )
    gain_row = gain_two[None]
    router_rows = router_weight.T
    *own, in_one, in_two, slot_blocks, slot_rows, grad_slots = pinned(
        *own, in_one, in_two, slot_blocks, slot_rows, grad_slots
    )
    own[3], weight_in, weight_out = pinned(own[3], expert_in[0], expert_out[0])
    out_one, out_two = to_chip(weight_out, 1), to_chip(weight_out, 2)
    other = [to_core(block) for block in own]

    bucket_pick = (
        bucket_table[:, None] == lax.iota(jnp.int32, rel_weight.shape[0])[None, :]
    ).astype(jnp.float32)
    head_table = jnp.dot(bucket_pick, rel_weight, precision=PRECISE).T
    line = bias_lines(head_table, core)
    *attended, prob, keyval, query = attend_call(ids, tiny_of(half_rows), own, other, line)
    attended[3], *weight_parts = pinned(attended[3], *weight_parts)
    weight_parts = [out_weight] + weight_parts + [to_core(part) for part in weight_parts]
    attended = chip_swap(attended)
    *attended, out_one, out_two = pinned(*attended, out_one, out_two)
    attended[3], late_in, late_out = pinned(attended[3], weight_in, weight_out)
    in_three, out_three = to_chip(late_in, 3), to_chip(late_out, 3)
    att_rows = gather_rows_call(ids, attended)
    att_planes = [att_rows] + [to_plane(att_rows, away) for away in range(1, 4)]
    weights_in, weights_out = [], []
    for block in (weight_in, in_one, in_two, in_three):
        weights_in += [block, to_core(block)]
    for block in (weight_out, out_one, out_two, out_three):
        weights_out += [block, to_core(block)]
    my_resid, my_probs, sent_slots, gate_slots, out_weights = route_call(
        ids, att_planes, weight_parts, token_blocks, gain_row, router_rows, route_blocks, slot_rows
    )
    *homes, hidden, grad_pre = expert_call(
        ids, sent_slots, grad_slots, weights_in, weights_out, slot_blocks
    )
    tiny = tiny_of(homes[0])
    homes = plane_swap(homes)

    weight_grads = weight_grad_call(
        tiny, ids, sent_slots, grad_slots, gate_slots, hidden, grad_pre, weights_out, slot_blocks
    )
    grad_parts, expert_homes = weight_grads[:8], weight_grads[8:]
    *homes, expert_one, expert_two = pinned(*homes, *expert_homes[:2])
    expert_homes = [expert_one, expert_two] + list(expert_homes[2:])
    my_grad_resid, my_branch, *att_grads, grad_gain_two, grad_router = resid_back_call(
        ids,
        homes,
        my_resid,
        my_probs,
        route_blocks,
        grad_blocks,
        gain_row,
        router_rows,
        out_weights,
    )
    att_grads[0], *parts = pinned(att_grads[0], *grad_parts)
    near = add_pairs_call(parts[:4] + [to_core(part) for part in parts[4:]])
    grad_mixed = turn_swap(att_grads)
    packed = pack_call(my_branch, expert_homes[1:])
    rest = pinned(*grad_mixed, *near[1:], *packed)
    grad_mixed, (near_one, near_two, near_three) = rest[:4], rest[4:7]
    packed = plane_shift([None] + list(rest[7:10]))[1:]
    near_one, near_two = to_chip(near_one, 1), to_chip(near_two, 2)
    mine_back, theirs_back, lags, tiny = attend_back_call(ids, query, prob, keyval, grad_mixed)
    theirs_back, near_one, near_two, near_three, *packed = pinned(
        theirs_back, near_one, near_two, near_three, *packed
    )
    out = output_call(ids, expert_homes[0], packed, my_resid, my_probs, route_blocks)
    grad_projected = list(add_queries_call(ids, mine_back, to_core(theirs_back)))
    grad_projected = chip_swap(grad_projected)
    def spread_planes(block):
        return jnp.stack([block] + [to_plane(block, away) for away in range(1, 4)])

    def to_tokens(gathered):
        by_place = jnp.stack([pick(gathered, (plane - at) % 4) for at in range(4)])
        return jnp.swapaxes(lax.optimization_barrier(by_place), 0, 1)

    *grad_projected, near_three = pinned(*grad_projected, near_three)
    near_three = to_chip(near_three, 3)
    *partial, tiny = project_back_call(
        ids,
        grad_projected,
        weight_qkv,
        token_blocks,
        grad_gain_two,
        grad_router,
    )
    tiny, lags = pinned(tiny, lags)
    grad_rel = jnp.dot(bucket_pick.T, table_grad(lags, core), precision=PRECISE)
    rel_row = jnp.where(
        (lax.iota(jnp.int32, 4) == plane)[None, :, None], grad_rel[:, None, :], 0.0
    ).reshape(-1)
    rel_row = jnp.pad(rel_row, (0, width - rel_row.shape[0]))
    kept, *sent = dense_grad_call(
        to_core(tiny), ids, grad_projected, att_rows, [my_branch] + packed, normed_low
    )
    arrived = plane_shift(partial)
    *arrived, kept, sent_one, sent_two, sent_three, sent_four, near_three, rel_row = pinned(
        *arrived, kept, *sent, near_three, rel_row
    )
    weight_sum = 0.0
    for block in (near[0], near_one, near_two, near_three):
        weight_sum = weight_sum + block.astype(jnp.float32)
    grad_weight_out = weight_sum[None, :, :768]
    grad_weight_in = jnp.concatenate([weight_sum[:, 768:1152], weight_sum[:, 1152:]])[None]
    sent = [to_core(part) for part in (sent_one, sent_two, sent_three, sent_four)]
    dense = list(add_dense_call(ids, kept, sent, arrived, rel_row[None]))
    dense_own = dense[0]
    dense = chip_swap(dense)
    ending, tiny = finish_call(
        ids, arrived, token_blocks, gain_one[None], my_grad_resid, out, dense_own
    )
    ending = [ending] + [
        lax.ppermute(ending, "wsh", [(at, (at + step) % 4) for at in range(4)])
        for step in range(1, 4)
    ]
    summed = sum_dense_call(to_core(tiny), dense)
    gathered = chip_swap([summed] * 4)
    both = pinned(*ending, *gathered)
    ending, gathered = both[:4], both[4:]
    both = [gathered, [to_core(block) for block in gathered]]
    ordered = jnp.stack([jnp.stack(part) for part in both])
    ordered = jnp.stack([pick(ordered, core), pick(ordered, 1 - core)])
    ordered = jnp.stack([pick(jnp.swapaxes(ordered, 0, 1), at ^ chip) for at in range(4)], axis=1)
    summed = ordered.reshape(8, 128, width)
    small = summed[0, 120:].astype(jnp.float32) + summed[4, 120:].astype(jnp.float32)
    grad_out_all = summed[:, 96:120].astype(jnp.float32).reshape(192, width)
    grad_qkv = summed[:, :96, :576].astype(jnp.float32).reshape(width, 576)
    grad_qkv = jnp.stack([grad_qkv[:, 384:], grad_qkv[:, :192], grad_qkv[:, 192:384]], axis=1)
    out = to_tokens(jnp.stack([block[128:] for block in ending]))
    grad_tokens = tokens_call(ids, ending)
    rel_all = small[2 + expert_count][: 4 * grad_rel.size].reshape(-1, 4, grad_rel.shape[1])
    return (
        out,
        grad_tokens,
        small[0],
        grad_qkv,
        grad_out_all,
        pick(jnp.swapaxes(rel_all, 0, 1), plane),
        small[1],
        small[2 : 2 + expert_count].T,
        grad_weight_in,
        grad_weight_out,
    )


def solution(mesh):
    placed = (
        P("ctx", None, None),
        P(),
        P(None, None, "wsh"),
        P("wsh", None),
        P(None, "wsh"),
        P(),
        P(),
        P("ctx", None, "wsh"),
        P("ctx", "wsh", None),
        P("ctx", None, None),
        P(),
        P("ctx", None, None),
    )
    planned = mesh.shape['ctx'] == 8 and mesh.shape['wsh'] == 4
    return jax.shard_map(
        local_planned if planned else local,
        mesh=mesh,
        in_specs=placed,
        out_specs=(
            P("ctx", None, None),
            P("ctx", None, None),
            P(),
            P(None, None, "wsh"),
            P("wsh", None),
            P(None, "wsh"),
            P(),
            P(),
            P("ctx", None, "wsh"),
            P("ctx", "wsh", None),
        ),
        check_vma=False,
    )
```

```python
import functools

import jax
import jax.numpy as jnp
from jax import lax
from jax.experimental import pallas as pl
from jax.experimental.pallas import tpu as pltpu
from jax.sharding import PartitionSpec as P

HD = 64
MAXD = 128
BLK = 64


EPSILON = 1e-06
MASKED = -1e30
PRECISE = lax.Precision.HIGHEST


def norm_forward(values, gain_vec):
    inverse = lax.rsqrt(jnp.mean(values * values, axis=-1, keepdims=True) + EPSILON)
    return (values * inverse * gain_vec, inverse)


def norm_backward(values, inverse, gain_vec, gradient):
    weighted = gradient * gain_vec
    inner_mean = jnp.mean(weighted * values, axis=-1, keepdims=True)
    grad_values = inverse * weighted - values * inverse**3 * inner_mean
    grad_gain = jnp.sum(gradient * values * inverse, axis=0)
    return (grad_values, grad_gain)


def exact_gelu(values):
    return jax.nn.gelu(values, approximate=False)


def dealt_positions(first_row, row_total, devices):
    row_ids = first_row + lax.iota(jnp.int32, row_total)
    owner_dev = row_ids // (2 * BLK)
    within = row_ids % (2 * BLK)
    early_pos = owner_dev * BLK + within
    late_pos = (2 * devices - 1 - owner_dev) * BLK + within - BLK
    return jnp.where(within < BLK, early_pos, late_pos)


def block_size():
    return 512


def split_heads(packed, head_count):
    return packed.reshape(
        packed.shape[0], packed.shape[1], head_count, packed.shape[2] // head_count
    )


def run_bias(pos_query, pos_keys, head_table):
    span = 2 * BLK - 1
    starts_query = pos_query[::BLK]
    starts_keys = pos_keys[::BLK]
    query_runs = starts_query.shape[0]
    key_runs = starts_keys.shape[0]
    head_count = head_table.shape[0]
    offsets = lax.iota(jnp.int32, span) - (BLK - 1)
    distance = starts_query[:, None, None] - starts_keys[None, :, None] + offsets[None, None, :]
    clipped = jnp.clip(distance, 0, MAXD - 1)
    onehot = (clipped.reshape(-1)[:, None] == lax.iota(jnp.int32, MAXD)[None, :]).astype(
        jnp.float32
    )
    diag_values = jnp.dot(onehot, head_table.T, precision=PRECISE)
    diag_values = jnp.transpose(
        diag_values.reshape(query_runs, key_runs, span, head_count), (3, 0, 1, 2)
    )
    tiled = jnp.tile(diag_values, (1, 1, 1, BLK + 1))[..., : BLK * (span + 1)]
    tiled = tiled.reshape(head_count, query_runs, key_runs, BLK, span + 1)[..., :BLK][..., ::-1]
    bias = jnp.transpose(tiled, (1, 3, 0, 2, 4)).reshape(
        query_runs * BLK, head_count, key_runs * BLK
    )
    return (bias[:, None], onehot)


def score_block(query, key_heads, pos_query, pos_keys, head_table):
    raw_score = jnp.einsum(
        "qshd,kshd->qshk", query, key_heads, preferred_element_type=jnp.float32
    ) * HD ** (-0.5)
    distance = pos_query[:, None] - pos_keys[None, :]
    score_bias, onehot = run_bias(pos_query, pos_keys, head_table)
    score = jnp.where((distance >= 0)[:, None, None, :], raw_score + score_bias, MASKED)
    return (score, onehot)


def bias_grad(grad_score, onehot):
    span = 2 * BLK - 1
    summed = jnp.sum(grad_score.astype(jnp.float32), axis=1)
    query_rows, head_count, key_rows = summed.shape
    query_runs = query_rows // BLK
    key_runs = key_rows // BLK
    tiles = jnp.transpose(
        summed.reshape(query_runs, BLK, head_count, key_runs, BLK), (2, 0, 3, 1, 4)
    )[..., ::-1]
    widened = jnp.pad(tiles, ((0, 0), (0, 0), (0, 0), (0, 0), (0, span + 1 - BLK)))
    flat = widened.reshape(head_count, query_runs, key_runs, BLK * (span + 1))
    flat = jnp.pad(flat, ((0, 0), (0, 0), (0, 0), (0, (BLK + 1) * span - BLK * (span + 1))))
    diag_sums = jnp.sum(flat.reshape(head_count, query_runs, key_runs, BLK + 1, span), axis=3)
    diag_rows = jnp.transpose(diag_sums, (1, 2, 3, 0)).reshape(-1, head_count)
    return jnp.dot(onehot.T, diag_rows, precision=PRECISE)


def over_blocks(step_fn, carried, piece):
    piece_rows = piece[0].shape[0]
    step_rows = block_size()
    block_count = piece_rows // step_rows
    blocks = tuple(
        (member.reshape((block_count, step_rows) + member.shape[1:]) for member in piece)
    )
    firsts = step_rows * lax.iota(jnp.int32, block_count)

    def advance(carry_state, scan_item):
        return (step_fn(carry_state, scan_item[0], scan_item[1]), None)

    carried, _ = lax.scan(advance, carried, (blocks, firsts))
    return carried


def local(
    tokens,
    gain_one,
    qkv_weight,
    out_weight,
    rel_weight,
    gain_two,
    router_weight,
    expert_in,
    expert_out,
    routes,
    bucket_table,
    grad_out,
):
    ctx_count = lax.axis_size("ctx")
    row_count, seq_count, model_width = tokens.shape
    token_count = row_count * seq_count
    head_count = qkv_weight.shape[2] // HD
    head_width = head_count * HD
    score_scale = HD ** (-0.5)
    pos_query = dealt_positions(lax.axis_index("ctx") * row_count, row_count, ctx_count)
    token_rows = tokens.astype(jnp.float32).reshape(token_count, model_width)
    normed_one, inverse_one = norm_forward(token_rows, gain_one)
    normed_low = normed_one.astype(jnp.bfloat16)
    projected = jnp.einsum(
        "nd,dce->nce", normed_low, qkv_weight, preferred_element_type=jnp.float32
    ).astype(jnp.bfloat16)
    query_flat = projected[:, 0].reshape(row_count, seq_count, head_width)
    query = split_heads(query_flat, head_count)
    keyval = projected[:, 1:].reshape(row_count, seq_count, 2 * head_width)
    own_keys = split_heads(keyval[..., :head_width], head_count)
    own_values = split_heads(keyval[..., head_width:], head_count)
    bucket_pick = (
        bucket_table[:, None] == lax.iota(jnp.int32, rel_weight.shape[0])[None, :]
    ).astype(jnp.float32)
    head_table = jnp.dot(bucket_pick, rel_weight, precision=PRECISE).T

    def attend(carry_state, key_block, first_row):
        key_heads = split_heads(key_block[0][..., :head_width], head_count)
        value_heads = split_heads(key_block[0][..., head_width:], head_count)
        pos_keys = dealt_positions(first_row, key_heads.shape[0], ctx_count)
        score, _ = score_block(query, key_heads, pos_query, pos_keys, head_table)
        row_max, denominator, weighted = carry_state
        new_max = jnp.maximum(row_max, jnp.max(score, axis=-1))
        rescale = jnp.exp(row_max - new_max)
        weights = jnp.exp(score - new_max[..., None])
        denominator = rescale * denominator + jnp.sum(weights, axis=-1)
        weighted = rescale[..., None] * weighted + jnp.einsum(
            "qshk,kshd->qshd",
            weights.astype(jnp.bfloat16),
            value_heads,
            preferred_element_type=jnp.float32,
        )
        return (new_max, denominator, weighted)

    stat_shape = (row_count, seq_count, head_count)
    zero_heads = jnp.zeros((row_count, seq_count, head_count, HD), jnp.float32)
    initial = (
        jnp.full(stat_shape, MASKED, jnp.float32),
        jnp.zeros(stat_shape, jnp.float32),
        zero_heads,
    )
    row_max, denominator, weighted = over_blocks(
        attend, initial, (lax.all_gather(keyval, "ctx", axis=0, tiled=True),)
    )
    attended = weighted / denominator[..., None]
    log_total = row_max + jnp.log(denominator)
    attended_low = attended.reshape(token_count, head_width).astype(jnp.bfloat16)
    branch = lax.psum(
        jnp.dot(attended_low, out_weight, preferred_element_type=jnp.float32).astype(jnp.bfloat16),
        "wsh",
    ).astype(jnp.float32)
    resid = token_rows + branch
    normed_two, inverse_two = norm_forward(resid, gain_two)
    logits = jnp.dot(normed_two, router_weight, precision=PRECISE)
    shifted = jnp.exp(logits - jnp.max(logits, axis=-1, keepdims=True))
    gate_probs = shifted / jnp.sum(shifted, axis=-1, keepdims=True)
    expert_count = router_weight.shape[1]
    expert_ids = routes.reshape(token_count)
    choose = expert_ids[:, None] == lax.iota(jnp.int32, expert_count)[None, :]
    gate_value = jnp.sum(jnp.where(choose, gate_probs, 0.0), axis=1)
    lower_ones = (
        lax.iota(jnp.int32, token_count)[:, None] >= lax.iota(jnp.int32, token_count)[None, :]
    ).astype(jnp.bfloat16)
    filled = jnp.dot(
        lower_ones, choose.astype(jnp.bfloat16), preferred_element_type=jnp.float32
    ).astype(jnp.int32)
    slot_index = jnp.sum(jnp.where(choose, filled - 1, 0), axis=1)
    capacity = max(2, 2 * token_count // expert_count)
    target = expert_ids * capacity + slot_index
    slot_pick = target[:, None] == lax.iota(jnp.int32, expert_count * capacity)[None, :]
    slot_low = slot_pick.astype(jnp.bfloat16)
    slot_full = slot_pick.astype(jnp.float32)
    weight_in = expert_in[0]
    weight_out = expert_out[0]

    def spread(values):
        buffer = jnp.einsum(
            "nm,nd->md", slot_low, values, preferred_element_type=jnp.float32
        ).astype(jnp.bfloat16)
        doubled = jnp.broadcast_to(
            buffer.reshape(expert_count, 1, capacity, model_width),
            (expert_count, 2, capacity, model_width),
        )
        return doubled.reshape(2 * expert_count, capacity, model_width)

    def collect(returned):
        row_width = returned.shape[-1]
        paired = jnp.sum(returned.reshape(expert_count, 2, capacity, row_width), axis=1)
        return jnp.dot(
            slot_full, paired.reshape(expert_count * capacity, row_width), precision=PRECISE
        )

    arrived_rows = lax.all_to_all(
        spread(normed_two.astype(jnp.bfloat16)), "ctx", split_axis=0, concat_axis=0, tiled=True
    )
    flat_rows = arrived_rows.reshape(-1, model_width)
    pre_act = jnp.dot(flat_rows, weight_in, preferred_element_type=jnp.float32)
    hidden = exact_gelu(pre_act).astype(jnp.bfloat16)
    returned = lax.all_to_all(
        jnp.dot(hidden, weight_out, preferred_element_type=jnp.float32)
        .reshape(arrived_rows.shape)
        .astype(jnp.bfloat16),
        "ctx",
        split_axis=0,
        concat_axis=0,
        tiled=True,
    ).astype(jnp.float32)
    expert_rows = lax.psum(collect(returned).astype(jnp.bfloat16), "wsh").astype(jnp.float32)
    result = resid + gate_value[:, None] * expert_rows
    out = result.astype(jnp.bfloat16).reshape(row_count, seq_count, model_width)
    grad_rows_f = grad_out.astype(jnp.float32).reshape(token_count, model_width)
    grad_gate = jnp.sum(grad_rows_f * expert_rows, axis=1)
    grad_expert_rows = (gate_value[:, None] * grad_rows_f).astype(jnp.bfloat16)
    arrived_grad = lax.all_to_all(
        spread(grad_expert_rows), "ctx", split_axis=0, concat_axis=0, tiled=True
    )
    flat_rows = arrived_rows.reshape(-1, model_width)
    flat_grad = arrived_grad.reshape(-1, model_width)
    pre_act = jnp.dot(flat_rows, weight_in, preferred_element_type=jnp.float32)
    hidden, gelu_pull = jax.vjp(exact_gelu, pre_act)
    hidden_low = hidden.astype(jnp.bfloat16)
    grad_weight_out = jnp.einsum(
        "rf,rd->fd", hidden_low, flat_grad, preferred_element_type=jnp.float32
    )
    grad_hidden = jnp.einsum("rd,fd->rf", flat_grad, weight_out, preferred_element_type=jnp.float32)
    grad_pre = gelu_pull(grad_hidden)[0].astype(jnp.bfloat16)
    grad_weight_in = jnp.einsum(
        "rd,rf->df", flat_rows, grad_pre, preferred_element_type=jnp.float32
    )
    partial_back = jnp.einsum(
        "rf,df->rd", grad_pre, weight_in, preferred_element_type=jnp.float32
    ).reshape(arrived_rows.shape)
    returned_grad = lax.all_to_all(
        partial_back.astype(jnp.bfloat16), "ctx", split_axis=0, concat_axis=0, tiled=True
    ).astype(partial_back.dtype)
    grad_sent = lax.psum(collect(returned_grad).astype(jnp.bfloat16), "wsh").astype(jnp.float32)
    grad_sent = lax.optimization_barrier(grad_sent.astype(jnp.bfloat16)).astype(jnp.float32)
    grad_logits = gate_probs * (
        jnp.where(choose, grad_gate[:, None], 0.0) - (gate_value * grad_gate)[:, None]
    )
    grad_router = jnp.dot(normed_two.T, grad_logits, precision=PRECISE)
    grad_normed_two = grad_sent + jnp.dot(grad_logits, router_weight.T, precision=PRECISE)
    grad_resid, grad_gain_two = norm_backward(resid, inverse_two, gain_two, grad_normed_two)
    grad_resid = grad_resid + grad_rows_f
    grad_branch = grad_resid.astype(jnp.bfloat16)
    grad_out_rows = jnp.einsum(
        "nw,nd->wd", attended_low, grad_branch, preferred_element_type=jnp.float32
    )
    grad_att = jnp.einsum(
        "nd,wd->nw", grad_branch, out_weight, preferred_element_type=jnp.float32
    ).astype(jnp.bfloat16)
    grad_att_flat = grad_att.reshape(row_count, seq_count, head_width)
    grad_att_heads = split_heads(grad_att_flat, head_count)
    row_inner = jnp.sum(grad_att_heads.astype(jnp.float32) * attended, axis=-1)

    def query_grads(carry_state, key_block, first_row):
        key_heads = split_heads(key_block[0][..., :head_width], head_count)
        value_heads = split_heads(key_block[0][..., head_width:], head_count)
        pos_keys = dealt_positions(first_row, key_heads.shape[0], ctx_count)
        score, onehot = score_block(query, key_heads, pos_query, pos_keys, head_table)
        weights = jnp.exp(score - log_total[..., None])
        grad_weights = jnp.einsum(
            "qshd,kshd->qshk", grad_att_heads, value_heads, preferred_element_type=jnp.float32
        )
        grad_score = (weights * (grad_weights - row_inner[..., None])).astype(jnp.bfloat16)
        grad_query = (
            carry_state[0]
            + jnp.einsum(
                "qshk,kshd->qshd", grad_score, key_heads, preferred_element_type=jnp.float32
            )
            * score_scale
        )
        return (grad_query, carry_state[1] + bias_grad(grad_score, onehot))

    def key_grads(carry_state, query_block, first_row):
        query_heads = split_heads(query_block[0][..., :head_width], head_count)
        grad_heads = split_heads(query_block[0][..., head_width:], head_count)
        pos_rows = dealt_positions(first_row, query_heads.shape[0], ctx_count)
        score, _ = score_block(query_heads, own_keys, pos_rows, pos_query, head_table)
        weights = jnp.exp(score - query_block[1][..., None])
        grad_value = carry_state[1] + jnp.einsum(
            "qshk,qshd->kshd",
            weights.astype(jnp.bfloat16),
            grad_heads,
            preferred_element_type=jnp.float32,
        )
        grad_weights = jnp.einsum(
            "qshd,kshd->qshk", grad_heads, own_values, preferred_element_type=jnp.float32
        )
        grad_score = (weights * (grad_weights - query_block[2][..., None])).astype(jnp.bfloat16)
        grad_key = (
            carry_state[0]
            + jnp.einsum(
                "qshk,qshd->kshd", grad_score, query_heads, preferred_element_type=jnp.float32
            )
            * score_scale
        )
        return (grad_key, grad_value)

    packed = jnp.concatenate([query_flat, grad_att_flat], axis=-1)
    zero_table = jnp.zeros((MAXD, head_count), jnp.float32)
    grad_query, grad_table = over_blocks(
        query_grads, (zero_heads, zero_table), (lax.all_gather(keyval, "ctx", axis=0, tiled=True),)
    )
    grad_key, grad_value = over_blocks(
        key_grads,
        (zero_heads, zero_heads),
        (
            lax.all_gather(packed, "ctx", axis=0, tiled=True),
            lax.all_gather(log_total.astype(jnp.bfloat16), "ctx", axis=0, tiled=True).astype(
                jnp.float32
            ),
            lax.all_gather(row_inner.astype(jnp.bfloat16), "ctx", axis=0, tiled=True).astype(
                jnp.float32
            ),
        ),
    )
    grad_projected = jnp.stack(
        [member.reshape(token_count, head_width) for member in (grad_query, grad_key, grad_value)],
        axis=1,
    ).astype(jnp.bfloat16)
    grad_normed_one = lax.psum(
        jnp.einsum(
            "nce,dce->nd", grad_projected, qkv_weight, preferred_element_type=jnp.float32
        ).astype(jnp.bfloat16),
        "wsh",
    ).astype(jnp.float32)
    grad_qkv = jnp.einsum(
        "nd,nce->dce", normed_low, grad_projected, preferred_element_type=jnp.float32
    )
    grad_tokens, grad_gain_one = norm_backward(token_rows, inverse_one, gain_one, grad_normed_one)
    grad_tokens = grad_tokens + grad_resid
    grad_rel = jnp.dot(bucket_pick.T, grad_table, precision=PRECISE)
    summed_grads = lax.psum(
        (grad_qkv, grad_out_rows, grad_rel, grad_gain_one, grad_gain_two, grad_router), "ctx"
    )
    return (
        out,
        grad_tokens.reshape(row_count, seq_count, model_width),
        summed_grads[3],
        summed_grads[0],
        summed_grads[1],
        summed_grads[2],
        summed_grads[4],
        summed_grads[5],
        grad_weight_in[None],
        grad_weight_out[None],
    )


NT = (((1,), (1,)), ((), ()))
TN = (((0,), (0,)), ((), ()))
SCOPED = 16 * 1024 * 1024
LIGHT = pl.CostEstimate(flops=1_000_000, bytes_accessed=10_000, transcendentals=0)


def strip(step, side):
    width = 128 * (step + 1) if side == 0 else 128 * (8 - step)
    first = 0 if side == 0 else 128 * (step + 1)
    return (width, first)


def skewed(values, leftward):
    width = values.shape[1]
    row = lax.broadcasted_iota(jnp.int32, values.shape, 0)
    for bit in range(6):
        shift = width - (1 << bit) if leftward else 1 << bit
        moved = pltpu.roll(values, shift, 1)
        values = jnp.where((row & (1 << bit)) != 0, moved, values)
    return values


def attend_kernel(ids_ref, *refs):
    own_refs, other_refs, line_ref = refs[1:5], refs[5:9], refs[9]
    att_refs = refs[10:14]
    far_prob_ref, far_keyval_ref, far_query_ref = refs[14:17]
    bias_ref, own_ref, other_ref, all_ref, near_ref = refs[17:22]
    prob_ref, keyval_ref, query_ref, sems, out_sems = refs[22:]

    def prob_copy(step):
        return pltpu.make_async_copy(
            prob_ref.at[:, step], far_prob_ref.at[:, step], out_sems.at[step]
        )

    def other_copies():
        return (
            pltpu.make_async_copy(keyval_ref, far_keyval_ref, out_sems.at[4]),
            pltpu.make_async_copy(query_ref, far_query_ref, out_sems.at[5]),
        )

    chip = ids_ref[0]
    core = ids_ref[1]

    def gather_keys(parity):
        for place in range(16):
            owner = place if place < 8 else 15 - place
            half = 0 if place < 8 else BLK
            source = own_ref if owner % 2 == parity else other_ref
            keyval_ref[place * BLK : (place + 1) * BLK, :] = source[
                owner // 2, half : half + BLK, :
            ]

    @pl.when(pl.program_id(0) == 0)
    def _():
        fetch(list(own_refs) + list(other_refs), [near_ref.at[at] for at in range(8)], sems)
        for away in range(4):
            own_ref[chip ^ away] = near_ref[away, :, :384]
            other_ref[chip ^ away] = near_ref[4 + away, :, :384]
            query_ref[chip ^ away] = near_ref[away, :, 384:] * jnp.bfloat16(HD ** (-0.5))
        for head in range(3):
            for side in range(2):
                line = jnp.broadcast_to(line_ref[head, side : side + 1, :], (BLK, 512))
                bias_ref[head, side] = skewed(line, False)[:, 128:384]

        @pl.when(core == 0)
        def _():
            gather_keys(0)

        @pl.when(core == 1)
        def _():
            gather_keys(1)

        for copy in other_copies():
            copy.start()

    def attend_step(step):
        jobs = [(head, side) for side in range(2) for head in range(3)]
        scores = []
        for head, side in jobs:
            width, _ = strip(step, side)
            rows = slice(side * BLK, (side + 1) * BLK)
            query = query_ref[step, rows, HD * head : HD * (head + 1)]
            keys = keyval_ref[:width, HD * head : HD * (head + 1)]
            score = lax.dot_general(query, keys, NT, preferred_element_type=jnp.float32)
            near = min(width, 256)
            close = score[:, width - near :] + bias_ref[head, side, :, 256 - near :]
            if width > near:
                score = jnp.concatenate([score[:, : width - near], close], axis=1)
            else:
                score = close
            scores.append(score)
        tops = [jnp.max(score, axis=-1, keepdims=True) for score in scores]
        weights = [jnp.exp(score - top) for score, top in zip(scores, tops)]
        totals = [jnp.sum(weight, axis=-1, keepdims=True) for weight in weights]
        probs = [
            (weight * (1.0 / total)).astype(jnp.bfloat16)
            for weight, total in zip(weights, totals)
        ]
        for (head, side), prob in zip(jobs, probs):
            width, first = strip(step, side)
            prob_ref[head, step, :, first : first + width] = prob
        prob_copy(step).start()
        mixed = [
            jnp.dot(
                prob,
                keyval_ref[: prob.shape[1], 192 + HD * head : 192 + HD * (head + 1)],
                preferred_element_type=jnp.float32,
            ).astype(jnp.bfloat16)
            for (head, side), prob in zip(jobs, probs)
        ]
        for side in range(2):
            rows = slice(side * BLK, (side + 1) * BLK)
            all_ref[step, rows, :] = jnp.concatenate(
                mixed[3 * side : 3 * side + 3], axis=1
            )

    for step in range(4):
        pl.when(pl.program_id(0) == step)(functools.partial(attend_step, step))

    @pl.when(pl.program_id(0) == 3)
    def _():
        for away in range(4):
            att_refs[away][...] = all_ref[chip ^ away]
        for step in range(4):
            prob_copy(step).wait()
        for copy in other_copies():
            copy.wait()


def attend_back_kernel(ids_ref, *refs):
    far_query_ref, prob_ref, far_keyval_ref = refs[:3]
    grad_refs = refs[3:7]
    mine_ref, theirs_ref, lags_ref, tiny_ref, total_ref, near_ref, grad_ref = refs[7:14]
    query_ref, keyval_ref, sems = refs[14:]
    core = ids_ref[1]
    plane = ids_ref[2]

    @pl.when(pl.program_id(0) == 0)
    def _():
        total_ref[...] = jnp.zeros_like(total_ref)
        near_ref[...] = jnp.zeros_like(near_ref)
        fetch(
            list(grad_refs) + [far_query_ref, far_keyval_ref],
            [grad_ref.at[plane ^ away] for away in range(4)] + [query_ref, keyval_ref],
            sems,
        )

    def back_step(step):
        jobs = [(head, side) for side in range(2) for head in range(3)]
        queries, grads, probs, products = [], [], [], []
        for head, side in jobs:
            width, first = strip(step, side)
            rows = slice(side * BLK, (side + 1) * BLK)
            queries.append(query_ref[step, rows, HD * head : HD * (head + 1)])
            grad = grad_ref[step, rows, HD * head : HD * (head + 1)]
            grads.append(grad)
            values = keyval_ref[:width, 192 + HD * head : 192 + HD * (head + 1)]
            prob = prob_ref[head, 0, :, first : first + width]
            probs.append(prob)
            grad_prob = lax.dot_general(grad, values, NT, preferred_element_type=jnp.float32)
            products.append(prob.astype(jnp.float32) * grad_prob)
        inners = [jnp.sum(product, axis=-1, keepdims=True) for product in products]
        lows = [
            (product - prob.astype(jnp.float32) * inner).astype(jnp.bfloat16)
            for product, prob, inner in zip(products, probs, inners)
        ]
        dqs = [
            (
                jnp.dot(
                    low,
                    keyval_ref[: low.shape[1], HD * head : HD * (head + 1)],
                    preferred_element_type=jnp.float32,
                )
                * HD ** (-0.5)
            ).astype(jnp.bfloat16)
            for (head, side), low in zip(jobs, lows)
        ]
        for side in range(2):
            rows = slice(side * BLK, (side + 1) * BLK)
            width, _ = strip(step, side)
            mine_ref[step, rows, 384:] = jnp.concatenate(dqs[3 * side : 3 * side + 3], axis=1)
            parts = []
            for left, right in ((lows, queries), (probs, grads)):
                for head in range(3):
                    parts.append(
                        lax.dot_general(
                            left[3 * side + head],
                            right[3 * side + head],
                            TN,
                            preferred_element_type=jnp.float32,
                        )
                    )
            total_ref[:width, :] += jnp.concatenate(parts, axis=1)
        for (head, side), low in zip(jobs, lows):
            width, _ = strip(step, side)
            score = low.astype(jnp.float32)
            near_ref[head, 2 * side] += score[:, width - 128 :]
            if width >= 256:
                near_ref[head, 2 * side + 1] += score[:, width - 256 : width - 128]
            if width > 256:
                far = score[:, :128]
                for chunk in range(1, (width - 256) // 128):
                    far = far + score[:, 128 * chunk : 128 * (chunk + 1)]
                near_ref[head, 4] += far

    for step in range(4):
        pl.when(pl.program_id(0) == step)(functools.partial(back_step, step))

    def scatter_keys(parity):
        for place in range(16):
            owner = place if place < 8 else 15 - place
            half = 0 if place < 8 else BLK
            target = mine_ref if owner % 2 == parity else theirs_ref
            target[owner // 2, half : half + BLK, :384] = total_ref[
                place * BLK : (place + 1) * BLK, :
            ].astype(jnp.bfloat16)

    @pl.when(pl.program_id(0) == 3)
    def _():
        tiny_ref[...] = total_ref[:16, :128].astype(jnp.bfloat16)
        lags_ref[...] = jnp.zeros_like(lags_ref)
        for head in range(3):
            for kind in range(4):
                wide = jnp.concatenate(
                    [near_ref[head, kind], jnp.zeros((BLK, 128), jnp.float32)], axis=1
                )
                lags_ref[head, kind : kind + 1, :] = jnp.sum(
                    skewed(wide, True), axis=0, keepdims=True
                )
            lags_ref[head, 4:5, :128] = jnp.sum(near_ref[head, 4], axis=0, keepdims=True)

        @pl.when(core == 0)
        def _():
            scatter_keys(0)

        @pl.when(core == 1)
        def _():
            scatter_keys(1)


def whole(*shape):
    return pl.BlockSpec(shape, lambda at: (0,) * len(shape))


def in_hbm():
    return pl.BlockSpec(memory_space=pltpu.HBM)


def by_step():
    return pl.BlockSpec((3, 1, BLK, 1152), lambda at: (0, at, 0, 0))


def in_vmem(count):
    return [pl.BlockSpec(memory_space=pltpu.VMEM)] * count


def attend_call(ids, tiny, own, other, line):
    return pl.pallas_call(
        attend_kernel,
        grid=(4,),
        out_shape=(jax.ShapeDtypeStruct((128, 192), jnp.bfloat16),) * 4
        + (
            jax.ShapeDtypeStruct((3, 4, BLK, 1152), jnp.bfloat16),
            jax.ShapeDtypeStruct((1024, 384), jnp.bfloat16),
            jax.ShapeDtypeStruct((4, 128, 192), jnp.bfloat16),
        ),
        in_specs=[in_smem(), whole(16, 128)] + [in_hbm()] * 8 + [whole(3, 2, 512)],
        out_specs=(whole(128, 192),) * 4 + (in_hbm(),) * 3,
        scratch_shapes=[
            pltpu.VMEM((3, 2, BLK, 256), jnp.float32),
            pltpu.VMEM((4, 128, 384), jnp.bfloat16),
            pltpu.VMEM((4, 128, 384), jnp.bfloat16),
            pltpu.VMEM((4, 128, 192), jnp.bfloat16),
            pltpu.VMEM((8, 128, 576), jnp.bfloat16),
            pltpu.VMEM((3, 4, BLK, 1152), jnp.bfloat16),
            pltpu.VMEM((1024, 384), jnp.bfloat16),
            pltpu.VMEM((4, 128, 192), jnp.bfloat16),
            pltpu.SemaphoreType.DMA((8,)),
            pltpu.SemaphoreType.DMA((6,)),
        ],
        compiler_params=pltpu.CompilerParams(
            vmem_limit_bytes=SCOPED, dimension_semantics=("arbitrary",)
        ),
        cost_estimate=LIGHT,
        name="attend",
    )(ids, tiny, *own, *other, line)


def attend_back_call(ids, query, prob, keyval, grads):
    return pl.pallas_call(
        attend_back_kernel,
        grid=(4,),
        out_shape=(
            jax.ShapeDtypeStruct((4, 128, 576), jnp.bfloat16),
            jax.ShapeDtypeStruct((4, 128, 384), jnp.bfloat16),
            jax.ShapeDtypeStruct((3, 8, 256), jnp.float32),
            jax.ShapeDtypeStruct((16, 128), jnp.bfloat16),
        ),
        in_specs=[
            in_smem(),
            in_hbm(),
            by_step(),
            in_hbm(),
        ]
        + [in_hbm()] * 4,
        out_specs=(
            whole(4, 128, 576),
            whole(4, 128, 384),
            whole(3, 8, 256),
            whole(16, 128),
        ),
        scratch_shapes=[
            pltpu.VMEM((1024, 384), jnp.float32),
            pltpu.VMEM((3, 5, BLK, 128), jnp.float32),
            pltpu.VMEM((4, 128, 192), jnp.bfloat16),
            pltpu.VMEM((4, 128, 192), jnp.bfloat16),
            pltpu.VMEM((1024, 384), jnp.bfloat16),
            pltpu.SemaphoreType.DMA((6,)),
        ],
        compiler_params=pltpu.CompilerParams(
            vmem_limit_bytes=SCOPED, dimension_semantics=("arbitrary",)
        ),
        cost_estimate=LIGHT,
        name="attend_back",
    )(ids, query, prob, keyval, *grads)


def to_core(values):
    return lax.ppermute(values, "ctx", [(at, at ^ 1) for at in range(8)])


def to_chip(values, away):
    return lax.ppermute(values, "ctx", [(at, at ^ (2 * away)) for at in range(8)])


def to_plane(values, away):
    return lax.ppermute(values, "wsh", [(at, at ^ away) for at in range(4)])


def tiny_of(source):
    return to_core(source.reshape(-1, source.shape[-1])[:16, :128])


def chip_swap(blocks):
    return [blocks[0]] + [to_chip(blocks[away], away) for away in range(1, 4)]


def plane_shift(blocks):
    return [blocks[0]] + [
        lax.ppermute(blocks[step], "wsh", [(at, (at + step) % 4) for at in range(4)])
        for step in range(1, 4)
    ]


def plane_swap(blocks):
    return [blocks[0]] + [to_plane(blocks[away], away) for away in range(1, 4)]


def seat(chip, core, plane):
    return (2 * chip + core) * 4 + plane


def turn_swap(blocks):
    return [
        lax.ppermute(
            block,
            ("ctx", "wsh"),
            [
                (seat(chip, core, plane), seat(plane, core, chip ^ away))
                for chip in range(4)
                for core in range(2)
                for plane in range(4)
            ],
        )
        for away, block in enumerate(blocks)
    ]


def pick(blocks, at):
    return lax.dynamic_index_in_dim(blocks, at, 0, keepdims=False)


def bias_lines(head_table, core):
    shifted = head_table - head_table[:, MAXD - 1 :]
    turned = shifted[:, ::-1]

    def line(zeros):
        return jnp.pad(
            jnp.pad(turned, ((0, 0), (zeros, 0))),
            ((0, 0), (0, 512 - MAXD - zeros)),
            constant_values=MASKED,
        )

    even, odd = line(129), line(193)
    return jnp.where(
        core == 0, jnp.stack([even, odd], axis=1), jnp.stack([odd, even], axis=1)
    )


def table_grad(lags, core):
    offsets = lax.iota(jnp.int32, 256)
    offsets = jnp.where(offsets < 128, offsets, offsets - 256)
    base = BLK * jnp.stack([core, core + 2, 1 - core, 3 - core])
    clipped = jnp.clip(base[:, None] - offsets[None, :], 0, MAXD - 1)
    onehot = (clipped[..., None] == lax.iota(jnp.int32, MAXD)).astype(jnp.float32)
    table = jnp.einsum("hkz,kzd->dh", lags[:, :4], onehot, precision=PRECISE)
    last = (lax.iota(jnp.int32, MAXD) == MAXD - 1).astype(jnp.float32)
    return table + last[:, None] * jnp.sum(lags[:, 4], axis=-1)


def gelu_parts(values):
    cdf = 0.5 * (1.0 + lax.erf(values * (0.5**0.5)))
    density = jnp.exp(-0.5 * values * values) * ((0.5 / jnp.pi) ** 0.5)
    return (values * cdf, cdf + values * density)


def in_smem():
    return pl.BlockSpec(memory_space=pltpu.SMEM)


def split_column(column):
    high = column.astype(jnp.bfloat16)
    low = (column - high.astype(jnp.float32)).astype(jnp.bfloat16)
    lane = lax.broadcasted_iota(jnp.int32, (column.shape[0], 128), 1)
    wide = jnp.where(
        lane == 0,
        high.astype(jnp.float32),
        jnp.where(lane == 1, low.astype(jnp.float32), 0.0),
    )
    return wide.astype(jnp.bfloat16)


def project_kernel(ids_ref, token_ref, gain_ref, weight_ref, turn_ref, *refs):
    normed_ref, rows_ref, refs = refs[0], refs[1], refs[2:]
    for seq in range(4):
        rows_ref[seq] = turn_ref[:, seq, :]
    chip = ids_ref[0]
    tokens = token_ref[...].reshape(512, 768).astype(jnp.float32)
    inverse = lax.rsqrt(jnp.mean(tokens * tokens, axis=-1, keepdims=True) + EPSILON)
    normed = (tokens * inverse * gain_ref[...]).astype(jnp.bfloat16)
    normed_ref[...] = normed
    projected = jnp.dot(normed, weight_ref[...], preferred_element_type=jnp.float32)
    refs[4][...] = projected.astype(jnp.bfloat16).reshape(4, 128, 576)
    for away in range(4):
        refs[away][...] = refs[4][chip ^ away]


def project_call(ids, tokens, gain, weight, grad):
    return pl.pallas_call(
        project_kernel,
        out_shape=(
            jax.ShapeDtypeStruct((512, 768), jnp.bfloat16),
            jax.ShapeDtypeStruct((4, 128, 768), jnp.bfloat16),
        )
        + (jax.ShapeDtypeStruct((128, 576), jnp.bfloat16),) * 4,
        in_specs=[in_smem()] + in_vmem(4),
        out_specs=tuple(in_vmem(6)),
        scratch_shapes=[pltpu.VMEM((4, 128, 576), jnp.bfloat16)],
        compiler_params=pltpu.CompilerParams(vmem_limit_bytes=SCOPED),
        cost_estimate=LIGHT,
        name="project",
    )(ids, tokens, gain, weight, grad)


def gather_rows_kernel(ids_ref, *refs):
    chip = ids_ref[0]
    for away in range(4):
        refs[4][pl.ds(pl.multiple_of(128 * (chip ^ away), 128), 128), :] = refs[away][...]


def gather_rows_call(ids, blocks):
    return pl.pallas_call(
        gather_rows_kernel,
        out_shape=jax.ShapeDtypeStruct((512, 192), jnp.bfloat16),
        in_specs=[in_smem()] + in_vmem(4),
        out_specs=in_vmem(1)[0],
        compiler_params=pltpu.CompilerParams(vmem_limit_bytes=SCOPED),
        cost_estimate=LIGHT,
        name="gather_rows",
    )(ids, *blocks)


def add_queries_kernel(ids_ref, mine_ref, theirs_ref, *sum_refs):
    chip = ids_ref[0]
    for away, sum_ref in enumerate(sum_refs):
        mine = mine_ref[chip ^ away]
        total = mine[:, :384].astype(jnp.float32) + theirs_ref[chip ^ away].astype(jnp.float32)
        sum_ref[:, :384] = total.astype(jnp.bfloat16)
        sum_ref[:, 384:] = mine[:, 384:]


def add_queries_call(ids, mine, theirs):
    return pl.pallas_call(
        add_queries_kernel,
        out_shape=(jax.ShapeDtypeStruct((128, 576), jnp.bfloat16),) * 4,
        in_specs=[in_smem()] + in_vmem(2),
        out_specs=tuple(in_vmem(4)),
        compiler_params=pltpu.CompilerParams(vmem_limit_bytes=SCOPED),
        cost_estimate=LIGHT,
        name="add_queries",
    )(ids, mine, theirs)


def fetch(sources, targets, sems):
    copies = [
        pltpu.make_async_copy(source, target, sems.at[at])
        for at, (source, target) in enumerate(zip(sources, targets))
    ]
    for copy in copies:
        copy.start()
    for copy in copies:
        copy.wait()


def route_kernel(*refs):
    ids_ref = refs[0]
    att_refs, part_refs = refs[1:5], refs[5:12]
    token_ref, gain_ref, router_ref, route_ref, slot_ref = refs[12:17]
    resid_ref, probs_ref, sent_ref, gate_ref, out_weight_ref = refs[17:22]
    payload_ref, branch_ref, all_probs_ref, att_ref, own_ref, half_ref, sems = refs[22:]
    fetch(
        list(att_refs) + list(part_refs),
        [att_ref.at[at] for at in range(4)] + [own_ref] + [half_ref.at[at] for at in range(6)],
        sems,
    )
    att_refs = [att_ref.at[at] for at in range(4)]
    part_refs = [own_ref] + [half_ref.at[at] for at in range(6)]
    core = ids_ref[1]
    plane = ids_ref[2]
    out_weight_ref[0] = part_refs[0][...]
    own_rows = pl.ds(pl.multiple_of(96 * core, 32), 96)
    other_rows = pl.ds(pl.multiple_of(96 - 96 * core, 32), 96)
    for away in range(1, 4):
        out_weight_ref[away, own_rows, :] = part_refs[away][...]
        out_weight_ref[away, other_rows, :] = part_refs[3 + away][...]
    branch = token_ref[...].reshape(512, 768).astype(jnp.float32)
    for away, att_ref in enumerate(att_refs):
        branch = branch + jnp.dot(
            att_ref[...], out_weight_ref[away], preferred_element_type=jnp.float32
        )
    branch_ref[...] = branch.reshape(4, 128, 768)
    inverse = lax.rsqrt(jnp.mean(branch * branch, axis=-1, keepdims=True) + EPSILON)
    normed = branch * inverse * gain_ref[...]
    payload_ref[:, :768] = normed.astype(jnp.bfloat16)
    router = jnp.concatenate([router_ref[...], jnp.zeros((124, 768), jnp.float32)], axis=0)
    logits = lax.dot_general(
        normed, router, NT, precision=PRECISE, preferred_element_type=jnp.float32
    )
    lane = lax.broadcasted_iota(jnp.int32, (512, 128), 1)
    logits = jnp.where(lane < 4, logits, MASKED)
    shifted = jnp.exp(logits - jnp.max(logits, axis=-1, keepdims=True))
    probs = shifted / jnp.sum(shifted, axis=-1, keepdims=True)
    all_probs_ref[...] = probs.reshape(4, 128, 128)
    gate = jnp.sum(
        jnp.where(lane == route_ref[...].reshape(512, 1), probs, 0.0), axis=-1, keepdims=True
    )
    payload_ref[:, 768:] = split_column(gate)
    resid_ref[...] = branch_ref[plane]
    probs_ref[...] = all_probs_ref[plane]
    placed = jnp.dot(slot_ref[...], payload_ref[...], preferred_element_type=jnp.float32)
    sent_ref[...] = placed[:, :768].astype(jnp.bfloat16).reshape(4, 256, 768)
    gate_ref[...] = jnp.broadcast_to(
        placed[:, 768:769] + placed[:, 769:770], (1024, 128)
    ).reshape(4, 256, 128)


def route_call(ids, att, parts, tokens, gain, router, route, slot_rows):
    return pl.pallas_call(
        route_kernel,
        out_shape=(
            jax.ShapeDtypeStruct((128, 768), jnp.float32),
            jax.ShapeDtypeStruct((128, 128), jnp.float32),
            jax.ShapeDtypeStruct((4, 256, 768), jnp.bfloat16),
            jax.ShapeDtypeStruct((4, 256, 128), jnp.float32),
            jax.ShapeDtypeStruct((4, 192, 768), jnp.bfloat16),
        ),
        in_specs=[in_smem()] + [pl.BlockSpec(memory_space=pltpu.HBM)] * 11 + in_vmem(5),
        out_specs=tuple(in_vmem(5)),
        scratch_shapes=[
            pltpu.VMEM((512, 896), jnp.bfloat16),
            pltpu.VMEM((4, 128, 768), jnp.float32),
            pltpu.VMEM((4, 128, 128), jnp.float32),
            pltpu.VMEM((4, 512, 192), jnp.bfloat16),
            pltpu.VMEM((192, 768), jnp.bfloat16),
            pltpu.VMEM((6, 96, 768), jnp.bfloat16),
            pltpu.SemaphoreType.DMA((11,)),
        ],
        compiler_params=pltpu.CompilerParams(vmem_limit_bytes=SCOPED),
        cost_estimate=LIGHT,
        name="route",
    )(ids, *att, *parts, tokens, gain, router, route, slot_rows)


def slot_kernel(tiny_ref, route_ref, turned_ref, grad_ref, low_ref, rows_ref, slots_ref):
    route = route_ref[...]
    lane = lax.broadcasted_iota(jnp.int32, (512, 128), 1)
    choose = lane == route
    later = lax.broadcasted_iota(jnp.int32, (512, 512), 0)
    earlier = lax.broadcasted_iota(jnp.int32, (512, 512), 1)
    filled = jnp.dot(
        (later >= earlier).astype(jnp.float32).astype(jnp.bfloat16),
        choose.astype(jnp.float32).astype(jnp.bfloat16),
        preferred_element_type=jnp.float32,
    )
    index = jnp.sum(jnp.where(choose, filled, 0.0), axis=-1, keepdims=True).astype(jnp.int32) - 1
    target = route * 256 + index
    low_ref[...] = (
        (lax.broadcasted_iota(jnp.int32, (512, 1024), 1) == target)
        .astype(jnp.float32)
        .astype(jnp.bfloat16)
        .reshape(4, 128, 1024)
    )
    turned = turned_ref[...]
    choose = lax.broadcasted_iota(jnp.int32, (8, 512), 0) == turned
    filled = jnp.dot(
        choose.astype(jnp.float32).astype(jnp.bfloat16),
        (later <= earlier).astype(jnp.float32).astype(jnp.bfloat16),
        preferred_element_type=jnp.float32,
    )
    index = jnp.sum(jnp.where(choose, filled, 0.0), axis=0, keepdims=True).astype(jnp.int32) - 1
    target = turned * 256 + index
    rows = (
        (lax.broadcasted_iota(jnp.int32, (1024, 512), 0) == target)
        .astype(jnp.float32)
        .astype(jnp.bfloat16)
    )
    rows_ref[...] = rows
    slots_ref[...] = (
        jnp.dot(rows, grad_ref[...], preferred_element_type=jnp.float32)
        .astype(jnp.bfloat16)
        .reshape(4, 256, 768)
    )


def slot_call(tiny, route, grad):
    return pl.pallas_call(
        slot_kernel,
        out_shape=(
            jax.ShapeDtypeStruct((4, 128, 1024), jnp.bfloat16),
            jax.ShapeDtypeStruct((1024, 512), jnp.bfloat16),
            jax.ShapeDtypeStruct((4, 256, 768), jnp.bfloat16),
        ),
        in_specs=in_vmem(4),
        out_specs=tuple(in_vmem(3)),
        compiler_params=pltpu.CompilerParams(vmem_limit_bytes=SCOPED),
        cost_estimate=LIGHT,
        name="slots",
    )(tiny, route[:, None], route[None, :], grad)


def expert_kernel(*refs):
    ids_ref, sent_ref, grad_ref = refs[:3]
    in_refs, out_refs = refs[3:11], refs[11:19]
    pick_ref, home_refs = refs[19], refs[20:24]
    hidden_ref, grad_pre_ref, total_ref = refs[24:]
    plane = ids_ref[2]
    for expert in range(4):
        back = None
        inner = None
        for half in range(2):
            in_ref, out_ref = in_refs[2 * expert + half], out_refs[2 * expert + half]
            pre_act = jnp.dot(sent_ref[expert], in_ref[...], preferred_element_type=jnp.float32)
            grad_hidden = lax.dot_general(
                grad_ref[expert], out_ref[...], NT, preferred_element_type=jnp.float32
            )
            hidden, slope = gelu_parts(pre_act)
            hidden_ref[half, expert] = hidden.astype(jnp.bfloat16)
            grad_pre = (grad_hidden * slope).astype(jnp.bfloat16)
            grad_pre_ref[half, expert] = grad_pre
            part_inner = jnp.sum(hidden * grad_hidden, axis=-1, keepdims=True)
            part_back = lax.dot_general(
                grad_pre, in_ref[...], NT, preferred_element_type=jnp.float32
            )
            back = part_back if half == 0 else back + part_back
            inner = part_inner if half == 0 else inner + part_inner
        payload = jnp.concatenate([back.astype(jnp.bfloat16), split_column(inner)], axis=1)
        columns = slice(256 * expert, 256 * (expert + 1))
        picked = pick_ref[:, :, columns].reshape(512, 256)
        part = jnp.dot(picked, payload, preferred_element_type=jnp.float32)
        if expert == 0:
            total_ref[...] = part.reshape(4, 128, 896)
        else:
            total_ref[...] += part.reshape(4, 128, 896)
    for away in range(4):
        home_refs[away][...] = total_ref[plane ^ away].astype(jnp.bfloat16)


def expert_call(ids, sent, grad, weights_in, weights_out, slot_pick):
    return pl.pallas_call(
        expert_kernel,
        out_shape=(jax.ShapeDtypeStruct((128, 896), jnp.bfloat16),) * 4
        + (jax.ShapeDtypeStruct((2, 4, 256, 384), jnp.bfloat16),) * 2,
        in_specs=[in_smem()] + in_vmem(19),
        out_specs=tuple(in_vmem(6)),
        scratch_shapes=[pltpu.VMEM((4, 128, 896), jnp.float32)],
        compiler_params=pltpu.CompilerParams(vmem_limit_bytes=SCOPED),
        cost_estimate=LIGHT,
        name="experts",
    )(ids, sent, grad, *weights_in, *weights_out, slot_pick)


def weight_grad_kernel(*refs):
    ids_ref, sent_ref, grad_ref, gate_ref, hidden_ref, grad_pre_ref = refs[1:7]
    out_refs = refs[7:15]
    pick_ref = refs[15]
    grad_refs = refs[16:24]
    home_refs, total_ref = refs[24:28], refs[28]
    plane = ids_ref[2]
    for expert in range(4):
        gate = gate_ref[expert][:, :1]
        rows = (grad_ref[expert].astype(jnp.float32) * gate).astype(jnp.bfloat16)
        for half in range(2):
            grad_refs[4 * half + expert][:, :768] = lax.dot_general(
                hidden_ref[half, expert], rows, TN, preferred_element_type=jnp.float32
            ).astype(jnp.bfloat16)
    for expert in range(4):
        gate = gate_ref[expert][:, :1]
        part = None
        for half in range(2):
            grad_pre = (grad_pre_ref[half, expert].astype(jnp.float32) * gate).astype(jnp.bfloat16)
            in_grad = lax.dot_general(
                sent_ref[expert], grad_pre, TN, preferred_element_type=jnp.float32
            ).astype(jnp.bfloat16)
            grad_refs[4 * half + expert][:, 768:1152] = in_grad[:384]
            grad_refs[4 * half + expert][:, 1152:] = in_grad[384:]
            product = jnp.dot(
                hidden_ref[half, expert],
                out_refs[2 * expert + half][...],
                preferred_element_type=jnp.float32,
            )
            part = product if half == 0 else part + product
        part = part.astype(jnp.bfloat16)
        columns = slice(256 * expert, 256 * (expert + 1))
        picked = pick_ref[:, :, columns].reshape(512, 256)
        placed = jnp.dot(picked, part, preferred_element_type=jnp.float32)
        if expert == 0:
            total_ref[...] = placed.reshape(4, 128, 768)
        else:
            total_ref[...] += placed.reshape(4, 128, 768)
    for away in range(4):
        home_refs[away][...] = total_ref[lax.rem(plane + away, 4)].astype(jnp.bfloat16)


def weight_grad_call(tiny, ids, sent, grad, gate, hidden, grad_pre, weights_out, slot_pick):
    return pl.pallas_call(
        weight_grad_kernel,
        out_shape=(jax.ShapeDtypeStruct((384, 1536), jnp.bfloat16),) * 8
        + (jax.ShapeDtypeStruct((128, 768), jnp.bfloat16),) * 4,
        in_specs=in_vmem(1) + [in_smem()] + in_vmem(14),
        out_specs=tuple(in_vmem(12)),
        scratch_shapes=[pltpu.VMEM((4, 128, 768), jnp.float32)],
        compiler_params=pltpu.CompilerParams(vmem_limit_bytes=SCOPED),
        cost_estimate=LIGHT,
        name="weight_grads",
    )(tiny, ids, sent, grad, gate, hidden, grad_pre, *weights_out, slot_pick)


def project_back_kernel(ids_ref, *refs):
    grad_refs = refs[:4]
    weight_ref, token_ref, gain_two_ref, router_ref = refs[4:8]
    block_refs = refs[8:12]
    tiny_ref, low_ref, small_ref = refs[12:]
    chip = ids_ref[0]
    plane = ids_ref[2]
    gain = None
    for away in range(4):
        part = lax.dot_general(
            grad_refs[away][...], weight_ref[...], NT, preferred_element_type=jnp.float32
        )
        low_ref[chip ^ away] = part.astype(jnp.bfloat16)
        tokens = token_ref[chip ^ away].astype(jnp.float32)
        inverse = lax.rsqrt(jnp.mean(tokens * tokens, axis=-1, keepdims=True) + EPSILON)
        added = jnp.sum(part * tokens * inverse, axis=0, keepdims=True)
        gain = added if away == 0 else gain + added
    small_ref[...] = jnp.zeros_like(small_ref)
    small_ref[0:1, :] = gain
    small_ref[1:2, :] = gain_two_ref[...]
    small_ref[2:6, :] = router_ref[:4, :]
    small = small_ref[...]
    high = small.astype(jnp.bfloat16).astype(jnp.float32)
    rows = jnp.concatenate([high, small - high], axis=0).astype(jnp.bfloat16)
    for away, block_ref in enumerate(block_refs):
        block_ref[:128, :] = low_ref[lax.rem(plane + away, 4)]
        block_ref[128:, :] = rows
    tiny_ref[...] = low_ref[0, :16, :128]


def project_back_call(ids, grads, weight, tokens, gain_two, router):
    return pl.pallas_call(
        project_back_kernel,
        out_shape=(jax.ShapeDtypeStruct((144, 768), jnp.bfloat16),) * 4
        + (jax.ShapeDtypeStruct((16, 128), jnp.bfloat16),),
        in_specs=[in_smem()] + in_vmem(8),
        out_specs=tuple(in_vmem(5)),
        scratch_shapes=[
            pltpu.VMEM((4, 128, 768), jnp.bfloat16),
            pltpu.VMEM((8, 768), jnp.float32),
        ],
        compiler_params=pltpu.CompilerParams(vmem_limit_bytes=SCOPED),
        cost_estimate=LIGHT,
        name="project_back",
    )(ids, *grads, weight, tokens, gain_two, router)


def add_dense_kernel(ids_ref, kept_ref, *refs):
    arrived_refs, rel_ref, home_refs, total = refs[4:8], refs[8], refs[9:13], refs[13]
    chip = ids_ref[0]
    small = arrived_refs[0][128:, :].astype(jnp.float32)
    for at in range(1, 4):
        small = small + arrived_refs[at][128:, :].astype(jnp.float32)
    small = small[:8] + small[8:]
    for at in range(4):
        total[at] = kept_ref[at].astype(jnp.float32) + refs[at][...].astype(jnp.float32)
        total[at, 120:, :] = small
        total[at, 126:127, :] = rel_ref[...]
    for away in range(4):
        home_refs[away][...] = total[chip ^ away].astype(jnp.bfloat16)


def add_dense_call(ids, kept, theirs, arrived, rel):
    return pl.pallas_call(
        add_dense_kernel,
        out_shape=(jax.ShapeDtypeStruct((128, 768), jnp.bfloat16),) * 4,
        in_specs=[in_smem()] + in_vmem(10),
        out_specs=tuple(in_vmem(4)),
        scratch_shapes=[pltpu.VMEM((4, 128, 768), jnp.float32)],
        compiler_params=pltpu.CompilerParams(vmem_limit_bytes=SCOPED),
        cost_estimate=LIGHT,
        name="add_dense",
    )(ids, kept, *theirs, *arrived, rel)


def sum_dense_kernel(tiny_ref, *refs):
    total = refs[0][...].astype(jnp.float32)
    for at in range(1, 4):
        total = total + refs[at][...].astype(jnp.float32)
    refs[4][...] = total.astype(jnp.bfloat16)


def sum_dense_call(tiny, blocks):
    return pl.pallas_call(
        sum_dense_kernel,
        out_shape=jax.ShapeDtypeStruct((128, 768), jnp.bfloat16),
        in_specs=in_vmem(5),
        out_specs=in_vmem(1)[0],
        compiler_params=pltpu.CompilerParams(vmem_limit_bytes=SCOPED),
        cost_estimate=LIGHT,
        name="sum_dense",
    )(tiny, *blocks)


def pack_kernel(branch_ref, *refs):
    for at in range(3):
        refs[3 + at][:128, :] = refs[at][...]
        refs[3 + at][128:, :] = branch_ref[...]


def pack_call(branch, homes):
    return pl.pallas_call(
        pack_kernel,
        out_shape=(jax.ShapeDtypeStruct((256, 768), jnp.bfloat16),) * 3,
        in_specs=in_vmem(4),
        out_specs=tuple(in_vmem(3)),
        compiler_params=pltpu.CompilerParams(vmem_limit_bytes=SCOPED),
        cost_estimate=LIGHT,
        name="pack",
    )(branch, *homes)


def output_kernel(ids_ref, home_ref, *refs):
    plane = ids_ref[2]
    resid_ref, probs_ref, route_ref, out_ref = refs[3:]
    rows = home_ref[...].astype(jnp.float32)
    for at in range(3):
        rows = rows + refs[at][:128, :].astype(jnp.float32)
    lane = lax.broadcasted_iota(jnp.int32, (128, 128), 1)
    gate = jnp.sum(
        jnp.where(lane == route_ref[plane], probs_ref[...], 0.0), axis=-1, keepdims=True
    )
    out_ref[...] = (resid_ref[...] + gate * rows).astype(jnp.bfloat16)


def output_call(ids, home, packed, resid, probs, route):
    return pl.pallas_call(
        output_kernel,
        out_shape=jax.ShapeDtypeStruct((128, 768), jnp.bfloat16),
        in_specs=[in_smem()] + in_vmem(7),
        out_specs=in_vmem(1)[0],
        compiler_params=pltpu.CompilerParams(vmem_limit_bytes=SCOPED),
        cost_estimate=LIGHT,
        name="output",
    )(ids, home, *packed, resid, probs, route)


def finish_kernel(ids_ref, *refs):
    token_ref, gain_ref, grad_ref, out_ref = refs[4:8]
    ending_ref, tiny_ref = refs[9:]
    plane = ids_ref[2]
    gradient = refs[0][:128, :].astype(jnp.float32)
    for at in range(1, 4):
        gradient = gradient + refs[at][:128, :].astype(jnp.float32)
    tokens = token_ref[plane].astype(jnp.float32)
    inverse = lax.rsqrt(jnp.mean(tokens * tokens, axis=-1, keepdims=True) + EPSILON)
    weighted = gradient * gain_ref[...]
    inner = jnp.mean(weighted * tokens, axis=-1, keepdims=True)
    result = inverse * weighted - tokens * (inverse * inverse * inverse * inner) + grad_ref[...]
    ending = result.astype(jnp.bfloat16)
    ending_ref[:128, :] = ending
    ending_ref[128:, :] = out_ref[...]
    tiny_ref[...] = ending[:16, :128]


def finish_call(ids, arrived, tokens, gain, grad, out, ready):
    return pl.pallas_call(
        finish_kernel,
        out_shape=(
            jax.ShapeDtypeStruct((256, 768), jnp.bfloat16),
            jax.ShapeDtypeStruct((16, 128), jnp.bfloat16),
        ),
        in_specs=[in_smem()] + in_vmem(9),
        out_specs=tuple(in_vmem(2)),
        compiler_params=pltpu.CompilerParams(vmem_limit_bytes=SCOPED),
        cost_estimate=LIGHT,
        name="finish",
    )(ids, *arrived, tokens, gain, grad, out, ready)


def dense_grad_kernel(tiny_ref, ids_ref, *refs):
    grad_refs, att_ref, branch_refs = refs[:4], refs[4], refs[5:9]
    normed_ref, kept_ref = refs[9:11]
    sent_refs, total_ref = refs[11:15], refs[15]
    chip = ids_ref[0]
    core = ids_ref[1]
    plane = ids_ref[2]
    total = None
    for away in range(4):
        part = lax.dot_general(
            normed_ref[pl.ds(pl.multiple_of(128 * (chip ^ away), 128), 128), :],
            grad_refs[away][...],
            TN,
            preferred_element_type=jnp.float32,
        )
        total = part if away == 0 else total + part
    rows = None
    for away, branch_ref in enumerate(branch_refs):
        branch = branch_ref[...] if away == 0 else branch_ref[128:, :]
        part = lax.dot_general(
            att_ref[pl.ds(pl.multiple_of(128 * lax.rem(plane + 4 - away, 4), 128), 128), :],
            branch,
            TN,
            preferred_element_type=jnp.float32,
        )
        rows = part if away == 0 else rows + part
    total_ref[...] = jnp.zeros_like(total_ref)
    for half in range(2):
        for place in range(4):
            first = 384 * half + 96 * place
            total_ref[half, place, :96, :576] = total[first : first + 96]
            first = 96 * half + 24 * place
            total_ref[half, place, 96:120, :] = rows[first : first + 24]
    kept_ref[...] = total_ref[core].astype(jnp.bfloat16)
    for place in range(4):
        sent_refs[place][...] = total_ref[1 - core, place].astype(jnp.bfloat16)


def dense_grad_call(tiny, ids, grads, att, branches, normed):
    return pl.pallas_call(
        dense_grad_kernel,
        out_shape=(jax.ShapeDtypeStruct((4, 128, 768), jnp.bfloat16),)
        + (jax.ShapeDtypeStruct((128, 768), jnp.bfloat16),) * 4,
        in_specs=in_vmem(1) + [in_smem()] + in_vmem(10),
        out_specs=tuple(in_vmem(5)),
        scratch_shapes=[pltpu.VMEM((2, 4, 128, 768), jnp.float32)],
        compiler_params=pltpu.CompilerParams(vmem_limit_bytes=SCOPED),
        cost_estimate=LIGHT,
        name="dense_grads",
    )(tiny, ids, *grads, att, *branches, normed)


def tokens_kernel(ids_ref, *refs):
    grad_ref, all_ref = refs[4:]
    plane = ids_ref[2]
    for step in range(4):
        all_ref[lax.rem(plane + 4 - step, 4)] = refs[step][:128, :].astype(jnp.float32)
    for seq in range(4):
        grad_ref[:, seq, :] = all_ref[seq]


def tokens_call(ids, blocks):
    return pl.pallas_call(
        tokens_kernel,
        out_shape=jax.ShapeDtypeStruct((128, 4, 768), jnp.float32),
        in_specs=[in_smem()] + in_vmem(4),
        out_specs=in_vmem(1)[0],
        scratch_shapes=[pltpu.VMEM((4, 128, 768), jnp.float32)],
        compiler_params=pltpu.CompilerParams(vmem_limit_bytes=SCOPED),
        cost_estimate=LIGHT,
        name="tokens_back",
    )(ids, *blocks)


def add_pairs_kernel(*refs):
    for at in range(4):
        total = refs[at][...].astype(jnp.float32) + refs[4 + at][...].astype(jnp.float32)
        refs[8 + at][...] = total.astype(jnp.bfloat16)


def add_pairs_call(parts):
    return pl.pallas_call(
        add_pairs_kernel,
        out_shape=(jax.ShapeDtypeStruct((384, 1536), jnp.bfloat16),) * 4,
        in_specs=in_vmem(8),
        out_specs=tuple(in_vmem(4)),
        compiler_params=pltpu.CompilerParams(vmem_limit_bytes=SCOPED),
        cost_estimate=LIGHT,
        name="add_pairs",
    )(*parts)


def resid_back_kernel(
    ids_ref,
    home0_ref,
    home1_ref,
    home2_ref,
    home3_ref,
    resid_ref,
    probs_ref,
    route_ref,
    grad_ref,
    gain_ref,
    router_ref,
    out_weight_ref,
    grad_resid_ref,
    branch_ref,
    att0_ref,
    att1_ref,
    att2_ref,
    att3_ref,
    gain_grad_ref,
    router_grad_ref,
    all_ref,
):
    chip = ids_ref[0]
    plane = ids_ref[2]
    lane = lax.broadcasted_iota(jnp.int32, (128, 128), 1)
    collected = home0_ref[...].astype(jnp.float32)
    for home_ref in (home1_ref, home2_ref, home3_ref):
        collected = collected + home_ref[...].astype(jnp.float32)
    grad_gate = collected[:, 768:769] + collected[:, 769:770]
    probs = probs_ref[...]
    chosen = lane == route_ref[plane]
    gate = jnp.sum(jnp.where(chosen, probs, 0.0), axis=-1, keepdims=True)
    grad_sent = (collected[:, :768] * gate).astype(jnp.bfloat16).astype(jnp.float32)
    grad_logits = probs * (jnp.where(chosen, grad_gate, 0.0) - gate * grad_gate)
    resid = resid_ref[...]
    gain = gain_ref[...]
    inverse = lax.rsqrt(jnp.mean(resid * resid, axis=-1, keepdims=True) + EPSILON)
    unit = resid * inverse
    router_grad = lax.dot_general(
        grad_logits, unit * gain, TN, precision=PRECISE, preferred_element_type=jnp.float32
    )
    router_grad_ref[...] = router_grad[:8]
    router = jnp.concatenate([router_ref[...], jnp.zeros((124, 768), jnp.float32)], axis=0)
    grad_normed = grad_sent + jnp.dot(
        grad_logits, router, precision=PRECISE, preferred_element_type=jnp.float32
    )
    gain_grad_ref[...] = jnp.sum(grad_normed * unit, axis=0, keepdims=True)
    weighted = grad_normed * gain
    inner = jnp.mean(weighted * resid, axis=-1, keepdims=True)
    grad_resid = inverse * weighted - unit * (inverse * inverse * inner)
    grad_resid = grad_resid + grad_ref[plane].astype(jnp.float32)
    grad_resid_ref[...] = grad_resid
    branch = grad_resid.astype(jnp.bfloat16)
    branch_ref[...] = branch
    for away in range(4):
        all_ref[plane ^ away] = lax.dot_general(
            branch, out_weight_ref[away], NT, preferred_element_type=jnp.float32
        ).astype(jnp.bfloat16)
    for away, att_ref in enumerate((att0_ref, att1_ref, att2_ref, att3_ref)):
        att_ref[...] = all_ref[chip ^ away]


def resid_back_call(ids, homes, resid, probs, route, grad, gain, router, out_weights):
    return pl.pallas_call(
        resid_back_kernel,
        out_shape=(
            jax.ShapeDtypeStruct((128, 768), jnp.float32),
            jax.ShapeDtypeStruct((128, 768), jnp.bfloat16),
        )
        + (jax.ShapeDtypeStruct((128, 192), jnp.bfloat16),) * 4
        + (
            jax.ShapeDtypeStruct((1, 768), jnp.float32),
            jax.ShapeDtypeStruct((8, 768), jnp.float32),
        ),
        in_specs=[in_smem()] + in_vmem(11),
        out_specs=tuple(in_vmem(8)),
        scratch_shapes=[pltpu.VMEM((4, 128, 192), jnp.bfloat16)],
        compiler_params=pltpu.CompilerParams(vmem_limit_bytes=SCOPED),
        cost_estimate=LIGHT,
        name="resid_back",
    )(ids, *homes, resid, probs, route, grad, gain, router, out_weights)


def pinned(first, *others):
    tied = lax.optimization_barrier((first,) + others)
    return tied


def gather_over_ctx(block, chip, core):
    gathered = jnp.stack([block] + [to_chip(block, away) for away in range(1, 4)])
    ordered = jnp.stack([pick(gathered, at ^ chip) for at in range(4)])
    both = jnp.stack([ordered, to_core(ordered)])
    whole = jnp.stack([pick(both, core), pick(both, 1 - core)])
    return whole.reshape((8,) + block.shape)


def local_planned(
    tokens,
    gain_one,
    qkv_weight,
    out_weight,
    rel_weight,
    gain_two,
    router_weight,
    expert_in,
    expert_out,
    routes,
    bucket_table,
    grad_out,
):
    row_count, seq_count, width = tokens.shape
    token_count = row_count * seq_count
    expert_count = router_weight.shape[1]
    capacity = 2 * token_count // expert_count
    slots = expert_count * capacity
    ctx_at = lax.axis_index("ctx")
    plane = lax.axis_index("wsh")
    chip = ctx_at // 2
    core = ctx_at % 2
    ids = jnp.stack([chip, core, plane]).astype(jnp.int32)

    def by_seq(values):
        return lax.optimization_barrier(jnp.swapaxes(values, 0, 1))

    token_blocks = by_seq(tokens)
    weight_qkv = jnp.concatenate(
        lax.optimization_barrier((qkv_weight[:, 1], qkv_weight[:, 2], qkv_weight[:, 0])), axis=1
    )
    normed_low, grad_blocks, *projected = project_call(
        ids, token_blocks, gain_one[None], weight_qkv, grad_out
    )
    in_one, in_two = to_chip(expert_in[0], 1), to_chip(expert_in[0], 2)
    half_rows = pick(out_weight.reshape(2, 96, width), core)
    weight_parts = plane_swap([half_rows] * 4)[1:]
    own = chip_swap(projected)
    route_blocks = by_seq(routes)
    slot_blocks, slot_rows, grad_slots = slot_call(
        tiny_of(projected[0]),
        route_blocks.reshape(token_count) ^ chip,
        grad_blocks.reshape(token_count, width),
    )
    gain_row = gain_two[None]
    router_rows = router_weight.T
    *own, in_one, in_two, slot_blocks, slot_rows, grad_slots = pinned(
        *own, in_one, in_two, slot_blocks, slot_rows, grad_slots
    )
    own[3], weight_in, weight_out = pinned(own[3], expert_in[0], expert_out[0])
    out_one, out_two = to_chip(weight_out, 1), to_chip(weight_out, 2)
    other = [to_core(block) for block in own]

    bucket_pick = (
        bucket_table[:, None] == lax.iota(jnp.int32, rel_weight.shape[0])[None, :]
    ).astype(jnp.float32)
    head_table = jnp.dot(bucket_pick, rel_weight, precision=PRECISE).T
    line = bias_lines(head_table, core)
    *attended, prob, keyval, query = attend_call(ids, tiny_of(half_rows), own, other, line)
    attended[3], *weight_parts = pinned(attended[3], *weight_parts)
    weight_parts = [out_weight] + weight_parts + [to_core(part) for part in weight_parts]
    attended = chip_swap(attended)
    *attended, out_one, out_two = pinned(*attended, out_one, out_two)
    attended[3], late_in, late_out = pinned(attended[3], weight_in, weight_out)
    in_three, out_three = to_chip(late_in, 3), to_chip(late_out, 3)
    att_rows = gather_rows_call(ids, attended)
    att_planes = [att_rows] + [to_plane(att_rows, away) for away in range(1, 4)]
    weights_in, weights_out = [], []
    for block in (weight_in, in_one, in_two, in_three):
        weights_in += [block, to_core(block)]
    for block in (weight_out, out_one, out_two, out_three):
        weights_out += [block, to_core(block)]
    my_resid, my_probs, sent_slots, gate_slots, out_weights = route_call(
        ids, att_planes, weight_parts, token_blocks, gain_row, router_rows, route_blocks, slot_rows
    )
    *homes, hidden, grad_pre = expert_call(
        ids, sent_slots, grad_slots, weights_in, weights_out, slot_blocks
    )
    tiny = tiny_of(homes[0])
    homes = plane_swap(homes)

    weight_grads = weight_grad_call(
        tiny, ids, sent_slots, grad_slots, gate_slots, hidden, grad_pre, weights_out, slot_blocks
    )
    grad_parts, expert_homes = weight_grads[:8], weight_grads[8:]
    *homes, expert_one, expert_two = pinned(*homes, *expert_homes[:2])
    expert_homes = [expert_one, expert_two] + list(expert_homes[2:])
    my_grad_resid, my_branch, *att_grads, grad_gain_two, grad_router = resid_back_call(
        ids,
        homes,
        my_resid,
        my_probs,
        route_blocks,
        grad_blocks,
        gain_row,
        router_rows,
        out_weights,
    )
    att_grads[0], *parts = pinned(att_grads[0], *grad_parts)
    near = add_pairs_call(parts[:4] + [to_core(part) for part in parts[4:]])
    grad_mixed = turn_swap(att_grads)
    packed = pack_call(my_branch, expert_homes[1:])
    rest = pinned(*grad_mixed, *near[1:], *packed)
    grad_mixed, (near_one, near_two, near_three) = rest[:4], rest[4:7]
    packed = plane_shift([None] + list(rest[7:10]))[1:]
    near_one, near_two = to_chip(near_one, 1), to_chip(near_two, 2)
    mine_back, theirs_back, lags, tiny = attend_back_call(ids, query, prob, keyval, grad_mixed)
    theirs_back, near_one, near_two, near_three, *packed = pinned(
        theirs_back, near_one, near_two, near_three, *packed
    )
    out = output_call(ids, expert_homes[0], packed, my_resid, my_probs, route_blocks)
    grad_projected = list(add_queries_call(ids, mine_back, to_core(theirs_back)))
    grad_projected = chip_swap(grad_projected)
    def spread_planes(block):
        return jnp.stack([block] + [to_plane(block, away) for away in range(1, 4)])

    def to_tokens(gathered):
        by_place = jnp.stack([pick(gathered, (plane - at) % 4) for at in range(4)])
        return jnp.swapaxes(lax.optimization_barrier(by_place), 0, 1)

    *grad_projected, near_three = pinned(*grad_projected, near_three)
    near_three = to_chip(near_three, 3)
    *partial, tiny = project_back_call(
        ids,
        grad_projected,
        weight_qkv,
        token_blocks,
        grad_gain_two,
        grad_router,
    )
    tiny, lags = pinned(tiny, lags)
    grad_rel = jnp.dot(bucket_pick.T, table_grad(lags, core), precision=PRECISE)
    rel_row = jnp.where(
        (lax.iota(jnp.int32, 4) == plane)[None, :, None], grad_rel[:, None, :], 0.0
    ).reshape(-1)
    rel_row = jnp.pad(rel_row, (0, width - rel_row.shape[0]))
    kept, *sent = dense_grad_call(
        to_core(tiny), ids, grad_projected, att_rows, [my_branch] + packed, normed_low
    )
    arrived = plane_shift(partial)
    *arrived, kept, sent_one, sent_two, sent_three, sent_four, near_three, rel_row, out = pinned(
        *arrived, kept, *sent, near_three, rel_row, out
    )
    sent = [to_core(part) for part in (sent_one, sent_two, sent_three, sent_four)]
    dense = list(add_dense_call(ids, kept, sent, arrived, rel_row[None]))
    dense_own = dense[0]
    dense = chip_swap(dense)
    ending, tiny = finish_call(
        ids, arrived, token_blocks, gain_one[None], my_grad_resid, out, dense_own
    )
    ending = [ending] + [
        lax.ppermute(ending, "wsh", [(at, (at + step) % 4) for at in range(4)])
        for step in range(1, 4)
    ]
    summed = sum_dense_call(to_core(tiny), dense)
    summed, near_one, near_two, near_three = pinned(summed, near_one, near_two, near_three)
    weight_sum = 0.0
    for block in (near[0], near_one, near_two, near_three):
        weight_sum = weight_sum + block.astype(jnp.float32)
    grad_weight_out = weight_sum[None, :, :768]
    grad_weight_in = jnp.concatenate([weight_sum[:, 768:1152], weight_sum[:, 1152:]])[None]
    gathered = chip_swap([summed] * 4)
    both = pinned(*ending, *gathered)
    ending, gathered = both[:4], both[4:]
    both = [gathered, [to_core(block) for block in gathered]]
    ordered = jnp.stack([jnp.stack(part) for part in both])
    ordered = jnp.stack([pick(ordered, core), pick(ordered, 1 - core)])
    ordered = jnp.stack([pick(jnp.swapaxes(ordered, 0, 1), at ^ chip) for at in range(4)], axis=1)
    summed = ordered.reshape(8, 128, width)
    small = summed[0, 120:].astype(jnp.float32) + summed[4, 120:].astype(jnp.float32)
    grad_out_all = summed[:, 96:120].astype(jnp.float32).reshape(192, width)
    grad_qkv = summed[:, :96, :576].astype(jnp.float32).reshape(width, 576)
    grad_qkv = jnp.stack([grad_qkv[:, 384:], grad_qkv[:, :192], grad_qkv[:, 192:384]], axis=1)
    out = to_tokens(jnp.stack([block[128:] for block in ending]))
    grad_tokens = tokens_call(ids, ending)
    rel_all = small[2 + expert_count][: 4 * grad_rel.size].reshape(-1, 4, grad_rel.shape[1])
    return (
        out,
        grad_tokens,
        small[0],
        grad_qkv,
        grad_out_all,
        pick(jnp.swapaxes(rel_all, 0, 1), plane),
        small[1],
        small[2 : 2 + expert_count].T,
        grad_weight_in,
        grad_weight_out,
    )


def solution(mesh):
    placed = (
        P("ctx", None, None),
        P(),
        P(None, None, "wsh"),
        P("wsh", None),
        P(None, "wsh"),
        P(),
        P(),
        P("ctx", None, "wsh"),
        P("ctx", "wsh", None),
        P("ctx", None, None),
        P(),
        P("ctx", None, None),
    )
    planned = mesh.shape['ctx'] == 8 and mesh.shape['wsh'] == 4
    return jax.shard_map(
        local_planned if planned else local,
        mesh=mesh,
        in_specs=placed,
        out_specs=(
            P("ctx", None, None),
            P("ctx", None, None),
            P(),
            P(None, None, "wsh"),
            P("wsh", None),
            P(None, "wsh"),
            P(),
            P(),
            P("ctx", None, "wsh"),
            P("ctx", "wsh", None),
        ),
        check_vma=False,
    )
```
